512 devices in a mesh: vocab: 32 (over x_hi, y, core), seq: 16 (over x_lo, z).
Axes of the slice: x: 4 (x_hi: 2, x_lo: 2; x = x_hi * 2 + x_lo), y: 8, z: 8, core: 2. Of those that a mesh axis runs over, the one named last changes fastest.
Arguments:
- hidden: bfloat16 [2048, 3584], P('seq', 'vocab'), may hold values from -64 to 64
- table: bfloat16 [128000, 3584], P(('vocab', 'seq')), may hold values from -2 to 2
- targets: int32 [2048], replicated, may hold values from 0 to 127999
- token_ids: int32 [2048], P('seq'), may hold values from 0 to 127999, as said below
- input_grad: bfloat16 [2048, 3584], P('seq'), may hold values from -6 to 6
Outputs:
- token_loss: float32 [2048], P('seq')
- table_grad: bfloat16 [128000, 3584], P(('vocab', 'seq'))
The draws below stay inside these ranges and needn't reach their ends.
Inputs may be any that keep to these rules, and one draw needn't show every extreme that they name: `token_ids`: among the 128 tokens of one index of seq, at most 12 have ids in the 4000 table rows of one index of vocab, and at most 1 distinct ids lie in the 250 rows of one device.
All inputs are finite; a program needn't handle non-finite values.
Results may differ from the reference program's by a relative error of at most 0.006.
Values may be sent and summed in bfloat16 or wider, within the bound.
A program may use at most 128 MiB of HBM per device.

```python
import math
import jax
import jax.numpy as jnp
import numpy as np
from jax import lax

D = 3584
VOCAB = 128000
TOK_DEV = 128
HOT = 8
HOT_IDS = 1
TOKENS = 2048
VOC_DEV = 250
N_VOCAB = 32
N_SEQ = 16


def anchor_vectors(key):
    vec_key = jax.random.fold_in(key, 101)
    row_key = jax.random.fold_in(key, 102)
    vectors = jax.random.normal(vec_key, (4, D), jnp.float32)
    first_row = jax.random.randint(row_key, (), 0, VOCAB // 4 - 1)
    anchor_rows = (first_row + jnp.arange(4) * (VOCAB // 4)).astype(jnp.int32)
    return (vectors, anchor_rows)


def draw_table(key, part):
    vectors, anchor_rows = anchor_vectors(key)
    key = jax.random.fold_in(key, 1)
    base_key, row_key = jax.random.split(key, 2)
    ramp = jnp.sqrt(1.0 + 2.0 * jnp.arange(VOCAB, dtype=jnp.float32) / VOCAB)
    values = jax.random.normal(base_key, (VOCAB, D), jnp.float32)
    row_scale = 0.5 * 10.0 ** jax.random.uniform(row_key, (VOCAB,), jnp.float32) * ramp
    weights = values * row_scale[:, None] / jnp.sqrt(jnp.float32(D))
    weights = weights.at[anchor_rows].set(vectors / jnp.sqrt(jnp.float32(D)))
    weights = weights.at[anchor_rows + 1].set(vectors * 1.01 / jnp.sqrt(jnp.float32(D)))
    weights = jnp.clip(weights, -2.0, 2.0)
    return weights.astype(jnp.bfloat16)


def draw_hidden(key, part):
    key = jax.random.fold_in(key, 2)
    values = jax.random.normal(key, (TOKENS, D), jnp.float32)
    return values.astype(jnp.bfloat16)


def draw_token_ids(key, part):
    key = jax.random.fold_in(key, 3)
    remain = TOK_DEV - HOT
    owners_all = N_VOCAB * N_SEQ

    def one_block(block_key):
        hot_key, anchor_key, base_key, group_key, order_key = jax.random.split(block_key, 5)
        hot_owner = jax.random.randint(hot_key, (), 0, owners_all)
        hot_group = hot_owner // N_SEQ
        anchors = jax.random.randint(anchor_key, (N_VOCAB,), 0, N_SEQ)
        anchors = anchors.at[hot_group].set(hot_owner % N_SEQ)
        hot_base = jax.random.randint(base_key, (), 0, VOC_DEV)
        hot_index = jnp.arange(HOT)
        hot_list = hot_owner * VOC_DEV + (hot_base + hot_index % HOT_IDS) % VOC_DEV
        rest_index = jnp.arange(remain)
        groups = (hot_group + rest_index % N_VOCAB) % N_VOCAB
        occurrence = rest_index // N_VOCAB
        owner_inner = (anchors[groups] + 1 + occurrence % (N_SEQ - 1)) % N_SEQ
        owners = groups * N_SEQ + owner_inner
        group_base = jax.random.randint(group_key, (N_VOCAB,), 0, VOC_DEV)
        rest_list = owners * VOC_DEV + (group_base[groups] + occurrence // (N_SEQ - 1)) % VOC_DEV
        id_list = jnp.concatenate([hot_list, rest_list])
        order = jax.random.permutation(order_key, TOK_DEV)
        return id_list[order]
    block_keys = jax.random.split(key, N_SEQ)
    return jax.vmap(one_block)(block_keys).reshape(-1).astype(jnp.int32)


def place_ends(values, stream_key, low, high):
    longest = values.shape.index(max(values.shape))
    spots = []
    for shift in (0, 1):
        where = [jax.random.randint(jax.random.fold_in(stream_key, axis), (), 0, length) for axis, length in enumerate(values.shape)]
        where[longest] = (where[longest] + shift) % values.shape[longest]
        spots.append(tuple(where))
    return values.at[spots[0]].set(low).at[spots[1]].set(high)


def level_of(own_key, dims, cuts, smallest, largest):
    level = 1.0
    for dim, parts in cuts:
        steps = jax.random.uniform(jax.random.fold_in(jax.random.fold_in(own_key, 6), dim), (parts,), jnp.float32, smallest / len(cuts), largest / len(cuts))
        level = level * jnp.repeat(jnp.exp(steps), dims[dim] // parts).reshape((-1,) + (1,) * (len(dims) - 1 - dim))
    return level


def skewed_wide(own_key, shape, amount, skew):
    portions = [min(1 << octave, amount + 1 - (1 << octave)) * (1 << 20) // math.isqrt((1 << octave) ** skew) + 1 for octave in range((amount + 1).bit_length()) if 1 << octave <= amount]
    deviation = 1 + sum(portions) // (1 << 30)
    table = np.cumsum(np.array([max(1, weight // deviation) for weight in portions]))
    ticket = jax.random.randint(jax.random.fold_in(own_key, 1), shape, 0, int(table[len(portions) - 1]))
    start = jnp.left_shift(1, jnp.searchsorted(jnp.asarray(table, jnp.int32), ticket, side="right").astype(jnp.int32))
    grade = start - 1 + jax.random.randint(jax.random.fold_in(own_key, 4), shape, 0, 1 << 30) % jnp.minimum(start, amount + 1 - start)
    return jax.random.permutation(jax.random.fold_in(own_key, 2), amount)[grade].astype(jnp.int32)


def normal_values(stream_key, extent, scale, most, shards=(), kind=jnp.bfloat16):
    values = scale * jax.random.normal(stream_key, extent, jnp.float32)
    if shards:
        values = values * level_of(stream_key, extent, shards, -0.22, 0.18)
    return jnp.clip(values, -most, most).astype(kind)


def setup_inputs(seed: int = 0) -> dict:
    arg_keys = jax.random.split(jax.random.key(seed), 6)
    hidden = draw_hidden(jax.random.fold_in(arg_keys[5], 71), 0)
    table = draw_table(jax.random.fold_in(arg_keys[5], 71), 0)
    targets = place_ends(skewed_wide(arg_keys[2], (TOKENS,), VOCAB, 2), jax.random.fold_in(arg_keys[2], 3), 0, VOCAB - 1).astype(jnp.int32)
    token_ids = draw_token_ids(jax.random.fold_in(arg_keys[5], 71), 0)
    input_grad = normal_values(arg_keys[4], (TOKENS, D), 1.0, 6.0, ((0, 16),))
    return dict(hidden=hidden, table=table, targets=targets, token_ids=token_ids, input_grad=input_grad)


def reference(hidden, table, targets, token_ids, input_grad):
    block_rows = VOCAB // N_VOCAB
    table_blocks = table.reshape(N_VOCAB, block_rows, D)
    block_starts = (jnp.arange(N_VOCAB) * block_rows).astype(jnp.int32)
    column_ids = jnp.arange(block_rows).astype(jnp.int32)

    def logits_of(table_rows):
        return lax.dot_general(hidden, table_rows, (((1,), (1,)), ((), ())), preferred_element_type=jnp.float32)

    def stats_step(carry, inputs):
        top_now, total_now, picked_now = carry
        table_rows, start_row = inputs
        logits = logits_of(table_rows)
        top_next = jnp.maximum(top_now, jnp.max(logits, axis=1))
        total_next = total_now * jnp.exp(top_now - top_next) + jnp.sum(jnp.exp(logits - top_next[:, None]), axis=1)
        local_target = (targets - start_row).astype(jnp.int32)
        target_hit = local_target[:, None] == column_ids[None, :]
        picked_next = picked_now + jnp.sum(jnp.where(target_hit, logits, jnp.float32(0.0)), axis=1)
        return (top_next, total_next, picked_next), None

    start_carry = (jnp.full((TOKENS,), -jnp.inf, jnp.float32), jnp.zeros((TOKENS,), jnp.float32), jnp.zeros((TOKENS,), jnp.float32))
    (top_all, total_all, picked_all), unused = lax.scan(stats_step, start_carry, (table_blocks, block_starts))
    token_loss = top_all + jnp.log(total_all) - picked_all
    grad_rows = input_grad.astype(jnp.float32)

    def grad_block(inputs):
        table_rows, start_row = inputs
        logits = logits_of(table_rows)
        probs = jnp.exp(logits - top_all[:, None]) / total_all[:, None]
        local_target = (targets - start_row).astype(jnp.int32)
        target_hit = (local_target[:, None] == column_ids[None, :]).astype(jnp.float32)
        score_grad = (probs - target_hit).astype(jnp.bfloat16)
        head_grad = lax.dot_general(score_grad, hidden, (((0,), (0,)), ((), ())), preferred_element_type=jnp.float32)
        local_ids = (token_ids - start_row).astype(jnp.int32)
        inside = (local_ids >= 0) & (local_ids < block_rows)
        target_rows = jnp.where(inside, local_ids, block_rows).astype(jnp.int32)
        embed_grad = jnp.zeros((block_rows, D), jnp.float32).at[target_rows].add(grad_rows, mode="drop")
        return (head_grad + embed_grad).astype(jnp.bfloat16)

    table_grad = lax.map(grad_block, (table_blocks, block_starts)).reshape(VOCAB, D)
    return token_loss, table_grad
```

```python
import heapq
import itertools

import jax
import jax.numpy as jnp
from jax import lax
from jax.experimental import pallas as pl
from jax.experimental.pallas import tpu as pltpu
from jax.sharding import PartitionSpec as P

MESH = pl.DeviceIdType.MESH
F32 = jnp.float32
BF16 = jnp.bfloat16

D = 3584
TOK = 128
FEAT = 112
ROWS = 250
SEQ = 16
VOC = 32
HALF = D // 2
ROW_A, ROW_B, ROW_C = (0, 32), (32, 32), (64, 48)
EXTRA = D + 128


def plan_messages():
    messages = {}

    def put(key, size, axis, hops, deps):
        messages[key] = dict(size=size, axis=axis, hops=hops, deps=list(deps))

    def ring(name, unit, axis, size, length, deps, flip):
        far = (length // 2, length // 2 - 1)
        for step, most in zip((1, -1), far[::-1] if flip else far):
            for dist in range(1, most + 1):
                put((name, unit, step, dist), size, axis, 1, deps if dist == 1 else [(name, unit, step, dist - 1)])

    def item(name, unit, rel, length, flip):
        rel %= length
        back = length // 2 if flip else length // 2 - 1
        if rel == 0:
            return []
        return [(name, unit, -1, rel)] if rel <= back else [(name, unit, 1, length - rel)]

    a, b, c = ROW_A[1], ROW_B[1], ROW_C[1]
    for rel in (1, -1, 2, -2, 3, -3, 4):
        put(("CQ", 0, 1 if rel > 0 else -1, abs(rel)), c, "q", abs(rel), [])
    for rel in (1, -1, 2):
        put(("X1", 0, 1 if rel > 0 else -1, abs(rel)), a + b, "x", abs(rel), [])
    all_q = [key for key in messages if key[0] == "CQ"]
    all_x = [key for key in messages if key[0] == "X1"]
    ring("CP", 0, "p", 8 * c, 8, all_q, False)
    for rel in range(8):
        ring("CX", rel, "x", 8 * c, 4, all_q + item("CP", 0, rel, 8, False), rel % 2 == 1)
    ring("AQ", 0, "q", 4 * a, 8, all_x, False)
    ring("BP", 0, "p", 4 * b, 8, all_x, True)
    pair = {0: (1, -1), 1: (1, 2, 3), 3: (-1, -2, -3), 2: (2, 3, 4, 5, 6)}
    for name, axis, source, flip, rows in (("AP", "p", "AQ", False, a), ("BQ", "q", "BP", True, b)):
        for unit in range(4):
            deps = all_x + [key for rel in pair[unit] for key in item(source, 0, rel, 8, flip)]
            ring(name, unit, axis, 8 * rows, 8, deps, unit % 2 == 1)
    return messages


def plan_order(messages):
    turned = {"x": "x", "p": "q", "q": "p"}
    counter = itertools.count()
    link, issue, events = {}, [0.0, 0.0], []
    arrival = [{}, {}]
    waits = [{key: set(m["deps"]) for key, m in messages.items()} for _ in range(2)]
    after = {}
    for key, m in messages.items():
        for dep in m["deps"]:
            after.setdefault(dep, []).append(key)

    def start(core, key, now):
        m = messages[key]
        issue[core] = now = max(now, issue[core]) + 0.05
        lane = (turned[m["axis"]] if core else m["axis"], key[2])
        link[lane] = max(now, link.get(lane, 0.0)) + m["size"] * 256 * m["hops"] / 1e5
        heapq.heappush(events, (link[lane] + 1.0 + 0.3 * (m["hops"] - 1), next(counter), core, key))

    for core in range(2):
        for key, m in messages.items():
            if not m["deps"]:
                start(core, key, 0.0)
    while events:
        now, _, core, key = heapq.heappop(events)
        arrival[core][key] = now
        for later in after.get(key, []):
            waits[core][later].discard(key)
            if not waits[core][later]:
                start(core, later, now)
    return sorted(messages, key=lambda key: arrival[0][key] + arrival[1][key])


MESSAGES = plan_messages()
ORDER = plan_order(MESSAGES)
RECV = {key: i for i, key in enumerate(MESSAGES)}
PHASES = ("X1", "CQ", "CP", "CX", "AQ", "BP", "AP", "BQ")


def gather_kernel(
    hidden_ref, ids_hbm, input_grad_ref, table_ref, targets_ref,
    g, emb_rows, emb_hot, table_v, targets_v,
    ids_ref, grad_v, emb_out, emb_in,
    recv_sem, send_sem, core_sem, emb_sem, local_sem,
):
    v, s = lax.axis_index("vocab"), lax.axis_index("seq")
    c = lax.rem(v, 2)
    y = lax.rem(lax.div(v, 2), 8)
    z = lax.rem(s, 8)
    x = 2 * lax.div(v, 16) + lax.div(s, 8)
    p = z + c * (y - z)
    q = y + c * (z - y)

    def device(x_at, p_at, q_at):
        z_at = p_at + c * (q_at - p_at)
        y_at = q_at + c * (p_at - q_at)
        return (lax.div(x_at, 2) * 16 + y_at * 2 + c, lax.rem(x_at, 2) * 8 + z_at)

    def turn(at, by, length):
        return lax.rem(at + (by + length), length) if by else at

    sibling = (v + 1 - 2 * c, s)
    mine = g.at[c]
    other = g.at[1 - c]

    own_copy = pltpu.make_async_copy(hidden_ref, mine.at[x, p, q], local_sem.at[0])
    own_copy.start()
    ids_copy = pltpu.make_async_copy(ids_hbm, ids_ref, local_sem.at[1])
    ids_copy.start()
    grad_copy = pltpu.make_async_copy(input_grad_ref, grad_v, local_sem.at[2])
    grad_copy.start()
    targets_copy = pltpu.make_async_copy(targets_ref, targets_v, local_sem.at[3])
    targets_copy.start()
    table_copy = pltpu.make_async_copy(table_ref, table_v, local_sem.at[4])
    table_copy.start()

    partners = [device(turn(x, d, 4), p, q) for d in (1, -1, 2)]
    partners += [device(x, turn(p, d, 8), q) for d in (1, -1)]
    partners += [device(x, p, turn(q, d, 8)) for d in (1, -1, 2, -2, 3, -3, 4)]
    partners += [sibling]
    barrier = pltpu.get_barrier_semaphore()
    for partner in partners:
        pl.semaphore_signal(barrier, inc=1, device_id=partner, device_id_type=MESH)
    pl.semaphore_wait(barrier, len(partners))
    own_copy.wait()

    def rows(part_rows):
        return pl.ds(part_rows[0], part_rows[1])

    def block(name, unit, shift):
        if name == "X1":
            return mine.at[turn(x, shift, 4), p, q, pl.ds(ROW_A[0], ROW_A[1] + ROW_B[1])]
        if name == "CQ":
            return mine.at[x, p, turn(q, shift, 8), rows(ROW_C)]
        if name == "CP":
            return mine.at[x, turn(p, shift, 8), :, rows(ROW_C)]
        if name == "CX":
            return mine.at[turn(x, shift, 4), turn(p, unit, 8), :, rows(ROW_C)]
        if name == "AQ":
            return mine.at[:, p, turn(q, shift, 8), rows(ROW_A)]
        if name == "BP":
            return mine.at[:, turn(p, shift, 8), q, rows(ROW_B)]
        if name == "AP":
            pair = 2 * turn(lax.div(q, 2), unit, 4)
            return mine.at[:, turn(p, shift, 8), pl.ds(pair, 2), rows(ROW_A)]
        pair = 2 * turn(lax.div(p, 2), unit, 4)
        return mine.at[:, pl.ds(pair, 2), turn(q, shift, 8), rows(ROW_B)]

    def message(key):
        name, unit, step, dist = key
        m = MESSAGES[key]
        by = step * m["hops"]
        target = {
            "x": lambda: device(turn(x, by, 4), p, q),
            "p": lambda: device(x, turn(p, by, 8), q),
            "q": lambda: device(x, p, turn(q, by, 8)),
        }[m["axis"]]()
        data = block(name, unit, -step * (dist - m["hops"]))
        return pltpu.make_async_remote_copy(
            src_ref=data, dst_ref=data, send_sem=send_sem.at[PHASES.index(name)], recv_sem=recv_sem.at[RECV[key]],
            device_id=target, device_id_type=MESH,
        )

    def wait_message(key):
        name, unit, step, dist = key
        data = block(name, unit, -step * dist)
        pltpu.make_async_copy(data, data, recv_sem.at[RECV[key]]).wait()

    def to_sibling(data):
        pltpu.make_async_remote_copy(
            src_ref=data, dst_ref=data, send_sem=core_sem.at[0], recv_sem=core_sem.at[1],
            device_id=sibling, device_id_type=MESH,
        ).start()

    passes = []
    by_phase = lambda *names: [key for key in MESSAGES if key[0] in names]
    passes.append((by_phase("X1", "AQ"), lambda: mine.at[:, p, :, rows(ROW_A)]))
    passes.append((by_phase("X1", "BP"), lambda: mine.at[:, :, q, rows(ROW_B)]))
    passes.append((by_phase("CQ"), lambda: mine.at[x, p, :, rows(ROW_C)]))
    for rel in range(1, 8):
        def origin(name, unit_keys, rel=rel):
            return [k for k in by_phase(name) if (-k[2] * k[3]) % 8 == rel]
        passes.append((origin("AP", None), lambda rel=rel: mine.at[:, turn(p, rel, 8), :, rows(ROW_A)]))
        passes.append((origin("BQ", None), lambda rel=rel: mine.at[:, :, turn(q, rel, 8), rows(ROW_B)]))
    for key in by_phase("CP", "CX"):
        passes.append(([key], lambda key=key: block(key[0], key[1], -key[2] * key[3])))

    done = set()
    sent = set()
    passed = set()

    def send_ready():
        for key, m in MESSAGES.items():
            if key not in sent and all(dep in done for dep in m["deps"]):
                sent.add(key)
                message(key).start()
        for i, (deps, data) in enumerate(passes):
            if i not in passed and all(dep in done for dep in deps):
                passed.add(i)
                to_sibling(data())

    def embed_rows():
        ids_copy.wait()
        grad_copy.wait()
        first = lax.broadcasted_iota(jnp.int32, (SEQ, TOK), 0) * ROWS + v * (SEQ * ROWS)
        local = ids_ref[...] - first
        inside = (local >= 0) & (local < ROWS)
        total = jnp.dot(inside.astype(F32).astype(BF16), grad_v[...], preferred_element_type=F32)
        local_id = jnp.max(jnp.where(inside, local, -1).astype(F32), axis=1, keepdims=True)
        tail = jnp.broadcast_to(local_id, (SEQ, 128))
        for j in range(SEQ):
            emb_out[j, :, 0:D] = total[j : j + 1, :]
            emb_out[j, :, D:EXTRA] = tail[j : j + 1, :]
        emb_in[s] = emb_out[s]

        def send(r, carry):
            j = lax.rem(s + r, SEQ)
            pltpu.make_async_remote_copy(
                src_ref=emb_out.at[j], dst_ref=emb_in.at[s], send_sem=emb_sem.at[0], recv_sem=emb_sem.at[1],
                device_id=(v, j), device_id_type=MESH,
            ).start()
            return carry

        lax.fori_loop(1, SEQ, send, 0)

    send_ready()
    embedded = False
    needed = set(by_phase("X1", "AQ", "BP"))
    for key in ORDER:
        wait_message(key)
        done.add(key)
        send_ready()
        if not embedded and needed <= done:
            embedded = True
            embed_rows()

    def wait_bytes(data, sem):
        pltpu.make_async_copy(data, data, sem).wait()

    wait_bytes(emb_in.at[pl.ds(0, SEQ - 1)], emb_sem.at[1])
    lane_ids = lax.broadcasted_iota(jnp.int32, (1, ROWS), 1).astype(F32)
    for j in range(SEQ):
        emb_rows[j : j + 1, :] = emb_in[j, :, 0:D]
        emb_hot[j : j + 1, :] = (lane_ids == emb_in[j, :, D : D + 1]).astype(F32)

    targets_copy.wait()
    table_copy.wait()
    wait_bytes(mine.at[0:3, p, q, pl.ds(0, 64)], send_sem.at[0])
    wait_bytes(mine.at[x, p, 0:7, rows(ROW_C)], send_sem.at[1])
    wait_bytes(mine.at[x, 0:7, :, rows(ROW_C)], send_sem.at[2])
    wait_bytes(mine.at[0:3, :, :, rows(ROW_C)], send_sem.at[3])
    wait_bytes(mine.at[:, p, 0:7, rows(ROW_A)], send_sem.at[4])
    wait_bytes(mine.at[:, 0:7, q, rows(ROW_B)], send_sem.at[5])
    wait_bytes(mine.at[:, 0:7, :, rows(ROW_A)], send_sem.at[6])
    wait_bytes(mine.at[:, :, 0:7, rows(ROW_B)], send_sem.at[7])
    wait_bytes(emb_out.at[pl.ds(0, SEQ - 1)], emb_sem.at[0])
    wait_bytes(mine, core_sem.at[0])
    wait_bytes(other, core_sem.at[1])


def hit_of(targets_ref, block_index):
    row_start = (lax.axis_index("vocab") * SEQ + lax.axis_index("seq")) * ROWS
    row_ids = lax.broadcasted_iota(jnp.int32, (ROWS, TOK), 0)
    return (targets_ref[pl.ds(block_index, 1), :] - row_start) == row_ids


def logits_kernel(g, table_ref, targets_ref, logit, stat):
    def step(z_at, carry):
        columns = []
        for xl in range(2):
            halves = []
            for xh in range(2):
                even = g[0, 2 * xh + xl, z_at]
                odd = g[1, 2 * xh + xl, :, z_at]
                halves.append(jnp.stack([even, odd], axis=1).reshape(HALF, TOK))
            columns.append(jnp.concatenate(halves, axis=0))
        both = jnp.dot(table_ref[...], jnp.concatenate(columns, axis=1), preferred_element_type=F32)
        for xl in range(2):
            block_index = xl * 8 + z_at
            values = both[:, xl * TOK : (xl + 1) * TOK]
            logit[block_index] = values
            most = jnp.max(values, axis=0, keepdims=True)
            stat[block_index, 0:1, :] = most
            stat[block_index, 1:2, :] = jnp.sum(jnp.exp(values - most), axis=0, keepdims=True)
            hit = hit_of(targets_ref, block_index)
            stat[block_index, 2:3, :] = jnp.sum(jnp.where(hit, values, 0.0), axis=0, keepdims=True)
        return carry

    lax.fori_loop(0, 8, step, 0)


def combine(ref):
    most = jnp.max(ref[:, 0, :], axis=0, keepdims=True)
    total = jnp.sum(ref[:, 1, :] * jnp.exp(ref[:, 0, :] - most), axis=0, keepdims=True)
    return most, total, jnp.sum(ref[:, 2, :], axis=0, keepdims=True)


def stats_kernel(stat, top_in, loss_ref, stat_in, part, part_in, top, stat_sem, part_sem, top_sem):
    v, s = lax.axis_index("vocab"), lax.axis_index("seq")
    barrier = pltpu.get_barrier_semaphore()

    def greet(r, carry):
        pl.semaphore_signal(barrier, inc=1, device_id=(v, lax.rem(s + r, SEQ)), device_id_type=MESH)
        return carry

    def greet_vocab(r, carry):
        pl.semaphore_signal(barrier, inc=1, device_id=(lax.rem(v + r, VOC), s), device_id_type=MESH)
        return carry

    lax.fori_loop(1, SEQ, greet, 0)
    lax.fori_loop(1, VOC, greet_vocab, 0)
    pl.semaphore_wait(barrier, SEQ + VOC - 2)

    def wait_bytes(data, sem):
        pltpu.make_async_copy(data, data, sem).wait()

    def scatter(r, carry):
        j = lax.rem(s + r, SEQ)
        pltpu.make_async_remote_copy(
            src_ref=stat.at[j], dst_ref=stat_in.at[s], send_sem=stat_sem.at[0], recv_sem=stat_sem.at[1],
            device_id=(v, j), device_id_type=MESH,
        ).start()
        return carry

    lax.fori_loop(1, SEQ, scatter, 0)
    stat_in[s] = stat[s]
    wait_bytes(stat_in.at[pl.ds(0, SEQ - 1)], stat_sem.at[1])
    most, total, picked = combine(stat_in)
    part[0:1, :] = most
    part[1:2, :] = total
    part[2:3, :] = picked

    def exchange(r, carry):
        j = lax.rem(v + r, VOC)
        pltpu.make_async_remote_copy(
            src_ref=part, dst_ref=part_in.at[v], send_sem=part_sem.at[0], recv_sem=part_sem.at[1],
            device_id=(j, s), device_id_type=MESH,
        ).start()
        return carry

    lax.fori_loop(1, VOC, exchange, 0)
    part_in[v] = part[...]
    wait_bytes(part_in.at[pl.ds(0, VOC - 1)], part_sem.at[1])
    most, total, picked = combine(part_in)
    top[0:1, :] = most
    top[1:2, :] = 1.0 / total

    def spread(r, carry):
        j = lax.rem(s + r, SEQ)
        pltpu.make_async_remote_copy(
            src_ref=top, dst_ref=top_in.at[s], send_sem=top_sem.at[0], recv_sem=top_sem.at[1],
            device_id=(v, j), device_id_type=MESH,
        ).start()
        return carry

    lax.fori_loop(1, SEQ, spread, 0)
    top_in[s] = top[...]
    loss_ref[...] = most + jnp.log(total) - picked
    wait_bytes(top_in.at[pl.ds(0, SEQ - 1)], top_sem.at[1])
    wait_bytes(stat_in.at[pl.ds(0, SEQ - 1)], stat_sem.at[0])
    wait_bytes(part_in.at[pl.ds(0, VOC - 1)], part_sem.at[0])
    wait_bytes(top_in.at[pl.ds(0, SEQ - 1)], top_sem.at[0])


def head_kernel(g, logit, top_in, targets_ref, emb_rows, emb_hot, loss_in, loss_ref, out_ref, score, out_v, out_sem):
    loss_ref[...] = loss_in[...]

    def score_step(block_index, carry):
        probs = jnp.exp(logit[block_index] - top_in[block_index, 0:1, :]) * top_in[block_index, 1:2, :]
        value = probs - hit_of(targets_ref, block_index).astype(F32)
        score[:, pl.ds(pl.multiple_of(block_index * TOK, TOK), TOK)] = value.astype(BF16)
        return carry

    lax.fori_loop(0, SEQ, score_step, 0)
    hot = emb_hot[...].astype(BF16)
    hot = jnp.concatenate([hot, hot, hot], axis=0)
    width = D // 4

    def head_step(i, carry):
        xh, y_first = lax.div(i, 2), 4 * lax.rem(i, 2)
        columns = []
        for xl in range(2):
            for z_at in range(8):
                even = g[0, 2 * xh + xl, z_at, pl.ds(y_first, 4)]
                odd = g[1, 2 * xh + xl, pl.ds(y_first, 4), z_at]
                columns.append(jnp.stack([even, odd], axis=1).reshape(width, TOK))
        features = jnp.concatenate(columns, axis=1)
        at = pl.ds(pl.multiple_of(i * width, 128), width)
        total = lax.dot_general(score[...], features, (((1,), (1,)), ((), ())), preferred_element_type=F32)
        rest = emb_rows[:, at]
        high = rest.astype(BF16)
        rest = rest - high.astype(F32)
        middle = rest.astype(BF16)
        low = (rest - middle.astype(F32)).astype(BF16)
        terms = jnp.concatenate([high, middle, low], axis=0)
        total += lax.dot_general(hot, terms, (((0,), (0,)), ((), ())), preferred_element_type=F32)
        out_v[:, at] = total.astype(BF16)
        pltpu.make_async_copy(out_v.at[:, at], out_ref.at[:, at], out_sem).start()
        return carry

    lax.fori_loop(0, 4, head_step, 0)
    pltpu.make_async_copy(out_v, out_ref, out_sem).wait()


def on_device(hidden, table, targets, token_ids, input_grad):
    any_space = pl.BlockSpec(memory_space=pl.ANY)
    vmem = pl.BlockSpec(memory_space=pltpu.VMEM)
    dma = pltpu.SemaphoreType.DMA
    targets = targets.reshape(SEQ, TOK)
    g, emb_rows, emb_hot, table, targets = pl.pallas_call(
        gather_kernel,
        out_shape=(
            pltpu.VMEM((2, 4, 8, 8, FEAT, TOK), BF16),
            pltpu.VMEM((SEQ, D), F32),
            pltpu.VMEM((SEQ, ROWS), F32),
            pltpu.VMEM((ROWS, D), BF16),
            pltpu.VMEM((SEQ, TOK), jnp.int32),
        ),
        in_specs=[any_space] * 5,
        out_specs=(vmem,) * 5,
        scratch_shapes=[
            pltpu.VMEM((1, TOK), jnp.int32),
            pltpu.VMEM((TOK, D), BF16),
            pltpu.VMEM((SEQ, 1, EXTRA), F32),
            pltpu.VMEM((SEQ, 1, EXTRA), F32),
            dma((len(MESSAGES),)),
            dma((len(PHASES),)),
            dma((2,)),
            dma((2,)),
            dma((5,)),
        ],
        compiler_params=pltpu.CompilerParams(collective_id=0, has_side_effects=True, vmem_limit_bytes=47 * 2**20),
        name="gather",
    )(hidden.T, token_ids.reshape(1, TOK), input_grad, table, targets)
    logit, stat = pl.pallas_call(
        logits_kernel,
        out_shape=(pltpu.VMEM((SEQ, ROWS, TOK), F32), pltpu.VMEM((SEQ, 8, TOK), F32)),
        in_specs=[vmem, vmem, vmem],
        out_specs=(vmem, vmem),
        compiler_params=pltpu.CompilerParams(vmem_limit_bytes=24 * 2**20),
        cost_estimate=pl.CostEstimate(flops=2 * 2048 * ROWS * D, bytes_accessed=2**21, transcendentals=2048 * ROWS),
        name="logits",
    )(g, table, targets)
    top_in, loss = pl.pallas_call(
        stats_kernel,
        out_shape=(pltpu.VMEM((SEQ, 8, TOK), F32), pltpu.VMEM((1, TOK), F32)),
        in_specs=[vmem],
        out_specs=(vmem, vmem),
        scratch_shapes=[
            pltpu.VMEM((SEQ, 8, TOK), F32),
            pltpu.VMEM((8, TOK), F32),
            pltpu.VMEM((VOC, 8, TOK), F32),
            pltpu.VMEM((8, TOK), F32),
            dma((2,)),
            dma((2,)),
            dma((2,)),
        ],
        compiler_params=pltpu.CompilerParams(collective_id=1, has_side_effects=True, vmem_limit_bytes=4 * 2**20),
        name="stats",
    )(stat)
    loss, table_grad = pl.pallas_call(
        head_kernel,
        out_shape=(jax.ShapeDtypeStruct((1, TOK), F32), jax.ShapeDtypeStruct((ROWS, D), BF16)),
        in_specs=[vmem] * 7,
        out_specs=(vmem, any_space),
        scratch_shapes=[pltpu.VMEM((ROWS, SEQ * TOK), BF16), pltpu.VMEM((ROWS, D), BF16), dma],
        compiler_params=pltpu.CompilerParams(vmem_limit_bytes=24 * 2**20),
        cost_estimate=pl.CostEstimate(flops=2 * 2048 * ROWS * D, bytes_accessed=2**21, transcendentals=2048 * ROWS),
        name="head",
    )(g, logit, top_in, targets, emb_rows, emb_hot, loss)
    return loss.reshape(TOK), table_grad


def solution(mesh):
    in_specs = (P("seq", "vocab"), P(("vocab", "seq"), None), P(), P("seq"), P("seq", None))
    out_specs = (P("seq"), P(("vocab", "seq"), None))
    return jax.shard_map(
        on_device, mesh=mesh, in_specs=in_specs, out_specs=out_specs, check_vma=False
    )
```

```python
import heapq
import itertools

import jax
import jax.numpy as jnp
from jax import lax
from jax.experimental import pallas as pl
from jax.experimental.pallas import tpu as pltpu
from jax.sharding import PartitionSpec as P

MESH = pl.DeviceIdType.MESH
F32 = jnp.float32
BF16 = jnp.bfloat16

D = 3584
TOK = 128
FEAT = 112
ROWS = 250
SEQ = 16
HALF = D // 2
EXTRA = D + 128
LEN_A, LEN_B, LEN_C = 32, 32, 48
GROUP = 4
PAIR = 1


def plan_messages():
    messages = {}

    def put(key, size, axis, hops, deps):
        messages[key] = dict(size=size * 256, axis=axis, hops=hops, deps=list(deps))

    def direct(name, axis, size, rels):
        for rel in rels:
            put((name, 0, 1 if rel > 0 else -1, abs(rel)), size, axis, abs(rel), [])

    def ring(name, unit, axis, size, length, deps, flip, stride=1):
        far = (length // 2, length // 2 - 1)
        for step, most in zip((1, -1), far[::-1] if flip else far):
            for dist in range(1, most + 1):
                hops = (dist - 1) % stride + 1
                put((name, unit, step, dist), size, axis, hops, deps if dist == hops else [(name, unit, step, dist - hops)])

    def item(name, rel, flip):
        rel %= 8
        back = 4 if flip else 3
        if rel == 0:
            return []
        return [(name, 0, -1, rel)] if rel <= back else [(name, 0, 1, 8 - rel)]

    def of(*names):
        return [key for key in messages if key[0] in names]

    whole = {
        1: {rel: (rel,) for rel in (0, 1, 7, 2, 6, 3, 5, 4)},
        2: {0: (1, -1), 1: (1, 2, 3), 3: (-1, -2, -3), 2: (2, 3, 4, 5, 6)},
        4: {0: (1, 2, 3, -1, -2, -3), 1: tuple(range(1, 8))},
    }
    direct("CQ", "q", LEN_C, (1, -1, 2, -2, 3, -3, 4))
    direct("XA", "x", LEN_A, (1, -1, 2))
    direct("XB", "x", LEN_B, (1, -1, 2))
    ring("CP", 0, "p", 8 * LEN_C, 8, of("CQ"), False)
    for unit, rels in whole[PAIR].items():
        deps = of("CQ") + [key for rel in rels for key in item("CP", rel, False)]
        ring("CX", unit, "x", PAIR * 8 * LEN_C, 4, deps, unit % 2 == 1)
    ring("AQ", 0, "q", 4 * LEN_A, 8, of("XA"), False, 2)
    ring("BP", 0, "p", 4 * LEN_B, 8, of("XB"), True, 2)
    for name, axis, first, source, flip, size in (("AP", "p", "XA", "AQ", False, LEN_A), ("BQ", "q", "XB", "BP", True, LEN_B)):
        for unit, rels in whole[GROUP].items():
            deps = of(first) + [key for rel in rels for key in item(source, rel, flip)]
            ring(name, unit, axis, 4 * GROUP * size, 8, deps, unit % 2 == 1)
    put(("SA", 0, 0, 0), 32 * LEN_A, "s", 1, of("XA", "AQ"))
    put(("SB", 0, 0, 0), 32 * LEN_B, "s", 1, of("XB", "BP"))
    put(("SC", 0, 0, 0), 64 * LEN_C, "s", 1, of("CQ", "CP"))
    for rel in range(1, 8):
        for name, source, size in (("SA", "AP", LEN_A), ("SB", "BQ", LEN_B)):
            put((name, rel, 0, 0), 32 * size, "s", 1, [k for k in of(source) if (-k[2] * k[3]) % 8 == rel])
    for key in of("CX"):
        put(("SC",) + key, PAIR * 8 * LEN_C, "s", 1, [key])
    return messages


def plan_order(messages):
    turned = {"x": "x", "p": "q", "q": "p", "s": "s"}
    counter = itertools.count()
    link, free, events = {}, [0.0, 0.0], []
    arrival = [{}, {}]
    waits = [{key: set(m["deps"]) for key, m in messages.items()} for _ in range(2)]
    after = {}
    for key, m in messages.items():
        for dep in m["deps"]:
            after.setdefault(dep, []).append(key)

    def start(core, key, now):
        m = messages[key]
        free[core] = now = max(now, free[core]) + 0.05
        lane = ("s", core) if m["axis"] == "s" else (turned[m["axis"]] if core else m["axis"], key[2])
        rate = 6e5 if m["axis"] == "s" else 8.5e4
        link[lane] = max(now, link.get(lane, 0.0)) + m["size"] * m["hops"] / rate
        heapq.heappush(events, (link[lane] + 3.0 + 0.5 * (m["hops"] - 1), next(counter), core, key))

    for core in range(2):
        for key, m in messages.items():
            if not m["deps"]:
                start(core, key, 0.0)
    while events:
        now, _, core, key = heapq.heappop(events)
        arrival[core][key] = now
        for later in after.get(key, []):
            waits[core][later].discard(key)
            if not waits[core][later]:
                start(core, later, now)
    here = [key for key, m in messages.items() if m["axis"] != "s"]
    return sorted(here, key=lambda key: arrival[0][key] + arrival[1][key])


MESSAGES = plan_messages()
ORDER = plan_order(MESSAGES)
RECV = {key: i for i, key in enumerate(ORDER)}
PHASES = ("XA", "XB", "CQ", "CP", "CX", "AQ", "BP", "AP", "BQ")


def wait_bytes(data, sem):
    pltpu.make_async_copy(data, data, sem).wait()


def gather_kernel(
    hidden_ref, ids_hbm, input_grad_ref, table_ref, targets_ref,
    part_a, part_b, part_c, emb_rows, emb_hot, table_v, targets_v,
    ids_ref, grad_v, emb_out, emb_in,
    recv_sem, send_sem, core_sem, emb_sem, local_sem,
):
    v, s = lax.axis_index("vocab"), lax.axis_index("seq")
    c = lax.rem(v, 2)
    y = lax.rem(lax.div(v, 2), 8)
    z = lax.rem(s, 8)
    x = 2 * lax.div(v, 16) + lax.div(s, 8)
    p = z + c * (y - z)
    q = y + c * (z - y)

    def device(x_at, p_at, q_at):
        z_at = p_at + c * (q_at - p_at)
        y_at = q_at + c * (p_at - q_at)
        return (lax.div(x_at, 2) * 16 + y_at * 2 + c, lax.rem(x_at, 2) * 8 + z_at)

    def turn(at, by, length):
        return lax.rem(at + (by + length), length) if by else at

    sibling = (v + 1 - 2 * c, s)
    a, b, cc = part_a.at[c], part_b.at[c], part_c.at[c]

    own = [
        pltpu.make_async_copy(hidden_ref.at[pl.ds(LEN_A + LEN_B, LEN_C)], cc.at[x, p, q], local_sem.at[0]),
        pltpu.make_async_copy(hidden_ref.at[pl.ds(0, LEN_A)], a.at[p, q, x], local_sem.at[1]),
        pltpu.make_async_copy(hidden_ref.at[pl.ds(LEN_A, LEN_B)], b.at[q, p, x], local_sem.at[2]),
    ]
    ids_copy = pltpu.make_async_copy(ids_hbm, ids_ref, local_sem.at[3])
    grad_copy = pltpu.make_async_copy(input_grad_ref, grad_v, local_sem.at[4])
    targets_copy = pltpu.make_async_copy(targets_ref, targets_v, local_sem.at[5])
    table_copy = pltpu.make_async_copy(table_ref, table_v, local_sem.at[6])
    for copy in own:
        copy.start()

    partners = [device(turn(x, d, 4), p, q) for d in (1, -1, 2)]
    partners += [device(x, turn(p, d, 8), q) for d in (1, -1, 2, -2)]
    partners += [device(x, p, turn(q, d, 8)) for d in (1, -1, 2, -2, 3, -3, 4)]
    partners += [sibling]
    barrier = pltpu.get_barrier_semaphore()
    for partner in partners:
        pl.semaphore_signal(barrier, inc=1, device_id=partner, device_id_type=MESH)
    for copy in (ids_copy, grad_copy, targets_copy, table_copy):
        copy.start()
    for copy in own:
        copy.wait()
    pl.semaphore_wait(barrier, len(partners))

    def group(at, unit, size):
        return pl.ds(size * turn(lax.div(at, size), unit, 8 // size), size)

    def block(key, shift):
        name, unit = key[0], key[1]
        if name == "XA":
            return a.at[p, q, turn(x, shift, 4)]
        if name == "XB":
            return b.at[q, p, turn(x, shift, 4)]
        if name == "CQ":
            return cc.at[x, p, turn(q, shift, 8)]
        if name == "CP":
            return cc.at[x, turn(p, shift, 8)]
        if name == "CX":
            return cc.at[turn(x, shift, 4), group(p, unit, PAIR)]
        if name == "AQ":
            return a.at[p, turn(q, shift, 8)]
        if name == "BP":
            return b.at[q, turn(p, shift, 8)]
        if name == "AP":
            return a.at[turn(p, shift, 8), group(q, unit, GROUP)]
        if name == "BQ":
            return b.at[turn(q, shift, 8), group(p, unit, GROUP)]
        if name == "SA":
            return a.at[turn(p, unit, 8)]
        if name == "SB":
            return b.at[turn(q, unit, 8)]
        return arrived(key[1:]) if unit else cc.at[x]

    def arrived(key):
        return block(key, -key[2] * key[3])

    def send(key):
        m = MESSAGES[key]
        if m["axis"] == "s":
            part = ("SA", "SB", "SC").index(key[0])
            data, target, sems = block(key, 0), sibling, (core_sem.at[0, part], core_sem.at[1, part])
        else:
            by = key[2] * m["hops"]
            data = block(key, -key[2] * (key[3] - m["hops"]))
            target = {
                "x": lambda: device(turn(x, by, 4), p, q),
                "p": lambda: device(x, turn(p, by, 8), q),
                "q": lambda: device(x, p, turn(q, by, 8)),
            }[m["axis"]]()
            sems = send_sem.at[PHASES.index(key[0])], recv_sem.at[RECV[key]]
        pltpu.make_async_remote_copy(
            src_ref=data, dst_ref=data, send_sem=sems[0], recv_sem=sems[1], device_id=target, device_id_type=MESH
        ).start()

    done, sent = set(), set()

    def send_ready():
        for key, m in MESSAGES.items():
            if key not in sent and all(dep in done for dep in m["deps"]):
                sent.add(key)
                send(key)

    def embed_rows():
        ids_copy.wait()
        grad_copy.wait()
        first = lax.broadcasted_iota(jnp.int32, (SEQ, TOK), 0) * ROWS + v * (SEQ * ROWS)
        local = ids_ref[...] - first
        inside = (local >= 0) & (local < ROWS)
        total = jnp.dot(inside.astype(F32).astype(BF16), grad_v[...], preferred_element_type=F32)
        local_id = jnp.max(jnp.where(inside, local, -1).astype(F32), axis=1, keepdims=True)
        tail = jnp.broadcast_to(local_id, (SEQ, 128))
        for j in range(SEQ):
            emb_out[j, :, 0:D] = total[j : j + 1, :]
            emb_out[j, :, D:EXTRA] = tail[j : j + 1, :]
        emb_in[s] = emb_out[s]

        def send_row(r, carry):
            j = lax.rem(s + r, SEQ)
            pltpu.make_async_remote_copy(
                src_ref=emb_out.at[j], dst_ref=emb_in.at[s], send_sem=emb_sem.at[0], recv_sem=emb_sem.at[1],
                device_id=(v, j), device_id_type=MESH,
            ).start()
            return carry

        lax.fori_loop(1, SEQ, send_row, 0)

    def embed_arrived():
        wait_bytes(emb_in.at[pl.ds(0, SEQ - 1)], emb_sem.at[1])
        lane_ids = lax.broadcasted_iota(jnp.int32, (1, ROWS), 1).astype(F32)
        for j in range(SEQ):
            emb_rows[j : j + 1, :] = emb_in[j, :, 0:D]
            emb_hot[j : j + 1, :] = (lane_ids == emb_in[j, :, D : D + 1]).astype(F32)

    send_ready()
    embedded = False
    needed = {key for key in MESSAGES if key[0] in ("XA", "XB", "AQ", "BP")}
    for key in ORDER:
        wait_bytes(arrived(key), recv_sem.at[RECV[key]])
        done.add(key)
        send_ready()
        if not embedded and needed <= done:
            embedded = True
            embed_rows()
        if len(done) == len(ORDER) * 4 // 5:
            embed_arrived()

    targets_copy.wait()
    table_copy.wait()
    wait_bytes(a.at[p, q, 0:3], send_sem.at[0])
    wait_bytes(b.at[q, p, 0:3], send_sem.at[1])
    wait_bytes(cc.at[x, p, 0:7], send_sem.at[2])
    wait_bytes(cc.at[x, 0:7], send_sem.at[3])
    wait_bytes(cc.at[0:3], send_sem.at[4])
    wait_bytes(a.at[p, 0:7], send_sem.at[5])
    wait_bytes(b.at[q, 0:7], send_sem.at[6])
    wait_bytes(a.at[0:7], send_sem.at[7])
    wait_bytes(b.at[0:7], send_sem.at[8])
    wait_bytes(emb_out.at[pl.ds(0, SEQ - 1)], emb_sem.at[0])
    for side in (0, 1):
        for i, data in enumerate((part_a, part_b, part_c)):
            wait_bytes(data.at[1 - c] if side else data.at[c], core_sem.at[side, i])


def hit_of(targets_ref, z_at):
    row_start = (lax.axis_index("vocab") * SEQ + lax.axis_index("seq")) * ROWS
    row_ids = lax.broadcasted_iota(jnp.int32, (ROWS, 2 * TOK), 0)
    both = jnp.concatenate([targets_ref[pl.ds(8 * xl + z_at, 1), :] for xl in range(2)], axis=1)
    return (both - row_start) == row_ids


def features_of(parts, xh, xl, z_at, ys):
    part_a, part_b, part_c = parts
    x = 2 * xh + xl
    even = jnp.concatenate([part_a[0, z_at, ys, x], part_b[0, ys, z_at, x], part_c[0, x, z_at, ys]], axis=1)
    odd = jnp.concatenate([part_a[1, ys, z_at, x], part_b[1, z_at, ys, x], part_c[1, x, ys, z_at]], axis=1)
    both = jnp.stack([even, odd], axis=1)
    return both.reshape(both.shape[0] * 2 * FEAT, TOK)


def combine(ref):
    most = jnp.max(ref[:, 0:2, :], axis=0)
    total = jnp.sum(ref[:, 2:4, :] * jnp.exp(ref[:, 0:2, :] - most), axis=0)
    return most, total, jnp.sum(ref[:, 4:6, :], axis=0)


def logits_kernel(
    part_a, part_b, part_c, table_ref, targets_ref,
    expo, stat, top_in, loss_ref,
    stat_in, part, part_in, more, more_in, top, send_sem, recv_sem,
):
    v, s = lax.axis_index("vocab"), lax.axis_index("seq")
    c, y, xh = lax.rem(v, 2), lax.rem(lax.div(v, 2), 8), lax.div(v, 16)
    z, xl_here = lax.rem(s, 8), lax.div(s, 8)
    side = (2 * xh + xl_here) * 2 + c

    def z_peer(r):
        return (v, xl_here * 8 + lax.rem(z + r, 8))

    def y_peer(r):
        return (xh * 16 + lax.rem(y + r, 8) * 2 + c, s)

    def x_peer(r):
        other = lax.rem(side + r, 8)
        x = lax.div(other, 2)
        return (lax.div(x, 2) * 16 + y * 2 + lax.rem(other, 2), lax.rem(x, 2) * 8 + z)

    barrier = pltpu.get_barrier_semaphore()

    def greet(r, carry):
        for peer in (z_peer(r), y_peer(r), x_peer(r)):
            pl.semaphore_signal(barrier, inc=1, device_id=peer, device_id_type=MESH)
        return carry

    lax.fori_loop(1, 8, greet, 0)

    def copy(phase, data, into, peer):
        pltpu.make_async_remote_copy(
            src_ref=data, dst_ref=into, send_sem=send_sem.at[phase], recv_sem=recv_sem.at[phase],
            device_id=peer, device_id_type=MESH,
        ).start()

    def logits_of(z_at):
        columns = []
        for xl in range(2):
            halves = [features_of((part_a, part_b, part_c), xh, xl, z_at, slice(None)) for xh in range(2)]
            columns.append(jnp.concatenate(halves, axis=0))
        return jnp.dot(table_ref[...], jnp.concatenate(columns, axis=1), preferred_element_type=F32)

    def statistics(z_at):
        values = expo[z_at]
        most = jnp.max(values, axis=0, keepdims=True)
        above = jnp.exp(values - most)
        total = jnp.sum(above, axis=0, keepdims=True)
        picked = jnp.sum(jnp.where(hit_of(targets_ref, z_at), values, 0.0), axis=0, keepdims=True)
        expo[z_at] = above
        for row, value in enumerate((most, total, picked)):
            for xl in range(2):
                stat[z_at, 2 * row + xl : 2 * row + xl + 1, :] = value[:, xl * TOK : (xl + 1) * TOK]

    first = lax.rem(side + 1, 8)
    expo[first] = logits_of(first)
    pl.semaphore_wait(barrier, 21)

    def step(i, carry):
        before, now = lax.rem(side + i, 8), lax.rem(side + 1 + i, 8)
        statistics(before)
        expo[now] = logits_of(now)
        copy(0, stat.at[before], stat_in.at[side], x_peer(i))
        return carry

    lax.fori_loop(1, 8, step, 0)
    statistics(side)
    stat_in[side] = stat[side]
    wait_bytes(stat_in.at[0:7], recv_sem.at[0])

    def merge(source, into):
        most, total, picked = combine(source)
        into[0:2, :] = most
        into[2:4, :] = total
        into[4:6, :] = picked

    merge(stat_in, part)
    for r in range(1, 8):
        copy(1, part, part_in.at[y], y_peer(r))
    part_in[y] = part[...]
    wait_bytes(part_in.at[0:7], recv_sem.at[1])
    merge(part_in, more)
    for r in range(1, 8):
        copy(2, more, more_in.at[z], z_peer(r))
    more_in[z] = more[...]
    wait_bytes(more_in.at[0:7], recv_sem.at[2])
    most, total, picked = combine(more_in)
    top[0:2, :] = most
    top[2:4, :] = 1.0 / total
    top[4:6, :] = most + jnp.log(total) - picked
    for r in range(1, 8):
        copy(3, top, top_in.at[side], x_peer(r))
    top_in[side] = top[...]
    wait_bytes(top_in.at[0:7], recv_sem.at[3])
    loss_ref[...] = jnp.where(xl_here == 0, top_in[z, 4:5, :], top_in[z, 5:6, :])
    for phase, data in enumerate((stat_in, part_in, more_in, top_in)):
        wait_bytes(data.at[0:7], send_sem.at[phase])


def head_kernel(
    part_a, part_b, part_c, expo, stat, top_in, targets_ref, emb_rows, emb_hot, loss_in,
    loss_ref, out_ref,
    score, out_v, out_sem,
):
    loss_ref[...] = loss_in[...]

    def score_step(z_at, carry):
        factor = jnp.exp(stat[z_at, 0:2, :] - top_in[z_at, 0:2, :]) * top_in[z_at, 2:4, :]
        factor = jnp.concatenate([factor[0:1, :], factor[1:2, :]], axis=1)
        value = expo[z_at] * factor - hit_of(targets_ref, z_at).astype(F32)
        score[0:ROWS, pl.ds(pl.multiple_of(z_at * 2 * TOK, 2 * TOK), 2 * TOK)] = value.astype(BF16)
        return carry

    lax.fori_loop(0, 8, score_step, 0)
    hot = emb_hot[...].astype(BF16)
    hot = jnp.concatenate([hot, hot, hot], axis=0)
    width = D // 4

    def head_step(i, carry):
        xh, ys = lax.div(i, 2), pl.ds(4 * lax.rem(i, 2), 4)
        columns = [features_of((part_a, part_b, part_c), xh, xl, z_at, ys) for z_at in range(8) for xl in range(2)]
        features = jnp.concatenate(columns, axis=1)
        at = pl.ds(pl.multiple_of(i * width, 128), width)
        turned = lax.dot_general(features, score[...], (((1,), (1,)), ((), ())), preferred_element_type=F32)
        total = jnp.transpose(turned)[0:ROWS, :]
        rest = emb_rows[:, at]
        high = rest.astype(BF16)
        rest = rest - high.astype(F32)
        middle = rest.astype(BF16)
        low = (rest - middle.astype(F32)).astype(BF16)
        terms = jnp.concatenate([high, middle, low], axis=0)
        total += lax.dot_general(hot, terms, (((0,), (0,)), ((), ())), preferred_element_type=F32)
        out_v[:, at] = total.astype(BF16)
        pltpu.make_async_copy(out_v.at[:, at], out_ref.at[:, at], out_sem).start()
        return carry

    lax.fori_loop(0, 4, head_step, 0)
    pltpu.make_async_copy(out_v, out_ref, out_sem).wait()


def on_device(hidden, table, targets, token_ids, input_grad):
    any_space = pl.BlockSpec(memory_space=pl.ANY)
    vmem = pl.BlockSpec(memory_space=pltpu.VMEM)
    dma = pltpu.SemaphoreType.DMA
    tile = pltpu.VMEM((8, TOK), F32)
    tiles = pltpu.VMEM((8, 8, TOK), F32)
    targets = targets.reshape(SEQ, TOK)
    *parts, emb_rows, emb_hot, table, targets = pl.pallas_call(
        gather_kernel,
        out_shape=(
            pltpu.VMEM((2, 8, 8, 4, LEN_A, TOK), BF16),
            pltpu.VMEM((2, 8, 8, 4, LEN_B, TOK), BF16),
            pltpu.VMEM((2, 4, 8, 8, LEN_C, TOK), BF16),
            pltpu.VMEM((SEQ, D), F32),
            pltpu.VMEM((SEQ, ROWS), F32),
            pltpu.VMEM((ROWS, D), BF16),
            pltpu.VMEM((SEQ, TOK), jnp.int32),
        ),
        in_specs=[any_space] * 5,
        out_specs=(vmem,) * 7,
        scratch_shapes=[
            pltpu.VMEM((1, TOK), jnp.int32),
            pltpu.VMEM((TOK, D), BF16),
            pltpu.VMEM((SEQ, 1, EXTRA), F32),
            pltpu.VMEM((SEQ, 1, EXTRA), F32),
            dma((len(ORDER),)),
            dma((len(PHASES),)),
            dma((2, 3)),
            dma((2,)),
            dma((7,)),
        ],
        compiler_params=pltpu.CompilerParams(collective_id=0, has_side_effects=True, vmem_limit_bytes=47 * 2**20),
        name="gather",
    )(hidden.T, token_ids.reshape(1, TOK), input_grad, table, targets)
    expo, stat, top_in, loss = pl.pallas_call(
        logits_kernel,
        out_shape=(pltpu.VMEM((8, ROWS, 2 * TOK), F32), tiles, tiles, pltpu.VMEM((1, TOK), F32)),
        in_specs=[vmem] * 5,
        out_specs=(vmem,) * 4,
        scratch_shapes=[tiles, tile, tiles, tile, tiles, tile, dma((4,)), dma((4,))],
        compiler_params=pltpu.CompilerParams(collective_id=1, has_side_effects=True, vmem_limit_bytes=24 * 2**20),
        cost_estimate=pl.CostEstimate(flops=2 * 2048 * ROWS * D, bytes_accessed=2**21, transcendentals=2048 * ROWS),
        name="logits",
    )(*parts, table, targets)
    loss, table_grad = pl.pallas_call(
        head_kernel,
        out_shape=(jax.ShapeDtypeStruct((1, TOK), F32), jax.ShapeDtypeStruct((ROWS, D), BF16)),
        in_specs=[vmem] * 10,
        out_specs=(vmem, any_space),
        scratch_shapes=[pltpu.VMEM((256, SEQ * TOK), BF16), pltpu.VMEM((ROWS, D), BF16), dma],
        compiler_params=pltpu.CompilerParams(vmem_limit_bytes=24 * 2**20),
        cost_estimate=pl.CostEstimate(flops=2 * 2048 * ROWS * D, bytes_accessed=2**21, transcendentals=2048 * ROWS),
        name="head",
    )(*parts, expo, stat, top_in, targets, emb_rows, emb_hot, loss)
    return loss.reshape(TOK), table_grad


def solution(mesh):
    in_specs = (P("seq", "vocab"), P(("vocab", "seq"), None), P(), P("seq"), P("seq", None))
    out_specs = (P("seq"), P(("vocab", "seq"), None))
    return jax.shard_map(
        on_device, mesh=mesh, in_specs=in_specs, out_specs=out_specs, check_vma=False
    )
```

```python
import heapq
import itertools

import jax
import jax.numpy as jnp
from jax import lax
from jax.experimental import pallas as pl
from jax.experimental.pallas import tpu as pltpu
from jax.sharding import PartitionSpec as P

MESH = pl.DeviceIdType.MESH
F32 = jnp.float32
BF16 = jnp.bfloat16

D = 3584
TOK = 128
FEAT = 112
ROWS = 250
SEQ = 16
HALF = D // 2
EXTRA = D + 128
LEN_A, LEN_B, LEN_C = 32, 32, 48
GROUP = 4
PAIR = 1


def plan_messages():
    messages = {}

    def put(key, size, axis, hops, deps):
        messages[key] = dict(size=size * 256, axis=axis, hops=hops, deps=list(deps))

    def direct(name, axis, size, rels):
        for rel in rels:
            put((name, 0, 1 if rel > 0 else -1, abs(rel)), size, axis, abs(rel), [])

    def ring(name, unit, axis, size, length, deps, flip, stride=1):
        far = (length // 2, length // 2 - 1)
        for step, most in zip((1, -1), far[::-1] if flip else far):
            for dist in range(1, most + 1):
                hops = (dist - 1) % stride + 1
                put((name, unit, step, dist), size, axis, hops, deps if dist == hops else [(name, unit, step, dist - hops)])

    def item(name, rel, flip):
        rel %= 8
        back = 4 if flip else 3
        if rel == 0:
            return []
        return [(name, 0, -1, rel)] if rel <= back else [(name, 0, 1, 8 - rel)]

    def of(*names):
        return [key for key in messages if key[0] in names]

    whole = {
        1: {rel: (rel,) for rel in (0, 1, 7, 2, 6, 3, 5, 4)},
        2: {0: (1, -1), 1: (1, 2, 3), 3: (-1, -2, -3), 2: (2, 3, 4, 5, 6)},
        4: {0: (1, 2, 3, -1, -2, -3), 1: tuple(range(1, 8))},
    }
    direct("CQ", "q", LEN_C, (1, -1, 2, -2, 3, -3, 4))
    direct("XA", "x", LEN_A, (1, -1, 2))
    direct("XB", "x", LEN_B, (1, -1, 2))
    ring("CP", 0, "p", 8 * LEN_C, 8, of("CQ"), False)
    for unit, rels in whole[PAIR].items():
        deps = of("CQ") + [key for rel in rels for key in item("CP", rel, False)]
        ring("CX", unit, "x", PAIR * 8 * LEN_C, 4, deps, unit % 2 == 1)
    ring("AQ", 0, "q", 4 * LEN_A, 8, of("XA"), False, 2)
    ring("BP", 0, "p", 4 * LEN_B, 8, of("XB"), True, 2)
    for name, axis, first, source, flip, size in (("AP", "p", "XA", "AQ", False, LEN_A), ("BQ", "q", "XB", "BP", True, LEN_B)):
        for unit, rels in whole[GROUP].items():
            deps = of(first) + [key for rel in rels for key in item(source, rel, flip)]
            ring(name, unit, axis, 4 * GROUP * size, 8, deps, unit % 2 == 1)
    put(("SA", 0, 0, 0), 32 * LEN_A, "s", 1, of("XA", "AQ"))
    put(("SB", 0, 0, 0), 32 * LEN_B, "s", 1, of("XB", "BP"))
    put(("SC", 0, 0, 0), 64 * LEN_C, "s", 1, of("CQ", "CP"))
    for rel in range(1, 8):
        for name, source, size in (("SA", "AP", LEN_A), ("SB", "BQ", LEN_B)):
            put((name, rel, 0, 0), 32 * size, "s", 1, [k for k in of(source) if (-k[2] * k[3]) % 8 == rel])
    for key in of("CX"):
        put(("SC",) + key, PAIR * 8 * LEN_C, "s", 1, [key])
    return messages


def plan_order(messages):
    turned = {"x": "x", "p": "q", "q": "p", "s": "s"}
    counter = itertools.count()
    link, free, events = {}, [0.0, 0.0], []
    arrival = [{}, {}]
    waits = [{key: set(m["deps"]) for key, m in messages.items()} for _ in range(2)]
    after = {}
    for key, m in messages.items():
        for dep in m["deps"]:
            after.setdefault(dep, []).append(key)

    def start(core, key, now):
        m = messages[key]
        free[core] = now = max(now, free[core]) + 0.05
        lane = ("s", core) if m["axis"] == "s" else (turned[m["axis"]] if core else m["axis"], key[2])
        rate = 6e5 if m["axis"] == "s" else 8.5e4
        link[lane] = max(now, link.get(lane, 0.0)) + m["size"] * m["hops"] / rate
        heapq.heappush(events, (link[lane] + 3.0 + 0.5 * (m["hops"] - 1), next(counter), core, key))

    for core in range(2):
        for key, m in messages.items():
            if not m["deps"]:
                start(core, key, 0.0)
    while events:
        now, _, core, key = heapq.heappop(events)
        arrival[core][key] = now
        for later in after.get(key, []):
            waits[core][later].discard(key)
            if not waits[core][later]:
                start(core, later, now)
    here = [key for key, m in messages.items() if m["axis"] != "s"]
    return sorted(here, key=lambda key: arrival[0][key] + arrival[1][key])


MESSAGES = plan_messages()
ORDER = plan_order(MESSAGES)
RECV = {key: i for i, key in enumerate(ORDER)}
PHASES = ("XA", "XB", "CQ", "CP", "CX", "AQ", "BP", "AP", "BQ")


def wait_bytes(data, sem):
    pltpu.make_async_copy(data, data, sem).wait()


def gather_kernel(
    hidden_ref, ids_hbm, input_grad_ref, table_ref, targets_ref,
    part_a, part_b, part_c, emb_rows, emb_hot, table_v, targets_v,
    ids_ref, grad_v, emb_out, emb_in,
    recv_sem, send_sem, core_sem, emb_sem, local_sem,
):
    v, s = lax.axis_index("vocab"), lax.axis_index("seq")
    c = lax.rem(v, 2)
    y = lax.rem(lax.div(v, 2), 8)
    z = lax.rem(s, 8)
    x = 2 * lax.div(v, 16) + lax.div(s, 8)
    p = z + c * (y - z)
    q = y + c * (z - y)

    def device(x_at, p_at, q_at):
        z_at = p_at + c * (q_at - p_at)
        y_at = q_at + c * (p_at - q_at)
        return (lax.div(x_at, 2) * 16 + y_at * 2 + c, lax.rem(x_at, 2) * 8 + z_at)

    def turn(at, by, length):
        return lax.rem(at + (by + length), length) if by else at

    sibling = (v + 1 - 2 * c, s)
    a, b, cc = part_a.at[c], part_b.at[c], part_c.at[c]

    own = [
        pltpu.make_async_copy(hidden_ref.at[pl.ds(LEN_A + LEN_B, LEN_C)], cc.at[x, p, q], local_sem.at[0]),
        pltpu.make_async_copy(hidden_ref.at[pl.ds(0, LEN_A)], a.at[p, q, x], local_sem.at[1]),
        pltpu.make_async_copy(hidden_ref.at[pl.ds(LEN_A, LEN_B)], b.at[q, p, x], local_sem.at[2]),
    ]
    ids_copy = pltpu.make_async_copy(ids_hbm, ids_ref, local_sem.at[3])
    grad_copy = pltpu.make_async_copy(input_grad_ref, grad_v, local_sem.at[4])
    targets_copy = pltpu.make_async_copy(targets_ref, targets_v, local_sem.at[5])
    table_copy = pltpu.make_async_copy(table_ref, table_v, local_sem.at[6])
    for copy in own:
        copy.start()

    partners = [device(turn(x, d, 4), p, q) for d in (1, -1, 2)]
    partners += [device(x, turn(p, d, 8), q) for d in (1, -1, 2, -2)]
    partners += [device(x, p, turn(q, d, 8)) for d in (1, -1, 2, -2, 3, -3, 4)]
    partners += [sibling]
    barrier = pltpu.get_barrier_semaphore()
    for partner in partners:
        pl.semaphore_signal(barrier, inc=1, device_id=partner, device_id_type=MESH)
    for copy in (ids_copy, grad_copy, targets_copy, table_copy):
        copy.start()
    for copy in own:
        copy.wait()
    pl.semaphore_wait(barrier, len(partners))

    def group(at, unit, size):
        return pl.ds(size * turn(lax.div(at, size), unit, 8 // size), size)

    def block(key, shift):
        name, unit = key[0], key[1]
        if name == "XA":
            return a.at[p, q, turn(x, shift, 4)]
        if name == "XB":
            return b.at[q, p, turn(x, shift, 4)]
        if name == "CQ":
            return cc.at[x, p, turn(q, shift, 8)]
        if name == "CP":
            return cc.at[x, turn(p, shift, 8)]
        if name == "CX":
            return cc.at[turn(x, shift, 4), group(p, unit, PAIR)]
        if name == "AQ":
            return a.at[p, turn(q, shift, 8)]
        if name == "BP":
            return b.at[q, turn(p, shift, 8)]
        if name == "AP":
            return a.at[turn(p, shift, 8), group(q, unit, GROUP)]
        if name == "BQ":
            return b.at[turn(q, shift, 8), group(p, unit, GROUP)]
        if name == "SA":
            return a.at[turn(p, unit, 8)]
        if name == "SB":
            return b.at[turn(q, unit, 8)]
        return arrived(key[1:]) if unit else cc.at[x]

    def arrived(key):
        return block(key, -key[2] * key[3])

    def send(key):
        m = MESSAGES[key]
        if m["axis"] == "s":
            part = ("SA", "SB", "SC").index(key[0])
            data, target, sems = block(key, 0), sibling, (core_sem.at[0, part], core_sem.at[1, part])
        else:
            by = key[2] * m["hops"]
            data = block(key, -key[2] * (key[3] - m["hops"]))
            target = {
                "x": lambda: device(turn(x, by, 4), p, q),
                "p": lambda: device(x, turn(p, by, 8), q),
                "q": lambda: device(x, p, turn(q, by, 8)),
            }[m["axis"]]()
            sems = send_sem.at[PHASES.index(key[0])], recv_sem.at[RECV[key]]
        pltpu.make_async_remote_copy(
            src_ref=data, dst_ref=data, send_sem=sems[0], recv_sem=sems[1], device_id=target, device_id_type=MESH
        ).start()

    done, sent = set(), set()

    def send_ready():
        for key, m in MESSAGES.items():
            if key not in sent and all(dep in done for dep in m["deps"]):
                sent.add(key)
                send(key)

    def embed_rows():
        ids_copy.wait()
        grad_copy.wait()
        first = lax.broadcasted_iota(jnp.int32, (SEQ, TOK), 0) * ROWS + v * (SEQ * ROWS)
        local = ids_ref[...] - first
        inside = (local >= 0) & (local < ROWS)
        total = jnp.dot(inside.astype(F32).astype(BF16), grad_v[...], preferred_element_type=F32)
        local_id = jnp.max(jnp.where(inside, local, -1).astype(F32), axis=1, keepdims=True)
        tail = jnp.broadcast_to(local_id, (SEQ, 128))
        for j in range(SEQ):
            emb_out[j, :, 0:D] = total[j : j + 1, :]
            emb_out[j, :, D:EXTRA] = tail[j : j + 1, :]
        emb_in[s] = emb_out[s]

        def send_row(r, carry):
            j = lax.rem(s + r, SEQ)
            pltpu.make_async_remote_copy(
                src_ref=emb_out.at[j], dst_ref=emb_in.at[s], send_sem=emb_sem.at[0], recv_sem=emb_sem.at[1],
                device_id=(v, j), device_id_type=MESH,
            ).start()
            return carry

        lax.fori_loop(1, SEQ, send_row, 0)

    def embed_arrived():
        wait_bytes(emb_in.at[pl.ds(0, SEQ - 1)], emb_sem.at[1])
        lane_ids = lax.broadcasted_iota(jnp.int32, (1, 256), 1).astype(F32)
        for j in range(SEQ):
            emb_rows[j : j + 1, :] = emb_in[j, :, 0:D]
            emb_hot[j : j + 1, :] = (lane_ids == emb_in[j, :, D : D + 1]).astype(F32)

    send_ready()
    embedded = False
    needed = {key for key in MESSAGES if key[0] in ("XA", "XB", "AQ", "BP")}
    for key in ORDER:
        wait_bytes(arrived(key), recv_sem.at[RECV[key]])
        done.add(key)
        send_ready()
        if not embedded and needed <= done:
            embedded = True
            embed_rows()
        if len(done) == len(ORDER) * 4 // 5:
            embed_arrived()

    targets_copy.wait()
    table_copy.wait()
    wait_bytes(a.at[p, q, 0:3], send_sem.at[0])
    wait_bytes(b.at[q, p, 0:3], send_sem.at[1])
    wait_bytes(cc.at[x, p, 0:7], send_sem.at[2])
    wait_bytes(cc.at[x, 0:7], send_sem.at[3])
    wait_bytes(cc.at[0:3], send_sem.at[4])
    wait_bytes(a.at[p, 0:7], send_sem.at[5])
    wait_bytes(b.at[q, 0:7], send_sem.at[6])
    wait_bytes(a.at[0:7], send_sem.at[7])
    wait_bytes(b.at[0:7], send_sem.at[8])
    wait_bytes(emb_out.at[pl.ds(0, SEQ - 1)], emb_sem.at[0])
    for side in (0, 1):
        for i, data in enumerate((part_a, part_b, part_c)):
            wait_bytes(data.at[1 - c] if side else data.at[c], core_sem.at[side, i])


def hit_of(targets_ref, xl, z_at):
    row_start = (lax.axis_index("vocab") * SEQ + lax.axis_index("seq")) * ROWS
    row_ids = lax.broadcasted_iota(jnp.int32, (ROWS, TOK), 0)
    return (targets_ref[pl.ds(8 * xl + z_at, 1), :] - row_start) == row_ids


def features_of(parts, xh, xl, z_at, ys):
    part_a, part_b, part_c = parts
    x = 2 * xh + xl
    even = jnp.concatenate([part_a[0, z_at, ys, x], part_b[0, ys, z_at, x], part_c[0, x, z_at, ys]], axis=1)
    odd = jnp.concatenate([part_a[1, ys, z_at, x], part_b[1, z_at, ys, x], part_c[1, x, ys, z_at]], axis=1)
    both = jnp.stack([even, odd], axis=1)
    return both.reshape(both.shape[0] * 2 * FEAT, TOK)


def combine(ref):
    most = jnp.max(ref[:, 0:1, :], axis=0)
    total = jnp.sum(ref[:, 1:2, :] * jnp.exp(ref[:, 0:1, :] - most), axis=0)
    return most, total, jnp.sum(ref[:, 2:3, :], axis=0)


def fill_score(xl, expo, stat, top_in, targets_ref, score):
    def step(z_at, carry):
        factor = jnp.exp(stat[xl, z_at, 0:1, :] - top_in[xl, z_at, 0:1, :]) * top_in[xl, z_at, 1:2, :]
        value = expo[xl, z_at] * factor - hit_of(targets_ref, xl, z_at).astype(F32)
        score[0:ROWS, pl.ds(pl.multiple_of(z_at * TOK, TOK), TOK)] = value.astype(BF16)
        return carry

    lax.fori_loop(0, 8, step, 0)


def head_block(parts, xl, i, score):
    xh, ys = lax.div(i, 2), pl.ds(4 * lax.rem(i, 2), 4)
    features = jnp.concatenate([features_of(parts, xh, xl, z_at, ys) for z_at in range(8)], axis=1)
    return lax.dot_general(features, score[...], (((1,), (1,)), ((), ())), preferred_element_type=F32)


def logits_kernel(
    part_a, part_b, part_c, table_ref, targets_ref, emb_rows, emb_hot,
    expo, stat, top_in, loss_ref, turned,
    stat_in, part, part_in, more, more_in, top, score, send_sem, recv_sem,
):
    parts = (part_a, part_b, part_c)
    v, s = lax.axis_index("vocab"), lax.axis_index("seq")
    c, y, xh = lax.rem(v, 2), lax.rem(lax.div(v, 2), 8), lax.div(v, 16)
    z, xl_here = lax.rem(s, 8), lax.div(s, 8)
    side = (2 * xh + xl_here) * 2 + c

    def z_peer(r):
        return (v, xl_here * 8 + lax.rem(z + r, 8))

    def y_peer(r):
        return (xh * 16 + lax.rem(y + r, 8) * 2 + c, s)

    def x_peer(r):
        other = lax.rem(side + r, 8)
        x = lax.div(other, 2)
        return (lax.div(x, 2) * 16 + y * 2 + lax.rem(other, 2), lax.rem(x, 2) * 8 + z)

    barrier = pltpu.get_barrier_semaphore()

    def greet(r, carry):
        for peer in (z_peer(r), y_peer(r), x_peer(r)):
            pl.semaphore_signal(barrier, inc=1, device_id=peer, device_id_type=MESH)
        return carry

    lax.fori_loop(1, 8, greet, 0)

    def copy(xl, phase, data, into, peer):
        pltpu.make_async_remote_copy(
            src_ref=data, dst_ref=into, send_sem=send_sem.at[xl, phase], recv_sem=recv_sem.at[xl, phase],
            device_id=peer, device_id_type=MESH,
        ).start()

    def blocks_of(n):
        xl, m = lax.div(n, 4), lax.rem(n, 4)
        return xl, m, [lax.rem(side + 1 + 2 * m + k, 8) for k in range(2)]

    def logits_step(n):
        xl, _, blocks = blocks_of(n)
        columns = [
            jnp.concatenate([features_of(parts, half, xl, z_at, slice(None)) for half in range(2)], axis=0)
            for z_at in blocks
        ]
        values = jnp.dot(table_ref[...], jnp.concatenate(columns, axis=1), preferred_element_type=F32)
        for k, z_at in enumerate(blocks):
            expo[xl, z_at] = values[:, k * TOK : (k + 1) * TOK]

    def statistics_step(n):
        xl, _, blocks = blocks_of(n)
        for z_at in blocks:
            values = expo[xl, z_at]
            most = jnp.max(values, axis=0, keepdims=True)
            above = jnp.exp(values - most)
            stat[xl, z_at, 0:1, :] = most
            stat[xl, z_at, 1:2, :] = jnp.sum(above, axis=0, keepdims=True)
            hit = hit_of(targets_ref, xl, z_at)
            stat[xl, z_at, 2:3, :] = jnp.sum(jnp.where(hit, values, 0.0), axis=0, keepdims=True)
            expo[xl, z_at] = above

    def send_step(n):
        xl, m, blocks = blocks_of(n)
        copy(xl, 0, stat.at[xl, blocks[0]], stat_in.at[xl, side], x_peer(1 + 2 * m))

        @pl.when(m < 3)
        def _():
            copy(xl, 0, stat.at[xl, blocks[1]], stat_in.at[xl, side], x_peer(2 + 2 * m))

    logits_step(jnp.int32(0))
    pl.semaphore_wait(barrier, 21)

    def step(n, carry):
        statistics_step(n - 1)
        logits_step(n)
        send_step(n - 1)
        return carry

    lax.fori_loop(1, 8, step, 0)
    statistics_step(jnp.int32(7))
    send_step(jnp.int32(7))

    def merge(source, into):
        most, total, picked = combine(source)
        into[0:1, :] = most
        into[1:2, :] = total
        into[2:3, :] = picked

    for xl in range(2):
        stat_in[xl, side] = stat[xl, side]
        wait_bytes(stat_in.at[xl, 0:7], recv_sem.at[xl, 0])
        merge(stat_in.at[xl], part.at[xl])
        for r in range(1, 8):
            copy(xl, 1, part.at[xl], part_in.at[xl, y], y_peer(r))
        part_in[xl, y] = part[xl]
    for xl in range(2):
        wait_bytes(part_in.at[xl, 0:7], recv_sem.at[xl, 1])
        merge(part_in.at[xl], more.at[xl])
        for r in range(1, 8):
            copy(xl, 2, more.at[xl], more_in.at[xl, z], z_peer(r))
        more_in[xl, z] = more[xl]
    for xl in range(2):
        wait_bytes(more_in.at[xl, 0:7], recv_sem.at[xl, 2])
        most, total, picked = combine(more_in.at[xl])
        top[xl, 0:1, :] = most
        top[xl, 1:2, :] = 1.0 / total
        top[xl, 2:3, :] = most + jnp.log(total) - picked
        for r in range(1, 8):
            copy(xl, 3, top.at[xl], top_in.at[xl, side], x_peer(r))
        top_in[xl, side] = top[xl]

    hot = emb_hot[...].astype(BF16)
    hot = jnp.concatenate([hot, hot, hot], axis=0)
    wait_bytes(top_in.at[0, 0:7], recv_sem.at[0, 3])
    fill_score(0, expo, stat, top_in, targets_ref, score)

    def head_step(i, carry):
        at = pl.ds(pl.multiple_of(i * (D // 4), 128), D // 4)
        rest = emb_rows[:, at]
        high = rest.astype(BF16)
        rest = rest - high.astype(F32)
        middle = rest.astype(BF16)
        low = (rest - middle.astype(F32)).astype(BF16)
        terms = jnp.concatenate([high, middle, low], axis=0)
        embed = lax.dot_general(terms, hot, (((0,), (0,)), ((), ())), preferred_element_type=F32)
        turned[i] = head_block(parts, 0, i, score) + embed
        return carry

    lax.fori_loop(0, 4, head_step, 0)
    wait_bytes(top_in.at[1, 0:7], recv_sem.at[1, 3])
    loss_ref[...] = top_in[xl_here, z, 2:3, :]
    for xl in range(2):
        for phase, data in enumerate((stat_in, part_in, more_in, top_in)):
            wait_bytes(data.at[xl, 0:7], send_sem.at[xl, phase])


def head_kernel(
    part_a, part_b, part_c, expo, stat, top_in, targets_ref, turned, loss_in,
    loss_ref, out_ref,
    score, out_v, out_sem,
):
    parts = (part_a, part_b, part_c)
    loss_ref[...] = loss_in[...]
    fill_score(1, expo, stat, top_in, targets_ref, score)

    def head_step(i, carry):
        at = pl.ds(pl.multiple_of(i * (D // 4), 128), D // 4)
        total = jnp.transpose(turned[i] + head_block(parts, 1, i, score))
        out_v[:, at] = total[0:ROWS, :].astype(BF16)
        pltpu.make_async_copy(out_v.at[:, at], out_ref.at[:, at], out_sem).start()
        return carry

    lax.fori_loop(0, 4, head_step, 0)
    pltpu.make_async_copy(out_v, out_ref, out_sem).wait()


def on_device(hidden, table, targets, token_ids, input_grad):
    any_space = pl.BlockSpec(memory_space=pl.ANY)
    vmem = pl.BlockSpec(memory_space=pltpu.VMEM)
    dma = pltpu.SemaphoreType.DMA
    tile = pltpu.VMEM((2, 8, TOK), F32)
    tiles = pltpu.VMEM((2, 8, 8, TOK), F32)
    targets = targets.reshape(SEQ, TOK)
    *parts, emb_rows, emb_hot, table, targets = pl.pallas_call(
        gather_kernel,
        out_shape=(
            pltpu.VMEM((2, 8, 8, 4, LEN_A, TOK), BF16),
            pltpu.VMEM((2, 8, 8, 4, LEN_B, TOK), BF16),
            pltpu.VMEM((2, 4, 8, 8, LEN_C, TOK), BF16),
            pltpu.VMEM((SEQ, D), F32),
            pltpu.VMEM((SEQ, 256), F32),
            pltpu.VMEM((ROWS, D), BF16),
            pltpu.VMEM((SEQ, TOK), jnp.int32),
        ),
        in_specs=[any_space] * 5,
        out_specs=(vmem,) * 7,
        scratch_shapes=[
            pltpu.VMEM((1, TOK), jnp.int32),
            pltpu.VMEM((TOK, D), BF16),
            pltpu.VMEM((SEQ, 1, EXTRA), F32),
            pltpu.VMEM((SEQ, 1, EXTRA), F32),
            dma((len(ORDER),)),
            dma((len(PHASES),)),
            dma((2, 3)),
            dma((2,)),
            dma((7,)),
        ],
        compiler_params=pltpu.CompilerParams(collective_id=0, has_side_effects=True, vmem_limit_bytes=47 * 2**20),
        name="gather",
    )(hidden.T, token_ids.reshape(1, TOK), input_grad, table, targets)
    expo, stat, top_in, loss, turned = pl.pallas_call(
        logits_kernel,
        out_shape=(
            pltpu.VMEM((2, 8, ROWS, TOK), F32), tiles, tiles, pltpu.VMEM((1, TOK), F32), pltpu.VMEM((4, D // 4, 256), F32),
        ),
        in_specs=[vmem] * 7,
        out_specs=(vmem,) * 5,
        scratch_shapes=[
            tiles, tile, tiles, tile, tiles, tile, pltpu.VMEM((256, 8 * TOK), BF16), dma((2, 4)), dma((2, 4)),
        ],
        compiler_params=pltpu.CompilerParams(collective_id=1, has_side_effects=True, vmem_limit_bytes=24 * 2**20),
        cost_estimate=pl.CostEstimate(flops=2 * 2048 * ROWS * D, bytes_accessed=2**21, transcendentals=2048 * ROWS),
        name="logits",
    )(*parts, table, targets, emb_rows, emb_hot)
    loss, table_grad = pl.pallas_call(
        head_kernel,
        out_shape=(jax.ShapeDtypeStruct((1, TOK), F32), jax.ShapeDtypeStruct((ROWS, D), BF16)),
        in_specs=[vmem] * 9,
        out_specs=(vmem, any_space),
        scratch_shapes=[pltpu.VMEM((256, 8 * TOK), BF16), pltpu.VMEM((ROWS, D), BF16), dma],
        compiler_params=pltpu.CompilerParams(vmem_limit_bytes=24 * 2**20),
        cost_estimate=pl.CostEstimate(flops=2 * 2048 * ROWS * D, bytes_accessed=2**21, transcendentals=2048 * ROWS),
        name="head",
    )(*parts, expo, stat, top_in, targets, turned, loss)
    return loss.reshape(TOK), table_grad


def solution(mesh):
    in_specs = (P("seq", "vocab"), P(("vocab", "seq"), None), P(), P("seq"), P("seq", None))
    out_specs = (P("seq"), P(("vocab", "seq"), None))
    return jax.shard_map(
        on_device, mesh=mesh, in_specs=in_specs, out_specs=out_specs, check_vma=False
    )
```

```python
import functools
import heapq
import itertools

import jax
import jax.numpy as jnp
from jax import lax
from jax.experimental import pallas as pl
from jax.experimental.pallas import tpu as pltpu
from jax.sharding import PartitionSpec as P

MESH = pl.DeviceIdType.MESH
F32 = jnp.float32
BF16 = jnp.bfloat16

D = 3584
TOK = 128
FEAT = 112
ROWS = 250
SEQ = 16
HALF = D // 2
EXTRA = D + 128
LEN_A, LEN_B, LEN_C = 32, 32, 48
GROUP = 4
PAIR = 1


def plan_messages():
    messages = {}

    def put(key, size, axis, hops, deps):
        messages[key] = dict(size=size * 256, axis=axis, hops=hops, deps=list(deps))

    def direct(name, axis, size, rels):
        for rel in rels:
            put((name, 0, 1 if rel > 0 else -1, abs(rel)), size, axis, abs(rel), [])

    def ring(name, unit, axis, size, length, deps, flip, stride=1):
        far = (length // 2, length // 2 - 1)
        for step, most in zip((1, -1), far[::-1] if flip else far):
            for dist in range(1, most + 1):
                hops = (dist - 1) % stride + 1
                put((name, unit, step, dist), size, axis, hops, deps if dist == hops else [(name, unit, step, dist - hops)])

    def item(name, rel, flip):
        rel %= 8
        back = 4 if flip else 3
        if rel == 0:
            return []
        return [(name, 0, -1, rel)] if rel <= back else [(name, 0, 1, 8 - rel)]

    def of(*names):
        return [key for key in messages if key[0] in names]

    whole = {
        1: {rel: (rel,) for rel in (0, 1, 7, 2, 6, 3, 5, 4)},
        2: {0: (1, -1), 1: (1, 2, 3), 3: (-1, -2, -3), 2: (2, 3, 4, 5, 6)},
        4: {0: (1, 2, 3, -1, -2, -3), 1: tuple(range(1, 8))},
    }
    direct("CQ", "q", LEN_C, (1, -1, 2, -2, 3, -3, 4))
    direct("XA", "x", LEN_A, (1, -1, 2))
    direct("XB", "x", LEN_B, (1, -1, 2))
    ring("CP", 0, "p", 8 * LEN_C, 8, of("CQ"), False)
    for unit, rels in whole[PAIR].items():
        deps = of("CQ") + [key for rel in rels for key in item("CP", rel, False)]
        ring("CX", unit, "x", PAIR * 8 * LEN_C, 4, deps, unit % 2 == 1)
    ring("AQ", 0, "q", 4 * LEN_A, 8, of("XA"), False, 2)
    ring("BP", 0, "p", 4 * LEN_B, 8, of("XB"), True, 2)
    for name, axis, first, source, flip, size in (("AP", "p", "XA", "AQ", False, LEN_A), ("BQ", "q", "XB", "BP", True, LEN_B)):
        for unit, rels in whole[GROUP].items():
            deps = of(first) + [key for rel in rels for key in item(source, rel, flip)]
            ring(name, unit, axis, 4 * GROUP * size, 8, deps, unit % 2 == 1)
    put(("SA", 0, 0, 0), 32 * LEN_A, "s", 1, of("XA", "AQ"))
    put(("SB", 0, 0, 0), 32 * LEN_B, "s", 1, of("XB", "BP"))
    put(("SC", 0, 0, 0), 64 * LEN_C, "s", 1, of("CQ", "CP"))
    for rel in range(1, 8):
        for name, source, size in (("SA", "AP", LEN_A), ("SB", "BQ", LEN_B)):
            put((name, rel, 0, 0), 32 * size, "s", 1, [k for k in of(source) if (-k[2] * k[3]) % 8 == rel])
    for key in of("CX"):
        put(("SC",) + key, PAIR * 8 * LEN_C, "s", 1, [key])
    return messages


def plan_order(messages):
    turned = {"x": "x", "p": "q", "q": "p", "s": "s"}
    counter = itertools.count()
    link, free, events = {}, [0.0, 0.0], []
    arrival = [{}, {}]
    waits = [{key: set(m["deps"]) for key, m in messages.items()} for _ in range(2)]
    after = {}
    for key, m in messages.items():
        for dep in m["deps"]:
            after.setdefault(dep, []).append(key)

    def start(core, key, now):
        m = messages[key]
        free[core] = now = max(now, free[core]) + 0.05
        lane = ("s", core) if m["axis"] == "s" else (turned[m["axis"]] if core else m["axis"], key[2])
        rate = 6e5 if m["axis"] == "s" else 8.5e4
        link[lane] = max(now, link.get(lane, 0.0)) + m["size"] * m["hops"] / rate
        heapq.heappush(events, (link[lane] + 3.0 + 0.5 * (m["hops"] - 1), next(counter), core, key))

    for core in range(2):
        for key, m in messages.items():
            if not m["deps"]:
                start(core, key, 0.0)
    while events:
        now, _, core, key = heapq.heappop(events)
        arrival[core][key] = now
        for later in after.get(key, []):
            waits[core][later].discard(key)
            if not waits[core][later]:
                start(core, later, now)
    here = [key for key, m in messages.items() if m["axis"] != "s"]
    return sorted(here, key=lambda key: arrival[0][key] + arrival[1][key])


MESSAGES = plan_messages()
ORDER = plan_order(MESSAGES)
RECV = {key: i for i, key in enumerate(ORDER)}
PHASES = ("XA", "XB", "CQ", "CP", "CX", "AQ", "BP", "AP", "BQ")


def wait_bytes(data, sem):
    pltpu.make_async_copy(data, data, sem).wait()


def main_kernel(
    hidden_ref, ids_hbm, input_grad_ref, table_ref, targets_hbm,
    part_a, part_b, part_c, targets_ref, expo, stat, top_in, loss_ref, turned,
    table_v, table_c, ids_ref, grad_v, emb_out, emb_in, emb_rows, emb_hot,
    stat_in, part, part_in, more, more_in, top, score,
    recv_sem, send_sem, core_sem, emb_sem, local_sem, round_send, round_recv,
):
    parts = (part_a, part_b, part_c)
    v, s = lax.axis_index("vocab"), lax.axis_index("seq")
    c = lax.rem(v, 2)
    y = lax.rem(lax.div(v, 2), 8)
    z = lax.rem(s, 8)
    x = 2 * lax.div(v, 16) + lax.div(s, 8)
    p = z + c * (y - z)
    q = y + c * (z - y)

    def device(x_at, p_at, q_at):
        z_at = p_at + c * (q_at - p_at)
        y_at = q_at + c * (p_at - q_at)
        return (lax.div(x_at, 2) * 16 + y_at * 2 + c, lax.rem(x_at, 2) * 8 + z_at)

    def turn(at, by, length):
        return lax.rem(at + (by + length), length) if by else at

    sibling = (v + 1 - 2 * c, s)
    a, b, cc = part_a.at[c], part_b.at[c], part_c.at[c]

    own = [
        pltpu.make_async_copy(hidden_ref.at[pl.ds(LEN_A + LEN_B, LEN_C)], cc.at[x, p, q], local_sem.at[0]),
        pltpu.make_async_copy(hidden_ref.at[pl.ds(0, LEN_A)], a.at[p, q, x], local_sem.at[1]),
        pltpu.make_async_copy(hidden_ref.at[pl.ds(LEN_A, LEN_B)], b.at[q, p, x], local_sem.at[2]),
    ]
    ids_copy = pltpu.make_async_copy(ids_hbm, ids_ref, local_sem.at[3])
    grad_copy = pltpu.make_async_copy(input_grad_ref, grad_v, local_sem.at[4])
    targets_copy = pltpu.make_async_copy(targets_hbm, targets_ref, local_sem.at[5])
    table_copy = pltpu.make_async_copy(table_ref, table_v, local_sem.at[6])
    for copy in own:
        copy.start()

    partners = [device(turn(x, d, 4), p, q) for d in (1, -1, 2)]
    partners += [device(x, turn(p, d, 8), q) for d in (1, -1, 2, -2)]
    partners += [device(x, p, turn(q, d, 8)) for d in (1, -1, 2, -2, 3, -3, 4)]
    partners += [sibling]
    barrier = pltpu.get_barrier_semaphore()
    for partner in partners:
        pl.semaphore_signal(barrier, inc=1, device_id=partner, device_id_type=MESH)
    for copy in (ids_copy, grad_copy, targets_copy, table_copy):
        copy.start()
    for copy in own:
        copy.wait()
    pl.semaphore_wait(barrier, len(partners))

    def group(at, unit, size):
        return pl.ds(size * turn(lax.div(at, size), unit, 8 // size), size)

    def block(key, shift):
        name, unit = key[0], key[1]
        if name == "XA":
            return a.at[p, q, turn(x, shift, 4)]
        if name == "XB":
            return b.at[q, p, turn(x, shift, 4)]
        if name == "CQ":
            return cc.at[x, p, turn(q, shift, 8)]
        if name == "CP":
            return cc.at[x, turn(p, shift, 8)]
        if name == "CX":
            return cc.at[turn(x, shift, 4), group(p, unit, PAIR)]
        if name == "AQ":
            return a.at[p, turn(q, shift, 8)]
        if name == "BP":
            return b.at[q, turn(p, shift, 8)]
        if name == "AP":
            return a.at[turn(p, shift, 8), group(q, unit, GROUP)]
        if name == "BQ":
            return b.at[turn(q, shift, 8), group(p, unit, GROUP)]
        if name == "SA":
            return a.at[turn(p, unit, 8)]
        if name == "SB":
            return b.at[turn(q, unit, 8)]
        return arrived(key[1:]) if unit else cc.at[x]

    def arrived(key):
        return block(key, -key[2] * key[3])

    def send(key):
        m = MESSAGES[key]
        if m["axis"] == "s":
            part = ("SA", "SB", "SC").index(key[0])
            data, target, sems = block(key, 0), sibling, (core_sem.at[0, part], core_sem.at[1, part])
        else:
            by = key[2] * m["hops"]
            data = block(key, -key[2] * (key[3] - m["hops"]))
            target = {
                "x": lambda: device(turn(x, by, 4), p, q),
                "p": lambda: device(x, turn(p, by, 8), q),
                "q": lambda: device(x, p, turn(q, by, 8)),
            }[m["axis"]]()
            sems = send_sem.at[PHASES.index(key[0])], recv_sem.at[RECV[key]]
        pltpu.make_async_remote_copy(
            src_ref=data, dst_ref=data, send_sem=sems[0], recv_sem=sems[1], device_id=target, device_id_type=MESH
        ).start()

    done, sent = set(), set()

    def send_ready():
        for key, m in MESSAGES.items():
            if key not in sent and all(dep in done for dep in m["deps"]):
                sent.add(key)
                send(key)

    def embed_rows():
        ids_copy.wait()
        grad_copy.wait()
        first = lax.broadcasted_iota(jnp.int32, (SEQ, TOK), 0) * ROWS + v * (SEQ * ROWS)
        local = ids_ref[...] - first
        inside = (local >= 0) & (local < ROWS)
        total = jnp.dot(inside.astype(F32).astype(BF16), grad_v[...], preferred_element_type=F32)
        local_id = jnp.max(jnp.where(inside, local, -1).astype(F32), axis=1, keepdims=True)
        tail = jnp.broadcast_to(local_id, (SEQ, 128))
        for j in range(SEQ):
            emb_out[j, :, 0:D] = total[j : j + 1, :]
            emb_out[j, :, D:EXTRA] = tail[j : j + 1, :]
        emb_in[s] = emb_out[s]

        def send_row(r, carry):
            j = lax.rem(s + r, SEQ)
            pltpu.make_async_remote_copy(
                src_ref=emb_out.at[j], dst_ref=emb_in.at[s], send_sem=emb_sem.at[0], recv_sem=emb_sem.at[1],
                device_id=(v, j), device_id_type=MESH,
            ).start()
            return carry

        lax.fori_loop(1, SEQ, send_row, 0)

    def embed_arrived():
        wait_bytes(emb_in.at[pl.ds(0, SEQ - 1)], emb_sem.at[1])
        lane_ids = lax.broadcasted_iota(jnp.int32, (1, 256), 1).astype(F32)
        for j in range(SEQ):
            emb_rows[j : j + 1, :] = emb_in[j, :, 0:D]
            emb_hot[j : j + 1, :] = (lane_ids == emb_in[j, :, D : D + 1]).astype(F32)

    def split_columns(core, j):
        n0 = 256 * j
        low = (n0 + FEAT * (n0 // FEAT) + FEAT * core) // 128 * 128
        width = min(768, D - low)
        n = lax.broadcasted_iota(jnp.int32, (width, 256), 1) + n0
        chunk = sum((n >= FEAT * k).astype(jnp.int32) for k in range(n0 // FEAT + 1, (n0 + 255) // FEAT + 1))
        source = n + FEAT * (chunk + n0 // FEAT + core) - low
        pick = (lax.broadcasted_iota(jnp.int32, (width, 256), 0) == source).astype(F32).astype(BF16)
        columns = jnp.dot(table_v[:, low : low + width], pick, preferred_element_type=F32)
        table_c[core, :, n0 : n0 + 256] = columns.astype(BF16)

    splits = [(core, j) for core in range(2) for j in range(HALF // 256)]
    send_ready()
    embedded = False
    needed = {key for key in MESSAGES if key[0] in ("XA", "XB", "AQ", "BP")}
    for key in ORDER:
        wait_bytes(arrived(key), recv_sem.at[RECV[key]])
        done.add(key)
        send_ready()
        if not embedded and needed <= done:
            embedded = True
            embed_rows()
        if len(done) == 20:
            table_copy.wait()
        if len(done) > 20 and splits:
            split_columns(*splits.pop(0))
        if len(done) == len(ORDER) * 4 // 5:
            embed_arrived()

    targets_copy.wait()
    xh, xl_here = lax.div(x, 2), lax.rem(x, 2)
    side = 2 * x + c

    def z_peer(r):
        return (v, xl_here * 8 + lax.rem(z + r, 8))

    def y_peer(r):
        return (xh * 16 + lax.rem(y + r, 8) * 2 + c, s)

    def x_peer(r):
        other = lax.rem(side + r, 8)
        x = lax.div(other, 2)
        return (lax.div(x, 2) * 16 + y * 2 + lax.rem(other, 2), lax.rem(x, 2) * 8 + z)

    def copy(xl, phase, data, into, peer):
        pltpu.make_async_remote_copy(
            src_ref=data, dst_ref=into, send_sem=round_send.at[xl, phase], recv_sem=round_recv.at[xl, phase],
            device_id=peer, device_id_type=MESH,
        ).start()

    def blocks_of(n):
        xl, m = lax.div(n, 4), lax.rem(n, 4)
        return xl, m, [lax.rem(side + 1 + 2 * m + k, 8) for k in range(2)]

    def logits_step(n, core):
        xl, _, blocks = blocks_of(n)
        columns = [
            jnp.concatenate([core_features(parts, core, half, xl, z_at, slice(None)).reshape(HALF // 2, TOK) for half in range(2)], axis=0)
            for z_at in blocks
        ]
        values = jnp.dot(table_c[core], jnp.concatenate(columns, axis=1), preferred_element_type=F32)
        return xl, [(z_at, values[:, k * TOK : (k + 1) * TOK]) for k, z_at in enumerate(blocks)]

    def statistics_step(n):
        xl, _, blocks = blocks_of(n)
        for z_at in blocks:
            values = expo[xl, z_at]
            most = jnp.max(values, axis=0, keepdims=True)
            above = jnp.exp(values - most)
            stat[xl, z_at, 0:1, :] = most
            stat[xl, z_at, 1:2, :] = jnp.sum(above, axis=0, keepdims=True)
            hit = hit_of(targets_ref, xl, z_at)
            stat[xl, z_at, 2:3, :] = jnp.sum(jnp.where(hit, values, 0.0), axis=0, keepdims=True)
            expo[xl, z_at] = above

    def send_step(n):
        xl, m, blocks = blocks_of(n)
        copy(xl, 0, stat.at[xl, blocks[0]], stat_in.at[xl, side], x_peer(1 + 2 * m))

        @pl.when(m < 3)
        def _():
            copy(xl, 0, stat.at[xl, blocks[1]], stat_in.at[xl, side], x_peer(2 + 2 * m))

    def first_pass(core):
        def step(n, carry):
            xl, values = logits_step(n, core)
            for z_at, value in values:
                expo[xl, z_at] = value
            return carry

        lax.fori_loop(0, 8, step, 0)

    def second_pass(core):
        def add(n):
            xl, values = logits_step(n, core)
            for z_at, value in values:
                expo[xl, z_at] += value

        def step(n, carry):
            statistics_step(n - 1)
            add(n)
            send_step(n - 1)
            return carry

        add(jnp.int32(0))
        lax.fori_loop(1, 8, step, 0)

    for core in range(2):
        pl.when(c == core)(functools.partial(first_pass, core))
    for i, data in enumerate((part_a, part_b, part_c)):
        wait_bytes(data.at[1 - c], core_sem.at[1, i])
    for core in range(2):
        pl.when(c == 1 - core)(functools.partial(second_pass, core))
    statistics_step(jnp.int32(7))
    send_step(jnp.int32(7))

    def merge(source, into):
        most, total, picked = combine(source)
        into[0:1, :] = most
        into[1:2, :] = total
        into[2:3, :] = picked

    for xl in range(2):
        stat_in[xl, side] = stat[xl, side]
        wait_bytes(stat_in.at[xl, 0:7], round_recv.at[xl, 0])
        merge(stat_in.at[xl], part.at[xl])
        for r in range(1, 8):
            copy(xl, 1, part.at[xl], part_in.at[xl, y], y_peer(r))
        part_in[xl, y] = part[xl]
    for xl in range(2):
        wait_bytes(part_in.at[xl, 0:7], round_recv.at[xl, 1])
        merge(part_in.at[xl], more.at[xl])
        for r in range(1, 8):
            copy(xl, 2, more.at[xl], more_in.at[xl, z], z_peer(r))
        more_in[xl, z] = more[xl]
    for xl in range(2):
        wait_bytes(more_in.at[xl, 0:7], round_recv.at[xl, 2])
        most, total, picked = combine(more_in.at[xl])
        top[xl, 0:1, :] = most
        top[xl, 1:2, :] = 1.0 / total
        top[xl, 2:3, :] = most + jnp.log(total) - picked
        for r in range(1, 8):
            copy(xl, 3, top.at[xl], top_in.at[xl, side], x_peer(r))
        top_in[xl, side] = top[xl]

    hot = emb_hot[...].astype(BF16)
    hot = jnp.concatenate([hot, hot, hot], axis=0)
    wait_bytes(top_in.at[0, 0:7], round_recv.at[0, 3])
    fill_score(0, expo, stat, top_in, targets_ref, score)

    def head_step(i, carry):
        at = pl.ds(pl.multiple_of(i * (D // 4), 128), D // 4)
        rest = emb_rows[:, at]
        high = rest.astype(BF16)
        rest = rest - high.astype(F32)
        middle = rest.astype(BF16)
        low = (rest - middle.astype(F32)).astype(BF16)
        terms = jnp.concatenate([high, middle, low], axis=0)
        embed = lax.dot_general(terms, hot, (((0,), (0,)), ((), ())), preferred_element_type=F32)
        turned[i] = head_block(parts, 0, i, score) + embed
        return carry

    lax.fori_loop(0, 4, head_step, 0)
    wait_bytes(top_in.at[1, 0:7], round_recv.at[1, 3])
    loss_ref[...] = top_in[xl_here, z, 2:3, :]
    for xl in range(2):
        for phase, data in enumerate((stat_in, part_in, more_in, top_in)):
            wait_bytes(data.at[xl, 0:7], round_send.at[xl, phase])
    wait_bytes(a.at[p, q, 0:3], send_sem.at[0])
    wait_bytes(b.at[q, p, 0:3], send_sem.at[1])
    wait_bytes(cc.at[x, p, 0:7], send_sem.at[2])
    wait_bytes(cc.at[x, 0:7], send_sem.at[3])
    wait_bytes(cc.at[0:3], send_sem.at[4])
    wait_bytes(a.at[p, 0:7], send_sem.at[5])
    wait_bytes(b.at[q, 0:7], send_sem.at[6])
    wait_bytes(a.at[0:7], send_sem.at[7])
    wait_bytes(b.at[0:7], send_sem.at[8])
    wait_bytes(emb_out.at[pl.ds(0, SEQ - 1)], emb_sem.at[0])
    for i, data in enumerate((part_a, part_b, part_c)):
        wait_bytes(data.at[c], core_sem.at[0, i])


def hit_of(targets_ref, xl, z_at):
    row_start = (lax.axis_index("vocab") * SEQ + lax.axis_index("seq")) * ROWS
    row_ids = lax.broadcasted_iota(jnp.int32, (ROWS, TOK), 0)
    return (targets_ref[pl.ds(8 * xl + z_at, 1), :] - row_start) == row_ids


def core_features(parts, core, xh, xl, z_at, ys):
    part_a, part_b, part_c = parts
    x = 2 * xh + xl
    if core == 0:
        return jnp.concatenate([part_a[0, z_at, ys, x], part_b[0, ys, z_at, x], part_c[0, x, z_at, ys]], axis=1)
    return jnp.concatenate([part_a[1, ys, z_at, x], part_b[1, z_at, ys, x], part_c[1, x, ys, z_at]], axis=1)


def features_of(parts, xh, xl, z_at, ys):
    both = jnp.stack([core_features(parts, core, xh, xl, z_at, ys) for core in range(2)], axis=1)
    return both.reshape(both.shape[0] * 2 * FEAT, TOK)


def combine(ref):
    most = jnp.max(ref[:, 0:1, :], axis=0)
    total = jnp.sum(ref[:, 1:2, :] * jnp.exp(ref[:, 0:1, :] - most), axis=0)
    return most, total, jnp.sum(ref[:, 2:3, :], axis=0)


def fill_score(xl, expo, stat, top_in, targets_ref, score):
    def step(z_at, carry):
        factor = jnp.exp(stat[xl, z_at, 0:1, :] - top_in[xl, z_at, 0:1, :]) * top_in[xl, z_at, 1:2, :]
        value = expo[xl, z_at] * factor - hit_of(targets_ref, xl, z_at).astype(F32)
        score[0:ROWS, pl.ds(pl.multiple_of(z_at * TOK, TOK), TOK)] = value.astype(BF16)
        return carry

    lax.fori_loop(0, 8, step, 0)


def head_block(parts, xl, i, score):
    xh, ys = lax.div(i, 2), pl.ds(4 * lax.rem(i, 2), 4)
    features = jnp.concatenate([features_of(parts, xh, xl, z_at, ys) for z_at in range(8)], axis=1)
    return lax.dot_general(features, score[...], (((1,), (1,)), ((), ())), preferred_element_type=F32)


def head_kernel(
    part_a, part_b, part_c, expo, stat, top_in, targets_ref, turned, loss_in,
    loss_ref, out_ref,
    score, out_v, out_sem,
):
    parts = (part_a, part_b, part_c)
    loss_ref[...] = loss_in[...]
    fill_score(1, expo, stat, top_in, targets_ref, score)

    def head_step(i, carry):
        at = pl.ds(pl.multiple_of(i * (D // 4), 128), D // 4)
        total = jnp.transpose(turned[i] + head_block(parts, 1, i, score))
        out_v[:, at] = total[0:ROWS, :].astype(BF16)
        pltpu.make_async_copy(out_v.at[:, at], out_ref.at[:, at], out_sem).start()
        return carry

    lax.fori_loop(0, 4, head_step, 0)
    pltpu.make_async_copy(out_v, out_ref, out_sem).wait()


def on_device(hidden, table, targets, token_ids, input_grad):
    any_space = pl.BlockSpec(memory_space=pl.ANY)
    vmem = pl.BlockSpec(memory_space=pltpu.VMEM)
    dma = pltpu.SemaphoreType.DMA
    tile = pltpu.VMEM((2, 8, TOK), F32)
    tiles = pltpu.VMEM((2, 8, 8, TOK), F32)
    targets = targets.reshape(SEQ, TOK)
    *parts, targets, expo, stat, top_in, loss, turned = pl.pallas_call(
        main_kernel,
        out_shape=(
            pltpu.VMEM((2, 8, 8, 4, LEN_A, TOK), BF16),
            pltpu.VMEM((2, 8, 8, 4, LEN_B, TOK), BF16),
            pltpu.VMEM((2, 4, 8, 8, LEN_C, TOK), BF16),
            pltpu.VMEM((SEQ, TOK), jnp.int32),
            pltpu.VMEM((2, 8, ROWS, TOK), F32),
            tiles,
            tiles,
            pltpu.VMEM((1, TOK), F32),
            pltpu.VMEM((4, D // 4, 256), F32),
        ),
        in_specs=[any_space] * 5,
        out_specs=(vmem,) * 9,
        scratch_shapes=[
            pltpu.VMEM((ROWS, D), BF16),
            pltpu.VMEM((2, ROWS, HALF), BF16),
            pltpu.VMEM((1, TOK), jnp.int32),
            pltpu.VMEM((TOK, D), BF16),
            pltpu.VMEM((SEQ, 1, EXTRA), F32),
            pltpu.VMEM((SEQ, 1, EXTRA), F32),
            pltpu.VMEM((SEQ, D), F32),
            pltpu.VMEM((SEQ, 256), F32),
            tiles, tile, tiles, tile, tiles, tile,
            pltpu.VMEM((256, 8 * TOK), BF16),
            dma((len(ORDER),)),
            dma((len(PHASES),)),
            dma((2, 3)),
            dma((2,)),
            dma((7,)),
            dma((2, 4)),
            dma((2, 4)),
        ],
        compiler_params=pltpu.CompilerParams(collective_id=0, has_side_effects=True, vmem_limit_bytes=41 * 2**20),
        cost_estimate=pl.CostEstimate(flops=3 * 2048 * ROWS * D, bytes_accessed=2**22, transcendentals=2048 * ROWS),
        name="main",
    )(hidden.T, token_ids.reshape(1, TOK), input_grad, table, targets)
    loss, table_grad = pl.pallas_call(
        head_kernel,
        out_shape=(jax.ShapeDtypeStruct((1, TOK), F32), jax.ShapeDtypeStruct((ROWS, D), BF16)),
        in_specs=[vmem] * 9,
        out_specs=(vmem, any_space),
        scratch_shapes=[pltpu.VMEM((256, 8 * TOK), BF16), pltpu.VMEM((ROWS, D), BF16), dma],
        compiler_params=pltpu.CompilerParams(vmem_limit_bytes=14 * 2**20),
        cost_estimate=pl.CostEstimate(flops=2 * 2048 * ROWS * D, bytes_accessed=2**21, transcendentals=2048 * ROWS),
        name="head",
    )(*parts, expo, stat, top_in, targets, turned, loss)
    return loss.reshape(TOK), table_grad


def solution(mesh):
    in_specs = (P("seq", "vocab"), P(("vocab", "seq"), None), P(), P("seq"), P("seq", None))
    out_specs = (P("seq"), P(("vocab", "seq"), None))
    return jax.shard_map(
        on_device, mesh=mesh, in_specs=in_specs, out_specs=out_specs, check_vma=False
    )
```

```python
import functools
import heapq
import itertools

import jax
import jax.numpy as jnp
from jax import lax
from jax.experimental import pallas as pl
from jax.experimental.pallas import tpu as pltpu
from jax.sharding import PartitionSpec as P

MESH = pl.DeviceIdType.MESH
F32 = jnp.float32
BF16 = jnp.bfloat16

D = 3584
TOK = 128
FEAT = 112
ROWS = 250
SEQ = 16
HALF = D // 2
EXTRA = D + 128
LEN_A, LEN_B, LEN_C = 32, 32, 48
GROUP = 4
PAIR = 1


def plan_messages():
    messages = {}

    def put(key, size, axis, hops, deps):
        messages[key] = dict(size=size * 256, axis=axis, hops=hops, deps=list(deps))

    def direct(name, axis, size, rels):
        for rel in rels:
            put((name, 0, 1 if rel > 0 else -1, abs(rel)), size, axis, abs(rel), [])

    def ring(name, unit, axis, size, length, deps, flip, stride=1):
        far = (length // 2, length // 2 - 1)
        for step, most in zip((1, -1), far[::-1] if flip else far):
            for dist in range(1, most + 1):
                hops = (dist - 1) % stride + 1
                put((name, unit, step, dist), size, axis, hops, deps if dist == hops else [(name, unit, step, dist - hops)])

    def item(name, rel, flip):
        rel %= 8
        back = 4 if flip else 3
        if rel == 0:
            return []
        return [(name, 0, -1, rel)] if rel <= back else [(name, 0, 1, 8 - rel)]

    def of(*names):
        return [key for key in messages if key[0] in names]

    whole = {
        1: {rel: (rel,) for rel in (0, 1, 7, 2, 6, 3, 5, 4)},
        2: {0: (1, -1), 1: (1, 2, 3), 3: (-1, -2, -3), 2: (2, 3, 4, 5, 6)},
        4: {0: (1, 2, 3, -1, -2, -3), 1: tuple(range(1, 8))},
    }
    direct("CQ", "q", LEN_C, (1, -1, 2, -2, 3, -3, 4))
    direct("XA", "x", LEN_A, (1, -1, 2))
    direct("XB", "x", LEN_B, (1, -1, 2))
    ring("CP", 0, "p", 8 * LEN_C, 8, of("CQ"), False)
    for unit, rels in whole[PAIR].items():
        deps = of("CQ") + [key for rel in rels for key in item("CP", rel, False)]
        ring("CX", unit, "x", PAIR * 8 * LEN_C, 4, deps, unit % 2 == 1)
    ring("AQ", 0, "q", 4 * LEN_A, 8, of("XA"), False, 2)
    ring("BP", 0, "p", 4 * LEN_B, 8, of("XB"), True, 2)
    for name, axis, first, source, flip, size in (("AP", "p", "XA", "AQ", False, LEN_A), ("BQ", "q", "XB", "BP", True, LEN_B)):
        for unit, rels in whole[GROUP].items():
            deps = of(first) + [key for rel in rels for key in item(source, rel, flip)]
            ring(name, unit, axis, 4 * GROUP * size, 8, deps, unit % 2 == 1)
    put(("SA", 0, 0, 0), 32 * LEN_A, "s", 1, of("XA", "AQ"))
    put(("SB", 0, 0, 0), 32 * LEN_B, "s", 1, of("XB", "BP"))
    put(("SC", 0, 0, 0), 64 * LEN_C, "s", 1, of("CQ", "CP"))
    for rel in range(1, 8):
        for name, source, size in (("SA", "AP", LEN_A), ("SB", "BQ", LEN_B)):
            put((name, rel, 0, 0), 32 * size, "s", 1, [k for k in of(source) if (-k[2] * k[3]) % 8 == rel])
    for key in of("CX"):
        put(("SC",) + key, PAIR * 8 * LEN_C, "s", 1, [key])
    return messages


def plan_order(messages):
    turned = {"x": "x", "p": "q", "q": "p", "s": "s"}
    counter = itertools.count()
    link, free, events = {}, [0.0, 0.0], []
    arrival = [{}, {}]
    waits = [{key: set(m["deps"]) for key, m in messages.items()} for _ in range(2)]
    after = {}
    for key, m in messages.items():
        for dep in m["deps"]:
            after.setdefault(dep, []).append(key)

    def start(core, key, now):
        m = messages[key]
        free[core] = now = max(now, free[core]) + 0.05
        lane = ("s", core) if m["axis"] == "s" else (turned[m["axis"]] if core else m["axis"], key[2])
        rate = 6e5 if m["axis"] == "s" else 8.5e4
        link[lane] = max(now, link.get(lane, 0.0)) + m["size"] * m["hops"] / rate
        heapq.heappush(events, (link[lane] + 3.0 + 0.5 * (m["hops"] - 1), next(counter), core, key))

    for core in range(2):
        for key, m in messages.items():
            if not m["deps"]:
                start(core, key, 0.0)
    while events:
        now, _, core, key = heapq.heappop(events)
        arrival[core][key] = now
        for later in after.get(key, []):
            waits[core][later].discard(key)
            if not waits[core][later]:
                start(core, later, now)
    here = [key for key, m in messages.items() if m["axis"] != "s"]
    return sorted(here, key=lambda key: arrival[0][key] + arrival[1][key])


MESSAGES = plan_messages()
ORDER = plan_order(MESSAGES)
RECV = {key: i for i, key in enumerate(ORDER)}
PHASES = ("XA", "XB", "CQ", "CP", "CX", "AQ", "BP", "AP", "BQ")


def wait_bytes(data, sem):
    pltpu.make_async_copy(data, data, sem).wait()


def main_kernel(
    hidden_ref, ids_hbm, input_grad_ref, table_ref, targets_hbm,
    part_a, part_b, part_c, targets_ref, expo, stat, top_in, loss_ref, turned,
    table_v, table_c, ids_ref, grad_v, emb_out, emb_in, emb_rows, emb_hot,
    stat_in, part, part_in, more, more_in, top, score,
    recv_sem, send_sem, core_sem, emb_sem, local_sem, round_send, round_recv,
):
    parts = (part_a, part_b, part_c)
    v, s = lax.axis_index("vocab"), lax.axis_index("seq")
    c = lax.rem(v, 2)
    y = lax.rem(lax.div(v, 2), 8)
    z = lax.rem(s, 8)
    x = 2 * lax.div(v, 16) + lax.div(s, 8)
    p = z + c * (y - z)
    q = y + c * (z - y)

    def device(x_at, p_at, q_at):
        z_at = p_at + c * (q_at - p_at)
        y_at = q_at + c * (p_at - q_at)
        return (lax.div(x_at, 2) * 16 + y_at * 2 + c, lax.rem(x_at, 2) * 8 + z_at)

    def turn(at, by, length):
        return lax.rem(at + (by + length), length) if by else at

    xh, xl_here = lax.div(x, 2), lax.rem(x, 2)
    side = 2 * x + c

    def z_peer(r):
        return (v, xl_here * 8 + lax.rem(z + r, 8))

    def y_peer(r):
        return (xh * 16 + lax.rem(y + r, 8) * 2 + c, s)

    def x_peer(r):
        other = lax.rem(side + r, 8)
        x_at = lax.div(other, 2)
        return (lax.div(x_at, 2) * 16 + y * 2 + lax.rem(other, 2), lax.rem(x_at, 2) * 8 + z)

    x_peers, y_peers, z_peers = ([peer(r) for r in range(1, 8)] for peer in (x_peer, y_peer, z_peer))
    sibling = (v + 1 - 2 * c, s)
    a, b, cc = part_a.at[c], part_b.at[c], part_c.at[c]

    own = [
        pltpu.make_async_copy(hidden_ref.at[pl.ds(LEN_A + LEN_B, LEN_C)], cc.at[x, p, q], local_sem.at[0]),
        pltpu.make_async_copy(hidden_ref.at[pl.ds(0, LEN_A)], a.at[p, q, x], local_sem.at[1]),
        pltpu.make_async_copy(hidden_ref.at[pl.ds(LEN_A, LEN_B)], b.at[q, p, x], local_sem.at[2]),
    ]
    ids_copy = pltpu.make_async_copy(ids_hbm, ids_ref, local_sem.at[3])
    grad_copy = pltpu.make_async_copy(input_grad_ref, grad_v, local_sem.at[4])
    targets_copy = pltpu.make_async_copy(targets_hbm, targets_ref, local_sem.at[5])
    table_copy = pltpu.make_async_copy(table_ref, table_v, local_sem.at[6])
    for copy in own:
        copy.start()
    table_copy.start()

    partners = [device(turn(x, d, 4), p, q) for d in (1, -1, 2)]
    partners += [device(x, turn(p, d, 8), q) for d in (1, -1, 2, -2)]
    partners += [device(x, p, turn(q, d, 8)) for d in (1, -1, 2, -2, 3, -3, 4)]
    partners += [sibling]
    barrier = pltpu.get_barrier_semaphore()
    for partner in partners:
        pl.semaphore_signal(barrier, inc=1, device_id=partner, device_id_type=MESH)
    for copy in (ids_copy, grad_copy, targets_copy):
        copy.start()

    def split_columns(core, j):
        n0 = 256 * j
        low = (n0 + FEAT * (n0 // FEAT) + FEAT * core) // 128 * 128
        width = min(768, D - low)
        n = lax.broadcasted_iota(jnp.int32, (width, 256), 1) + n0
        chunk = sum((n >= FEAT * k).astype(jnp.int32) for k in range(n0 // FEAT + 1, (n0 + 255) // FEAT + 1))
        source = n + FEAT * (chunk + n0 // FEAT + core) - low
        pick = (lax.broadcasted_iota(jnp.int32, (width, 256), 0) == source).astype(F32).astype(BF16)
        columns = jnp.dot(table_v[:, low : low + width], pick, preferred_element_type=F32)
        table_c[core, :, n0 : n0 + 256] = columns.astype(BF16)

    splits = [(core, j) for core in range(2) for j in range(HALF // 256)]
    table_copy.wait()
    for core, j in splits[:8]:
        split_columns(core, j)
    for copy in own:
        copy.wait()
    pl.semaphore_wait(barrier, len(partners))

    def group(at, unit, size):
        return pl.ds(size * turn(lax.div(at, size), unit, 8 // size), size)

    def block(key, shift):
        name, unit = key[0], key[1]
        if name == "XA":
            return a.at[p, q, turn(x, shift, 4)]
        if name == "XB":
            return b.at[q, p, turn(x, shift, 4)]
        if name == "CQ":
            return cc.at[x, p, turn(q, shift, 8)]
        if name == "CP":
            return cc.at[x, turn(p, shift, 8)]
        if name == "CX":
            return cc.at[turn(x, shift, 4), group(p, unit, PAIR)]
        if name == "AQ":
            return a.at[p, turn(q, shift, 8)]
        if name == "BP":
            return b.at[q, turn(p, shift, 8)]
        if name == "AP":
            return a.at[turn(p, shift, 8), group(q, unit, GROUP)]
        if name == "BQ":
            return b.at[turn(q, shift, 8), group(p, unit, GROUP)]
        if name == "SA":
            return a.at[turn(p, unit, 8)]
        if name == "SB":
            return b.at[turn(q, unit, 8)]
        return arrived(key[1:]) if unit else cc.at[x]

    def arrived(key):
        return block(key, -key[2] * key[3])

    def send(key):
        m = MESSAGES[key]
        if m["axis"] == "s":
            part = ("SA", "SB", "SC").index(key[0])
            data, target, sems = block(key, 0), sibling, (core_sem.at[0, part], core_sem.at[1, part])
        else:
            by = key[2] * m["hops"]
            data = block(key, -key[2] * (key[3] - m["hops"]))
            target = {
                "x": lambda: device(turn(x, by, 4), p, q),
                "p": lambda: device(x, turn(p, by, 8), q),
                "q": lambda: device(x, p, turn(q, by, 8)),
            }[m["axis"]]()
            sems = send_sem.at[PHASES.index(key[0])], recv_sem.at[RECV[key]]
        pltpu.make_async_remote_copy(
            src_ref=data, dst_ref=data, send_sem=sems[0], recv_sem=sems[1], device_id=target, device_id_type=MESH
        ).start()

    done, sent = set(), set()

    def send_ready():
        for key, m in MESSAGES.items():
            if key not in sent and all(dep in done for dep in m["deps"]):
                sent.add(key)
                send(key)

    def embed_rows():
        ids_copy.wait()
        grad_copy.wait()
        first = lax.broadcasted_iota(jnp.int32, (SEQ, TOK), 0) * ROWS + v * (SEQ * ROWS)
        local = ids_ref[...] - first
        inside = (local >= 0) & (local < ROWS)
        total = jnp.dot(inside.astype(F32).astype(BF16), grad_v[...], preferred_element_type=F32)
        local_id = jnp.max(jnp.where(inside, local, -1).astype(F32), axis=1, keepdims=True)
        tail = jnp.broadcast_to(local_id, (SEQ, 128))
        for j in range(SEQ):
            emb_out[j, :, 0:D] = total[j : j + 1, :]
            emb_out[j, :, D:EXTRA] = tail[j : j + 1, :]
        emb_in[s] = emb_out[s]

    def send_row(r):
        j = lax.rem(s + r, SEQ)
        pltpu.make_async_remote_copy(
            src_ref=emb_out.at[j], dst_ref=emb_in.at[s], send_sem=emb_sem.at[0], recv_sem=emb_sem.at[1],
            device_id=(v, j), device_id_type=MESH,
        ).start()

    def embed_arrived():
        wait_bytes(emb_in.at[pl.ds(0, SEQ - 1)], emb_sem.at[1])
        lane_ids = lax.broadcasted_iota(jnp.int32, (1, 256), 1).astype(F32)
        for j in range(SEQ):
            emb_rows[j : j + 1, :] = emb_in[j, :, 0:D]
            emb_hot[j : j + 1, :] = (lane_ids == emb_in[j, :, D : D + 1]).astype(F32)

    needed = {key for key in MESSAGES if key[0] in ("XA", "XB", "AQ", "BP")}
    middle = max(36, 1 + max(ORDER.index(key) for key in needed))
    others = [functools.partial(split_columns, *split) for split in splits[8:]]
    others += [embed_rows] + [functools.partial(send_row, r) for r in range(1, SEQ)]
    send_ready()
    for i, key in enumerate(ORDER):
        wait_bytes(arrived(key), recv_sem.at[RECV[key]])
        done.add(key)
        send_ready()
        if i >= middle and others:
            others.pop(0)()
    assert not others

    targets_copy.wait()
    def copy(xl, phase, data, into, peer):
        pltpu.make_async_remote_copy(
            src_ref=data, dst_ref=into, send_sem=round_send.at[xl, phase], recv_sem=round_recv.at[xl, phase],
            device_id=peer, device_id_type=MESH,
        ).start()

    def blocks_of(n):
        xl, m = lax.div(n, 4), lax.rem(n, 4)
        return xl, m, [lax.rem(side + 1 + 2 * m + k, 8) for k in range(2)]

    def logits_step(n, core):
        xl, _, blocks = blocks_of(n)
        columns = [
            jnp.concatenate([core_features(parts, core, half, xl, z_at, slice(None)).reshape(HALF // 2, TOK) for half in range(2)], axis=0)
            for z_at in blocks
        ]
        values = jnp.dot(table_c[core], jnp.concatenate(columns, axis=1), preferred_element_type=F32)
        return xl, [(z_at, values[:, k * TOK : (k + 1) * TOK]) for k, z_at in enumerate(blocks)]

    def statistics_step(n):
        xl, _, blocks = blocks_of(n)
        for z_at in blocks:
            values = expo[xl, z_at]
            most = jnp.max(values, axis=0, keepdims=True)
            above = jnp.exp(values - most)
            stat[xl, z_at, 0:1, :] = most
            stat[xl, z_at, 1:2, :] = jnp.sum(above, axis=0, keepdims=True)
            hit = hit_of(targets_ref, xl, z_at)
            stat[xl, z_at, 2:3, :] = jnp.sum(jnp.where(hit, values, 0.0), axis=0, keepdims=True)
            expo[xl, z_at] = above

    def send_step(n):
        xl, m, blocks = blocks_of(n)
        copy(xl, 0, stat.at[xl, blocks[0]], stat_in.at[xl, side], x_peer(1 + 2 * m))

        @pl.when(m < 3)
        def _():
            copy(xl, 0, stat.at[xl, blocks[1]], stat_in.at[xl, side], x_peer(2 + 2 * m))

    def first_pass(core):
        def step(n, carry):
            xl, values = logits_step(n, core)
            for z_at, value in values:
                expo[xl, z_at] = value
            return carry

        lax.fori_loop(0, 8, step, 0)

    def second_pass(core):
        def add(n):
            xl, values = logits_step(n, core)
            for z_at, value in values:
                expo[xl, z_at] += value

        def step(n, carry):
            statistics_step(n - 1)
            add(n)
            send_step(n - 1)
            return carry

        add(jnp.int32(0))
        lax.fori_loop(1, 8, step, 0)

    for core in range(2):
        pl.when(c == core)(functools.partial(first_pass, core))
    for i, data in enumerate((part_a, part_b, part_c)):
        wait_bytes(data.at[1 - c], core_sem.at[1, i])
    for core in range(2):
        pl.when(c == 1 - core)(functools.partial(second_pass, core))
    statistics_step(jnp.int32(7))
    send_step(jnp.int32(7))

    def merge(source, into):
        most, total, picked = combine(source)
        into[0:1, :] = most
        into[1:2, :] = total
        into[2:3, :] = picked

    for xl in range(2):
        stat_in[xl, side] = stat[xl, side]
        wait_bytes(stat_in.at[xl, 0:7], round_recv.at[xl, 0])
        merge(stat_in.at[xl], part.at[xl])
        for r in range(1, 8):
            copy(xl, 1, part.at[xl], part_in.at[xl, y], y_peers[r - 1])
        part_in[xl, y] = part[xl]
    for xl in range(2):
        wait_bytes(part_in.at[xl, 0:7], round_recv.at[xl, 1])
        merge(part_in.at[xl], more.at[xl])
        for r in range(1, 8):
            copy(xl, 2, more.at[xl], more_in.at[xl, z], z_peers[r - 1])
        more_in[xl, z] = more[xl]
    embed_arrived()
    for xl in range(2):
        wait_bytes(more_in.at[xl, 0:7], round_recv.at[xl, 2])
        most, total, picked = combine(more_in.at[xl])
        top[xl, 0:1, :] = most
        top[xl, 1:2, :] = 1.0 / total
        top[xl, 2:3, :] = most + jnp.log(total) - picked
        for r in range(1, 8):
            copy(xl, 3, top.at[xl], top_in.at[xl, side], x_peers[r - 1])
        top_in[xl, side] = top[xl]

    hot = emb_hot[...].astype(BF16)
    hot = jnp.concatenate([hot, hot, hot], axis=0)
    wait_bytes(top_in.at[0, 0:7], round_recv.at[0, 3])
    fill_score(0, expo, stat, top_in, targets_ref, score)

    for i in range(4):
        rest = emb_rows[:, i * (D // 4) : (i + 1) * (D // 4)]
        high = rest.astype(BF16)
        rest = rest - high.astype(F32)
        middle = rest.astype(BF16)
        low = (rest - middle.astype(F32)).astype(BF16)
        terms = jnp.concatenate([high, middle, low], axis=0)
        embed = lax.dot_general(terms, hot, (((0,), (0,)), ((), ())), preferred_element_type=F32)
        turned[i] = head_block(parts, 0, i, score) + embed
    wait_bytes(top_in.at[1, 0:7], round_recv.at[1, 3])
    loss_ref[...] = top_in[xl_here, z, 2:3, :]
    for xl in range(2):
        for phase, data in enumerate((stat_in, part_in, more_in, top_in)):
            wait_bytes(data.at[xl, 0:7], round_send.at[xl, phase])
    wait_bytes(a.at[p, q, 0:3], send_sem.at[0])
    wait_bytes(b.at[q, p, 0:3], send_sem.at[1])
    wait_bytes(cc.at[x, p, 0:7], send_sem.at[2])
    wait_bytes(cc.at[x, 0:7], send_sem.at[3])
    wait_bytes(cc.at[0:3], send_sem.at[4])
    wait_bytes(a.at[p, 0:7], send_sem.at[5])
    wait_bytes(b.at[q, 0:7], send_sem.at[6])
    wait_bytes(a.at[0:7], send_sem.at[7])
    wait_bytes(b.at[0:7], send_sem.at[8])
    wait_bytes(emb_out.at[pl.ds(0, SEQ - 1)], emb_sem.at[0])
    for i, data in enumerate((part_a, part_b, part_c)):
        wait_bytes(data.at[c], core_sem.at[0, i])


def hit_of(targets_ref, xl, z_at):
    row_start = (lax.axis_index("vocab") * SEQ + lax.axis_index("seq")) * ROWS
    row_ids = lax.broadcasted_iota(jnp.int32, (ROWS, TOK), 0)
    return (targets_ref[pl.ds(8 * xl + z_at, 1), :] - row_start) == row_ids


def core_features(parts, core, xh, xl, z_at, ys):
    part_a, part_b, part_c = parts
    x = 2 * xh + xl
    if core == 0:
        return jnp.concatenate([part_a[0, z_at, ys, x], part_b[0, ys, z_at, x], part_c[0, x, z_at, ys]], axis=1)
    return jnp.concatenate([part_a[1, ys, z_at, x], part_b[1, z_at, ys, x], part_c[1, x, ys, z_at]], axis=1)


def features_of(parts, xh, xl, z_at, ys):
    both = jnp.stack([core_features(parts, core, xh, xl, z_at, ys) for core in range(2)], axis=1)
    return both.reshape(both.shape[0] * 2 * FEAT, TOK)


def combine(ref):
    most = jnp.max(ref[:, 0:1, :], axis=0)
    total = jnp.sum(ref[:, 1:2, :] * jnp.exp(ref[:, 0:1, :] - most), axis=0)
    return most, total, jnp.sum(ref[:, 2:3, :], axis=0)


def fill_score(xl, expo, stat, top_in, targets_ref, score):
    def step(z_at, carry):
        factor = jnp.exp(stat[xl, z_at, 0:1, :] - top_in[xl, z_at, 0:1, :]) * top_in[xl, z_at, 1:2, :]
        value = expo[xl, z_at] * factor - hit_of(targets_ref, xl, z_at).astype(F32)
        score[0:ROWS, pl.ds(pl.multiple_of(z_at * TOK, TOK), TOK)] = value.astype(BF16)
        return carry

    lax.fori_loop(0, 8, step, 0)


def head_block(parts, xl, i, score):
    xh, ys = i // 2, slice(4 * (i % 2), 4 * (i % 2) + 4)
    features = jnp.concatenate([features_of(parts, xh, xl, z_at, ys) for z_at in range(8)], axis=1)
    return lax.dot_general(features, score[...], (((1,), (1,)), ((), ())), preferred_element_type=F32)


def head_kernel(
    part_a, part_b, part_c, expo, stat, top_in, targets_ref, turned, loss_in,
    loss_ref, out_ref,
    score, out_v, out_sem,
):
    parts = (part_a, part_b, part_c)
    loss_ref[...] = loss_in[...]
    fill_score(1, expo, stat, top_in, targets_ref, score)

    ready = None
    for i in range(5):
        total = (turned[i] + head_block(parts, 1, i, score)).astype(BF16) if i < 4 else None
        if ready is not None:
            at = pl.ds((i - 1) * (D // 4), D // 4)
            out_v[:, at] = jnp.transpose(ready)[0:ROWS, :]
            pltpu.make_async_copy(out_v.at[:, at], out_ref.at[:, at], out_sem).start()
        ready = total
    pltpu.make_async_copy(out_v, out_ref, out_sem).wait()


def on_device(hidden, table, targets, token_ids, input_grad):
    any_space = pl.BlockSpec(memory_space=pl.ANY)
    vmem = pl.BlockSpec(memory_space=pltpu.VMEM)
    dma = pltpu.SemaphoreType.DMA
    tile = pltpu.VMEM((2, 8, TOK), F32)
    tiles = pltpu.VMEM((2, 8, 8, TOK), F32)
    targets = targets.reshape(SEQ, TOK)
    *parts, targets, expo, stat, top_in, loss, turned = pl.pallas_call(
        main_kernel,
        out_shape=(
            pltpu.VMEM((2, 8, 8, 4, LEN_A, TOK), BF16),
            pltpu.VMEM((2, 8, 8, 4, LEN_B, TOK), BF16),
            pltpu.VMEM((2, 4, 8, 8, LEN_C, TOK), BF16),
            pltpu.VMEM((SEQ, TOK), jnp.int32),
            pltpu.VMEM((2, 8, ROWS, TOK), F32),
            tiles,
            tiles,
            pltpu.VMEM((1, TOK), F32),
            pltpu.VMEM((4, D // 4, 256), F32),
        ),
        in_specs=[any_space] * 5,
        out_specs=(vmem,) * 9,
        scratch_shapes=[
            pltpu.VMEM((ROWS, D), BF16),
            pltpu.VMEM((2, ROWS, HALF), BF16),
            pltpu.VMEM((1, TOK), jnp.int32),
            pltpu.VMEM((TOK, D), BF16),
            pltpu.VMEM((SEQ, 1, EXTRA), F32),
            pltpu.VMEM((SEQ, 1, EXTRA), F32),
            pltpu.VMEM((SEQ, D), F32),
            pltpu.VMEM((SEQ, 256), F32),
            tiles, tile, tiles, tile, tiles, tile,
            pltpu.VMEM((256, 8 * TOK), BF16),
            dma((len(ORDER),)),
            dma((len(PHASES),)),
            dma((2, 3)),
            dma((2,)),
            dma((7,)),
            dma((2, 4)),
            dma((2, 4)),
        ],
        compiler_params=pltpu.CompilerParams(collective_id=0, has_side_effects=True, vmem_limit_bytes=41 * 2**20),
        cost_estimate=pl.CostEstimate(flops=3 * 2048 * ROWS * D, bytes_accessed=2**22, transcendentals=2048 * ROWS),
        name="main",
    )(hidden.T, token_ids.reshape(1, TOK), input_grad, table, targets)
    loss, table_grad = pl.pallas_call(
        head_kernel,
        out_shape=(jax.ShapeDtypeStruct((1, TOK), F32), jax.ShapeDtypeStruct((ROWS, D), BF16)),
        in_specs=[vmem] * 9,
        out_specs=(vmem, any_space),
        scratch_shapes=[pltpu.VMEM((256, 8 * TOK), BF16), pltpu.VMEM((ROWS, D), BF16), dma],
        compiler_params=pltpu.CompilerParams(vmem_limit_bytes=14 * 2**20),
        cost_estimate=pl.CostEstimate(flops=2 * 2048 * ROWS * D, bytes_accessed=2**21, transcendentals=2048 * ROWS),
        name="head",
    )(*parts, expo, stat, top_in, targets, turned, loss)
    return loss.reshape(TOK), table_grad


def solution(mesh):
    in_specs = (P("seq", "vocab"), P(("vocab", "seq"), None), P(), P("seq"), P("seq", None))
    out_specs = (P("seq"), P(("vocab", "seq"), None))
    return jax.shard_map(
        on_device, mesh=mesh, in_specs=in_specs, out_specs=out_specs, check_vma=False
    )
```

```python
import functools
import heapq
import itertools

import jax
import jax.numpy as jnp
from jax import lax
from jax.experimental import pallas as pl
from jax.experimental.pallas import tpu as pltpu
from jax.sharding import PartitionSpec as P

MESH = pl.DeviceIdType.MESH
F32 = jnp.float32
BF16 = jnp.bfloat16

D = 3584
TOK = 128
FEAT = 112
ROWS = 250
SEQ = 16
HALF = D // 2
EXTRA = D + 128
LEN_A, LEN_B, LEN_C = 32, 32, 48
GROUP = 4
PAIR = 1


def plan_messages():
    messages = {}

    def put(key, size, axis, hops, deps):
        messages[key] = dict(size=size * 256, axis=axis, hops=hops, deps=list(deps))

    def direct(name, axis, size, rels):
        for rel in rels:
            put((name, 0, 1 if rel > 0 else -1, abs(rel)), size, axis, abs(rel), [])

    def ring(name, unit, axis, size, length, deps, flip, stride=1):
        far = (length // 2, length // 2 - 1)
        for step, most in zip((1, -1), far[::-1] if flip else far):
            for dist in range(1, most + 1):
                hops = (dist - 1) % stride + 1
                put((name, unit, step, dist), size, axis, hops, deps if dist == hops else [(name, unit, step, dist - hops)])

    def item(name, rel, flip):
        rel %= 8
        back = 4 if flip else 3
        if rel == 0:
            return []
        return [(name, 0, -1, rel)] if rel <= back else [(name, 0, 1, 8 - rel)]

    def of(*names):
        return [key for key in messages if key[0] in names]

    whole = {
        1: {rel: (rel,) for rel in (0, 1, 7, 2, 6, 3, 5, 4)},
        2: {0: (1, -1), 1: (1, 2, 3), 3: (-1, -2, -3), 2: (2, 3, 4, 5, 6)},
        4: {0: (1, 2, 3, -1, -2, -3), 1: tuple(range(1, 8))},
    }
    direct("CQ", "q", LEN_C, (1, -1, 2, -2, 3, -3, 4))
    direct("XA", "x", LEN_A, (1, -1, 2))
    direct("XB", "x", LEN_B, (1, -1, 2))
    ring("CP", 0, "p", 8 * LEN_C, 8, of("CQ"), False)
    for unit, rels in whole[PAIR].items():
        deps = of("CQ") + [key for rel in rels for key in item("CP", rel, False)]
        ring("CX", unit, "x", PAIR * 8 * LEN_C, 4, deps, unit % 2 == 1)
    ring("AQ", 0, "q", 4 * LEN_A, 8, of("XA"), False, 2)
    ring("BP", 0, "p", 4 * LEN_B, 8, of("XB"), True, 2)
    for name, axis, first, source, flip, size in (("AP", "p", "XA", "AQ", False, LEN_A), ("BQ", "q", "XB", "BP", True, LEN_B)):
        for unit, rels in whole[GROUP].items():
            deps = of(first) + [key for rel in rels for key in item(source, rel, flip)]
            ring(name, unit, axis, 4 * GROUP * size, 8, deps, unit % 2 == 1)
    put(("SA", 0, 0, 0), 32 * LEN_A, "s", 1, of("XA", "AQ"))
    put(("SB", 0, 0, 0), 32 * LEN_B, "s", 1, of("XB", "BP"))
    put(("SC", 0, 0, 0), 64 * LEN_C, "s", 1, of("CQ", "CP"))
    for rel in range(1, 8):
        for name, source, size in (("SA", "AP", LEN_A), ("SB", "BQ", LEN_B)):
            put((name, rel, 0, 0), 32 * size, "s", 1, [k for k in of(source) if (-k[2] * k[3]) % 8 == rel])
    for key in of("CX"):
        put(("SC",) + key, PAIR * 8 * LEN_C, "s", 1, [key])
    return messages


def plan_order(messages):
    turned = {"x": "x", "p": "q", "q": "p", "s": "s"}
    counter = itertools.count()
    link, free, events = {}, [0.0, 0.0], []
    arrival = [{}, {}]
    waits = [{key: set(m["deps"]) for key, m in messages.items()} for _ in range(2)]
    after = {}
    for key, m in messages.items():
        for dep in m["deps"]:
            after.setdefault(dep, []).append(key)

    def start(core, key, now):
        m = messages[key]
        free[core] = now = max(now, free[core]) + 0.05
        lane = ("s", core) if m["axis"] == "s" else (turned[m["axis"]] if core else m["axis"], key[2])
        rate = 6e5 if m["axis"] == "s" else 8.5e4
        link[lane] = max(now, link.get(lane, 0.0)) + m["size"] * m["hops"] / rate
        heapq.heappush(events, (link[lane] + 3.0 + 0.5 * (m["hops"] - 1), next(counter), core, key))

    for core in range(2):
        for key, m in messages.items():
            if not m["deps"]:
                start(core, key, 0.0)
    while events:
        now, _, core, key = heapq.heappop(events)
        arrival[core][key] = now
        for later in after.get(key, []):
            waits[core][later].discard(key)
            if not waits[core][later]:
                start(core, later, now)
    here = [key for key, m in messages.items() if m["axis"] != "s"]
    return sorted(here, key=lambda key: arrival[0][key] + arrival[1][key])


MESSAGES = plan_messages()
ORDER = plan_order(MESSAGES)
RECV = {key: i for i, key in enumerate(ORDER)}
PHASES = ("XA", "XB", "CQ", "CP", "CX", "AQ", "BP", "AP", "BQ")


def wait_bytes(data, sem):
    pltpu.make_async_copy(data, data, sem).wait()


def main_kernel(
    hidden_ref, ids_hbm, input_grad_ref, table_ref, targets_hbm,
    part_a, part_b, part_c, targets_ref, expo, most, lse, loss_ref, turned,
    table_v, table_c, ids_ref, grad_v, emb_out, emb_in, emb_rows, emb_hot,
    lse_out, lse_in, pick_out, pick_in, score,
    recv_sem, send_sem, core_sem, emb_sem, local_sem, round_send, round_recv,
):
    parts = (part_a, part_b, part_c)
    v, s = lax.axis_index("vocab"), lax.axis_index("seq")
    c = lax.rem(v, 2)
    y = lax.rem(lax.div(v, 2), 8)
    z = lax.rem(s, 8)
    x = 2 * lax.div(v, 16) + lax.div(s, 8)
    p = z + c * (y - z)
    q = y + c * (z - y)

    def device(x_at, p_at, q_at):
        z_at = p_at + c * (q_at - p_at)
        y_at = q_at + c * (p_at - q_at)
        return (lax.div(x_at, 2) * 16 + y_at * 2 + c, lax.rem(x_at, 2) * 8 + z_at)

    def turn(at, by, length):
        return lax.rem(at + (by + length), length) if by else at

    xh, xl_here = lax.div(x, 2), lax.rem(x, 2)
    side = 2 * x + c

    def z_peer(r):
        return (v, xl_here * 8 + lax.rem(z + r, 8))

    def y_peer(r):
        return (xh * 16 + lax.rem(y + r, 8) * 2 + c, s)

    def x_peer(r):
        other = lax.rem(side + r, 8)
        x_at = lax.div(other, 2)
        return (lax.div(x_at, 2) * 16 + y * 2 + lax.rem(other, 2), lax.rem(x_at, 2) * 8 + z)

    x_peers, y_peers, z_peers = ([peer(r) for r in range(1, 8)] for peer in (x_peer, y_peer, z_peer))
    sibling = (v + 1 - 2 * c, s)
    a, b, cc = part_a.at[c], part_b.at[c], part_c.at[c]

    own = [
        pltpu.make_async_copy(hidden_ref.at[pl.ds(LEN_A + LEN_B, LEN_C)], cc.at[x, p, q], local_sem.at[0]),
        pltpu.make_async_copy(hidden_ref.at[pl.ds(0, LEN_A)], a.at[p, q, x], local_sem.at[1]),
        pltpu.make_async_copy(hidden_ref.at[pl.ds(LEN_A, LEN_B)], b.at[q, p, x], local_sem.at[2]),
    ]
    ids_copy = pltpu.make_async_copy(ids_hbm, ids_ref, local_sem.at[3])
    grad_copy = pltpu.make_async_copy(input_grad_ref, grad_v, local_sem.at[4])
    targets_copy = pltpu.make_async_copy(targets_hbm, targets_ref, local_sem.at[5])
    table_copy = pltpu.make_async_copy(table_ref, table_v, local_sem.at[6])
    for copy in own:
        copy.start()
    table_copy.start()

    partners = [device(turn(x, d, 4), p, q) for d in (1, -1, 2)]
    partners += [device(x, turn(p, d, 8), q) for d in (1, -1, 2, -2)]
    partners += [device(x, p, turn(q, d, 8)) for d in (1, -1, 2, -2, 3, -3, 4)]
    partners += [sibling]
    barrier = pltpu.get_barrier_semaphore()
    for partner in partners:
        pl.semaphore_signal(barrier, inc=1, device_id=partner, device_id_type=MESH)
    for copy in (ids_copy, grad_copy, targets_copy):
        copy.start()

    def split_columns(core, j):
        n0 = 256 * j
        low = (n0 + FEAT * (n0 // FEAT) + FEAT * core) // 128 * 128
        width = min(768, D - low)
        n = lax.broadcasted_iota(jnp.int32, (1, 256), 1) + n0
        chunk = sum((n >= FEAT * k).astype(jnp.int32) for k in range(n0 // FEAT + 1, (n0 + 255) // FEAT + 1))
        source = n + FEAT * (chunk + n0 // FEAT + core) - low
        pick = (lax.broadcasted_iota(jnp.int32, (width, 256), 0) == source).astype(F32).astype(BF16)
        columns = jnp.dot(table_v[:, low : low + width], pick, preferred_element_type=F32)
        table_c[core, :, n0 : n0 + 256] = columns.astype(BF16)

    splits = [(core, j) for core in range(2) for j in range(HALF // 256)]
    table_copy.wait()
    for core, j in splits[:8]:
        split_columns(core, j)
    for copy in own:
        copy.wait()
    pl.semaphore_wait(barrier, len(partners))

    def group(at, unit, size):
        return pl.ds(size * turn(lax.div(at, size), unit, 8 // size), size)

    def block(key, shift):
        name, unit = key[0], key[1]
        if name == "XA":
            return a.at[p, q, turn(x, shift, 4)]
        if name == "XB":
            return b.at[q, p, turn(x, shift, 4)]
        if name == "CQ":
            return cc.at[x, p, turn(q, shift, 8)]
        if name == "CP":
            return cc.at[x, turn(p, shift, 8)]
        if name == "CX":
            return cc.at[turn(x, shift, 4), group(p, unit, PAIR)]
        if name == "AQ":
            return a.at[p, turn(q, shift, 8)]
        if name == "BP":
            return b.at[q, turn(p, shift, 8)]
        if name == "AP":
            return a.at[turn(p, shift, 8), group(q, unit, GROUP)]
        if name == "BQ":
            return b.at[turn(q, shift, 8), group(p, unit, GROUP)]
        if name == "SA":
            return a.at[turn(p, unit, 8)]
        if name == "SB":
            return b.at[turn(q, unit, 8)]
        return arrived(key[1:]) if unit else cc.at[x]

    def arrived(key):
        return block(key, -key[2] * key[3])

    def send(key):
        m = MESSAGES[key]
        if m["axis"] == "s":
            part = ("SA", "SB", "SC").index(key[0])
            data, target, sems = block(key, 0), sibling, (core_sem.at[0, part], core_sem.at[1, part])
        else:
            by = key[2] * m["hops"]
            data = block(key, -key[2] * (key[3] - m["hops"]))
            target = {
                "x": lambda: device(turn(x, by, 4), p, q),
                "p": lambda: device(x, turn(p, by, 8), q),
                "q": lambda: device(x, p, turn(q, by, 8)),
            }[m["axis"]]()
            sems = send_sem.at[PHASES.index(key[0])], recv_sem.at[RECV[key]]
        pltpu.make_async_remote_copy(
            src_ref=data, dst_ref=data, send_sem=sems[0], recv_sem=sems[1], device_id=target, device_id_type=MESH
        ).start()

    done, sent = set(), set()

    def send_ready():
        for key, m in MESSAGES.items():
            if key not in sent and all(dep in done for dep in m["deps"]):
                sent.add(key)
                send(key)

    def embed_rows():
        ids_copy.wait()
        grad_copy.wait()
        first = lax.broadcasted_iota(jnp.int32, (SEQ, TOK), 0) * ROWS + v * (SEQ * ROWS)
        local = ids_ref[...] - first
        inside = (local >= 0) & (local < ROWS)
        total = jnp.dot(inside.astype(F32).astype(BF16), grad_v[...], preferred_element_type=F32)
        local_id = jnp.max(jnp.where(inside, local, -1).astype(F32), axis=1, keepdims=True)
        tail = jnp.broadcast_to(local_id, (SEQ, 128))
        for j in range(SEQ):
            emb_out[j, :, 0:D] = total[j : j + 1, :]
            emb_out[j, :, D:EXTRA] = tail[j : j + 1, :]
        emb_in[s] = emb_out[s]

    def send_row(r):
        j = lax.rem(s + r, SEQ)
        pltpu.make_async_remote_copy(
            src_ref=emb_out.at[j], dst_ref=emb_in.at[s], send_sem=emb_sem.at[0], recv_sem=emb_sem.at[1],
            device_id=(v, j), device_id_type=MESH,
        ).start()

    def embed_arrived():
        wait_bytes(emb_in.at[pl.ds(0, SEQ - 1)], emb_sem.at[1])
        lane_ids = lax.broadcasted_iota(jnp.int32, (1, 256), 1).astype(F32)
        for j in range(SEQ):
            emb_rows[j : j + 1, :] = emb_in[j, :, 0:D]
            emb_hot[j : j + 1, :] = (lane_ids == emb_in[j, :, D : D + 1]).astype(F32)

    needed = {key for key in MESSAGES if key[0] in ("XA", "XB", "AQ", "BP")}
    middle = max(36, 1 + max(ORDER.index(key) for key in needed))
    others = [functools.partial(split_columns, *split) for split in splits[8:]]
    others += [embed_rows] + [functools.partial(send_row, r) for r in range(1, SEQ)]
    send_ready()
    for i, key in enumerate(ORDER):
        wait_bytes(arrived(key), recv_sem.at[RECV[key]])
        done.add(key)
        send_ready()
        if i >= middle and others:
            others.pop(0)()
    assert not others

    targets_copy.wait()
    def blocks_of(n):
        return lax.div(n, 4), [2 * lax.rem(n, 4) + k for k in range(2)]

    def logits_step(n, core):
        xl, blocks = blocks_of(n)
        columns = [
            jnp.concatenate([core_features(parts, core, half, xl, z_at, slice(None)).reshape(HALF // 2, TOK) for half in range(2)], axis=0)
            for z_at in blocks
        ]
        values = jnp.dot(table_c[core], jnp.concatenate(columns, axis=1), preferred_element_type=F32)
        return xl, [(z_at, values[:, k * TOK : (k + 1) * TOK]) for k, z_at in enumerate(blocks)]

    def statistics_step(n):
        xl, blocks = blocks_of(n)
        for z_at in blocks:
            values = expo[xl, z_at]
            top = jnp.max(values, axis=0, keepdims=True)
            above = jnp.exp(values - top)
            most[xl, pl.ds(z_at, 1), :] = top
            lse_out[xl, 0, pl.ds(z_at, 1), :] = top + jnp.log(jnp.sum(above, axis=0, keepdims=True))
            hit = hit_of(targets_ref, xl, z_at)
            pick_out[0, pl.ds(8 * xl + z_at, 1), :] = jnp.sum(jnp.where(hit, values, 0.0), axis=0, keepdims=True)
            expo[xl, z_at] = above

    def round_refs(stream, step):
        if stream < 2:
            return lse_out.at[stream, step], lse_in.at[stream, step]
        return pick_out.at[step], pick_in.at[step]

    def send_round(stream, step):
        data, into = round_refs(stream, step)
        here = (side, y, z)[step]
        for peer in (x_peers, y_peers, z_peers)[step]:
            pltpu.make_async_remote_copy(
                src_ref=data, dst_ref=into.at[here], send_sem=round_send.at[stream, step], recv_sem=round_recv.at[stream, step],
                device_id=peer, device_id_type=MESH,
            ).start()
        into[here] = data[...]

    def merged(stream, step):
        _, into = round_refs(stream, step)
        wait_bytes(into.at[0:7], round_recv.at[stream, step])
        values = into[...]
        if stream == 2:
            return jnp.sum(values, axis=0)
        top = jnp.max(values, axis=0)
        return top + jnp.log(jnp.sum(jnp.exp(values - top), axis=0))

    def first_pass(core):
        def step(n, carry):
            xl, values = logits_step(n, core)
            for z_at, value in values:
                expo[xl, z_at] = value
            return carry

        lax.fori_loop(0, 8, step, 0)

    def second_pass(core):
        def add(n):
            xl, values = logits_step(n, core)
            for z_at, value in values:
                expo[xl, z_at] += value

        def step(n, carry):
            statistics_step(n - 1)
            add(n)
            return carry

        add(jnp.int32(0))
        lax.fori_loop(1, 5, step, 0)
        send_round(0, 0)
        lax.fori_loop(5, 8, step, 0)

    for core in range(2):
        pl.when(c == core)(functools.partial(first_pass, core))
    for i, data in enumerate((part_a, part_b, part_c)):
        wait_bytes(data.at[1 - c], core_sem.at[1, i])
    for core in range(2):
        pl.when(c == 1 - core)(functools.partial(second_pass, core))
    statistics_step(jnp.int32(7))
    send_round(1, 0)
    send_round(2, 0)
    for step in range(2):
        for stream in range(3):
            data, _ = round_refs(stream, step + 1)
            data[...] = merged(stream, step)
            send_round(stream, step + 1)
    embed_arrived()

    hot = emb_hot[...].astype(BF16)
    hot = jnp.concatenate([hot, hot, hot], axis=0)
    lse[0] = merged(0, 2)
    fill_score(0, expo, most, lse, targets_ref, score)

    for i in range(4):
        rest = emb_rows[:, i * (D // 4) : (i + 1) * (D // 4)]
        high = rest.astype(BF16)
        rest = rest - high.astype(F32)
        middle = rest.astype(BF16)
        low = (rest - middle.astype(F32)).astype(BF16)
        terms = jnp.concatenate([high, middle, low], axis=0)
        embed = lax.dot_general(terms, hot, (((0,), (0,)), ((), ())), preferred_element_type=F32)
        turned[i] = head_block(parts, 0, i, score) + embed
    lse[1] = merged(1, 2)
    pick_out[3] = merged(2, 2)
    loss_ref[...] = lse[xl_here, pl.ds(z, 1), :] - pick_out[3, pl.ds(8 * xl_here + z, 1), :]
    for stream in range(3):
        for step in range(3):
            wait_bytes(round_refs(stream, step)[1].at[0:7], round_send.at[stream, step])
    wait_bytes(a.at[p, q, 0:3], send_sem.at[0])
    wait_bytes(b.at[q, p, 0:3], send_sem.at[1])
    wait_bytes(cc.at[x, p, 0:7], send_sem.at[2])
    wait_bytes(cc.at[x, 0:7], send_sem.at[3])
    wait_bytes(cc.at[0:3], send_sem.at[4])
    wait_bytes(a.at[p, 0:7], send_sem.at[5])
    wait_bytes(b.at[q, 0:7], send_sem.at[6])
    wait_bytes(a.at[0:7], send_sem.at[7])
    wait_bytes(b.at[0:7], send_sem.at[8])
    wait_bytes(emb_out.at[pl.ds(0, SEQ - 1)], emb_sem.at[0])
    for i, data in enumerate((part_a, part_b, part_c)):
        wait_bytes(data.at[c], core_sem.at[0, i])


def hit_of(targets_ref, xl, z_at):
    row_start = (lax.axis_index("vocab") * SEQ + lax.axis_index("seq")) * ROWS
    row_ids = lax.broadcasted_iota(jnp.int32, (ROWS, TOK), 0)
    return (targets_ref[pl.ds(8 * xl + z_at, 1), :] - row_start) == row_ids


def core_features(parts, core, xh, xl, z_at, ys):
    part_a, part_b, part_c = parts
    x = 2 * xh + xl
    if core == 0:
        return jnp.concatenate([part_a[0, z_at, ys, x], part_b[0, ys, z_at, x], part_c[0, x, z_at, ys]], axis=1)
    return jnp.concatenate([part_a[1, ys, z_at, x], part_b[1, z_at, ys, x], part_c[1, x, ys, z_at]], axis=1)


def features_of(parts, xh, xl, z_at, ys):
    both = jnp.stack([core_features(parts, core, xh, xl, z_at, ys) for core in range(2)], axis=1)
    return both.reshape(both.shape[0] * 2 * FEAT, TOK)


def fill_score(xl, expo, most, lse, targets_ref, score):
    def step(z_at, carry):
        factor = jnp.exp(most[xl, pl.ds(z_at, 1), :] - lse[xl, pl.ds(z_at, 1), :])
        value = expo[xl, z_at] * factor - hit_of(targets_ref, xl, z_at).astype(F32)
        score[0:ROWS, pl.ds(pl.multiple_of(z_at * TOK, TOK), TOK)] = value.astype(BF16)
        return carry

    lax.fori_loop(0, 8, step, 0)


def head_block(parts, xl, i, score):
    xh, ys = i // 2, slice(4 * (i % 2), 4 * (i % 2) + 4)
    features = jnp.concatenate([features_of(parts, xh, xl, z_at, ys) for z_at in range(8)], axis=1)
    return lax.dot_general(features, score[...], (((1,), (1,)), ((), ())), preferred_element_type=F32)


def head_kernel(
    part_a, part_b, part_c, expo, most, lse, targets_ref, turned, loss_in,
    loss_ref, out_ref,
    score, out_v, out_sem,
):
    parts = (part_a, part_b, part_c)
    loss_ref[...] = loss_in[...]
    fill_score(1, expo, most, lse, targets_ref, score)

    ready = None
    for i in range(5):
        total = (turned[i] + head_block(parts, 1, i, score)).astype(BF16) if i < 4 else None
        if ready is not None:
            at = pl.ds((i - 1) * (D // 4), D // 4)
            out_v[:, at] = jnp.transpose(ready)[0:ROWS, :]
            pltpu.make_async_copy(out_v.at[:, at], out_ref.at[:, at], out_sem).start()
        ready = total
    pltpu.make_async_copy(out_v, out_ref, out_sem).wait()


def on_device(hidden, table, targets, token_ids, input_grad):
    any_space = pl.BlockSpec(memory_space=pl.ANY)
    vmem = pl.BlockSpec(memory_space=pltpu.VMEM)
    dma = pltpu.SemaphoreType.DMA
    tiles = pltpu.VMEM((2, 8, TOK), F32)
    targets = targets.reshape(SEQ, TOK)
    *parts, targets, expo, most, lse, loss, turned = pl.pallas_call(
        main_kernel,
        out_shape=(
            pltpu.VMEM((2, 8, 8, 4, LEN_A, TOK), BF16),
            pltpu.VMEM((2, 8, 8, 4, LEN_B, TOK), BF16),
            pltpu.VMEM((2, 4, 8, 8, LEN_C, TOK), BF16),
            pltpu.VMEM((SEQ, TOK), jnp.int32),
            pltpu.VMEM((2, 8, ROWS, TOK), F32),
            tiles,
            tiles,
            pltpu.VMEM((1, TOK), F32),
            pltpu.VMEM((4, D // 4, 256), F32),
        ),
        in_specs=[any_space] * 5,
        out_specs=(vmem,) * 9,
        scratch_shapes=[
            pltpu.VMEM((ROWS, D), BF16),
            pltpu.VMEM((2, ROWS, HALF), BF16),
            pltpu.VMEM((1, TOK), jnp.int32),
            pltpu.VMEM((TOK, D), BF16),
            pltpu.VMEM((SEQ, 1, EXTRA), F32),
            pltpu.VMEM((SEQ, 1, EXTRA), F32),
            pltpu.VMEM((SEQ, D), F32),
            pltpu.VMEM((SEQ, 256), F32),
            pltpu.VMEM((2, 3, 8, TOK), F32),
            pltpu.VMEM((2, 3, 8, 8, TOK), F32),
            pltpu.VMEM((4, SEQ, TOK), F32),
            pltpu.VMEM((3, 8, SEQ, TOK), F32),
            pltpu.VMEM((256, 8 * TOK), BF16),
            dma((len(ORDER),)),
            dma((len(PHASES),)),
            dma((2, 3)),
            dma((2,)),
            dma((7,)),
            dma((3, 3)),
            dma((3, 3)),
        ],
        compiler_params=pltpu.CompilerParams(collective_id=0, has_side_effects=True, vmem_limit_bytes=41 * 2**20),
        cost_estimate=pl.CostEstimate(flops=3 * 2048 * ROWS * D, bytes_accessed=2**22, transcendentals=2048 * ROWS),
        name="main",
    )(hidden.T, token_ids.reshape(1, TOK), input_grad, table, targets)
    loss, table_grad = pl.pallas_call(
        head_kernel,
        out_shape=(jax.ShapeDtypeStruct((1, TOK), F32), jax.ShapeDtypeStruct((ROWS, D), BF16)),
        in_specs=[vmem] * 9,
        out_specs=(vmem, any_space),
        scratch_shapes=[pltpu.VMEM((256, 8 * TOK), BF16), pltpu.VMEM((ROWS, D), BF16), dma],
        compiler_params=pltpu.CompilerParams(vmem_limit_bytes=14 * 2**20),
        cost_estimate=pl.CostEstimate(flops=2 * 2048 * ROWS * D, bytes_accessed=2**21, transcendentals=2048 * ROWS),
        name="head",
    )(*parts, expo, most, lse, targets, turned, loss)
    return loss.reshape(TOK), table_grad


def solution(mesh):
    in_specs = (P("seq", "vocab"), P(("vocab", "seq"), None), P(), P("seq"), P("seq", None))
    out_specs = (P("seq"), P(("vocab", "seq"), None))
    return jax.shard_map(
        on_device, mesh=mesh, in_specs=in_specs, out_specs=out_specs, check_vma=False
    )
```

```python
import functools
import heapq
import itertools

import jax
import jax.numpy as jnp
from jax import lax
from jax.experimental import pallas as pl
from jax.experimental.pallas import tpu as pltpu
from jax.sharding import PartitionSpec as P

MESH = pl.DeviceIdType.MESH
F32 = jnp.float32
BF16 = jnp.bfloat16

D = 3584
TOK = 128
FEAT = 112
ROWS = 250
SEQ = 16
HALF = D // 2
EXTRA = D + 128
LEN_A, LEN_B, LEN_C = 32, 32, 48
GROUP = 2
PAIR = 1


def plan_messages():
    messages = {}

    def put(key, size, axis, hops, deps):
        messages[key] = dict(size=size * 256, axis=axis, hops=hops, deps=list(deps))

    def direct(name, axis, size, rels):
        for rel in rels:
            put((name, 0, 1 if rel > 0 else -1, abs(rel)), size, axis, abs(rel), [])

    def ring(name, unit, axis, size, length, deps, flip, hops_of=(1, 1, 1, 1)):
        far = (length // 2, length // 2 - 1)
        for step, most in zip((1, -1), far[::-1] if flip else far):
            for dist in range(1, most + 1):
                hops = hops_of[dist - 1]
                put((name, unit, step, dist), size, axis, hops, deps if dist == hops else [(name, unit, step, dist - hops)])

    def item(name, rel, flip):
        rel %= 8
        back = 4 if flip else 3
        if rel == 0:
            return []
        return [(name, 0, -1, rel)] if rel <= back else [(name, 0, 1, 8 - rel)]

    def of(*names):
        return [key for key in messages if key[0] in names]

    whole = {
        1: {rel: (rel,) for rel in (0, 1, 7, 2, 6, 3, 5, 4)},
        2: {0: (1, -1), 1: (1, 2, 3), 3: (-1, -2, -3), 2: (2, 3, 4, 5, 6)},
        4: {0: (1, 2, 3, -1, -2, -3), 1: tuple(range(1, 8))},
    }
    direct("CQ", "q", LEN_C, (1, -1, 2, -2, 3, -3, 4))
    direct("XA", "x", LEN_A, (1, -1, 2))
    direct("XB", "x", LEN_B, (1, -1, 2))
    ring("CP", 0, "p", 8 * LEN_C, 8, of("CQ"), False, (1, 2, 1, 1))
    for unit, rels in whole[PAIR].items():
        deps = of("CQ") + [key for rel in rels for key in item("CP", rel, False)]
        ring("CX", unit, "x", PAIR * 8 * LEN_C, 4, deps, unit % 2 == 1)
    ring("AQ", 0, "q", 4 * LEN_A, 8, of("XA"), False, (1, 2, 1, 2))
    ring("BP", 0, "p", 4 * LEN_B, 8, of("XB"), True, (1, 2, 1, 2))
    for name, axis, first, source, flip, size in (("AP", "p", "XA", "AQ", False, LEN_A), ("BQ", "q", "XB", "BP", True, LEN_B)):
        for unit, rels in whole[GROUP].items():
            deps = of(first) + [key for rel in rels for key in item(source, rel, flip)]
            ring(name, unit, axis, 4 * GROUP * size, 8, deps, unit % 2 == 1)
    put(("SA", 0, 0, 0), 32 * LEN_A, "s", 1, of("XA", "AQ"))
    put(("SB", 0, 0, 0), 32 * LEN_B, "s", 1, of("XB", "BP"))
    put(("SC", 0, 0, 0), 64 * LEN_C, "s", 1, of("CQ", "CP"))
    for rel in range(1, 8):
        for name, source, size in (("SA", "AP", LEN_A), ("SB", "BQ", LEN_B)):
            keys = [key for key in of(source) if (-key[2] * key[3]) % 8 == rel]
            if rel == 4:
                for key in keys:
                    put((name,) + key, messages[key]["size"] // 256, "s", 1, [key])
            else:
                put((name, rel, 0, 0), 32 * size, "s", 1, keys)
    for key in of("CX"):
        put(("SC",) + key, PAIR * 8 * LEN_C, "s", 1, [key])
    return messages


def plan_order(messages):
    turned = {"x": "x", "p": "q", "q": "p", "s": "s"}
    counter = itertools.count()
    link, free, events = {}, [0.0, 0.0], []
    arrival = [{}, {}]
    waits = [{key: set(m["deps"]) for key, m in messages.items()} for _ in range(2)]
    after = {}
    for key, m in messages.items():
        for dep in m["deps"]:
            after.setdefault(dep, []).append(key)

    def start(core, key, now):
        m = messages[key]
        free[core] = now = max(now, free[core]) + 0.1
        lane = ("s", core) if m["axis"] == "s" else (turned[m["axis"]] if core else m["axis"], key[2])
        rate = 6e5 if m["axis"] == "s" else 8.5e4
        link[lane] = max(now, link.get(lane, 0.0)) + m["size"] * m["hops"] / rate
        heapq.heappush(events, (link[lane] + 3.0 + 0.5 * (m["hops"] - 1), next(counter), core, key))

    for core in range(2):
        for key, m in messages.items():
            if not m["deps"]:
                start(core, key, 0.0)
    while events:
        now, _, core, key = heapq.heappop(events)
        arrival[core][key] = now
        for later in after.get(key, []):
            waits[core][later].discard(key)
            if not waits[core][later]:
                start(core, later, now)
    here = [key for key, m in messages.items() if m["axis"] != "s"]
    return sorted(here, key=lambda key: arrival[0][key] + arrival[1][key])


MESSAGES = plan_messages()
ORDER = plan_order(MESSAGES)
RECV = {key: i for i, key in enumerate(ORDER)}
PHASES = ("XA", "XB", "CQ", "CP", "CX", "AQ", "BP", "AP", "BQ")


def wait_bytes(data, sem):
    pltpu.make_async_copy(data, data, sem).wait()


def main_kernel(
    hidden_ref, ids_hbm, input_grad_ref, table_ref, targets_hbm,
    part_a, part_b, part_c, targets_ref, expo, most, lse, loss_ref, turned,
    table_v, table_c, ids_ref, grad_v, emb_out, emb_in, emb_rows, emb_hot,
    lse_out, lse_in, pick_first, pick_out, pick_in, score,
    recv_sem, send_sem, core_sem, emb_sem, local_sem, round_send, round_recv,
):
    parts = (part_a, part_b, part_c)
    v, s = lax.axis_index("vocab"), lax.axis_index("seq")
    c = lax.rem(v, 2)
    y = lax.rem(lax.div(v, 2), 8)
    z = lax.rem(s, 8)
    x = 2 * lax.div(v, 16) + lax.div(s, 8)
    p = z + c * (y - z)
    q = y + c * (z - y)

    def device(x_at, p_at, q_at):
        z_at = p_at + c * (q_at - p_at)
        y_at = q_at + c * (p_at - q_at)
        return (lax.div(x_at, 2) * 16 + y_at * 2 + c, lax.rem(x_at, 2) * 8 + z_at)

    def turn(at, by, length):
        return lax.rem(at + (by + length), length) if by else at

    xh, xl_here = lax.div(x, 2), lax.rem(x, 2)
    side = 2 * x + c

    def z_peer(r):
        return (v, xl_here * 8 + lax.rem(z + r, 8))

    def y_peer(r):
        return (xh * 16 + lax.rem(y + r, 8) * 2 + c, s)

    def x_peer(r):
        other = lax.rem(side + r, 8)
        x_at = lax.div(other, 2)
        return (lax.div(x_at, 2) * 16 + y * 2 + lax.rem(other, 2), lax.rem(x_at, 2) * 8 + z)

    x_peers, y_peers, z_peers = ([peer(r) for r in range(1, 8)] for peer in (x_peer, y_peer, z_peer))
    z_places = [lax.rem(z + r, 8) for r in range(1, 8)]
    sibling = (v + 1 - 2 * c, s)
    a, b, cc = part_a.at[c], part_b.at[c], part_c.at[c]

    own = [
        pltpu.make_async_copy(hidden_ref.at[pl.ds(LEN_A + LEN_B, LEN_C)], cc.at[x, p, q], local_sem.at[0]),
        pltpu.make_async_copy(hidden_ref.at[pl.ds(0, LEN_A)], a.at[p, q, x], local_sem.at[1]),
        pltpu.make_async_copy(hidden_ref.at[pl.ds(LEN_A, LEN_B)], b.at[q, p, x], local_sem.at[2]),
    ]
    ids_copy = pltpu.make_async_copy(ids_hbm, ids_ref, local_sem.at[3])
    grad_copy = pltpu.make_async_copy(input_grad_ref, grad_v, local_sem.at[4])
    targets_copy = pltpu.make_async_copy(targets_hbm, targets_ref, local_sem.at[5])
    table_copy = pltpu.make_async_copy(table_ref, table_v, local_sem.at[6])
    for copy in own:
        copy.start()
    table_copy.start()

    partners = [device(turn(x, d, 4), p, q) for d in (1, -1, 2)]
    partners += [device(x, turn(p, d, 8), q) for d in (1, -1, 2, -2)]
    partners += [device(x, p, turn(q, d, 8)) for d in (1, -1, 2, -2, 3, -3, 4)]
    partners += [sibling]
    barrier = pltpu.get_barrier_semaphore()
    for partner in partners:
        pl.semaphore_signal(barrier, inc=1, device_id=partner, device_id_type=MESH)
    for copy in (ids_copy, grad_copy, targets_copy):
        copy.start()

    def split_columns(core, j):
        n0 = 256 * j
        low = (n0 + FEAT * (n0 // FEAT) + FEAT * core) // 128 * 128
        width = min(768, D - low)
        n = lax.broadcasted_iota(jnp.int32, (1, 256), 1) + n0
        chunk = sum((n >= FEAT * k).astype(jnp.int32) for k in range(n0 // FEAT + 1, (n0 + 255) // FEAT + 1))
        source = n + FEAT * (chunk + n0 // FEAT + core) - low
        pick = (lax.broadcasted_iota(jnp.int32, (width, 256), 0) == source).astype(F32).astype(BF16)
        columns = jnp.dot(table_v[:, low : low + width], pick, preferred_element_type=F32)
        table_c[core, :, n0 : n0 + 256] = columns.astype(BF16)

    splits = [(core, j) for core in range(2) for j in range(HALF // 256)]
    table_copy.wait()
    for core, j in splits[:8]:
        split_columns(core, j)
    for copy in own:
        copy.wait()
    pl.semaphore_wait(barrier, len(partners))

    def group(at, unit, size):
        return pl.ds(size * turn(lax.div(at, size), unit, 8 // size), size)

    def block(key, shift):
        name, unit = key[0], key[1]
        if isinstance(unit, str):
            return arrived(key[1:])
        if name == "XA":
            return a.at[p, q, turn(x, shift, 4)]
        if name == "XB":
            return b.at[q, p, turn(x, shift, 4)]
        if name == "CQ":
            return cc.at[x, p, turn(q, shift, 8)]
        if name == "CP":
            return cc.at[x, turn(p, shift, 8)]
        if name == "CX":
            return cc.at[turn(x, shift, 4), group(p, unit, PAIR)]
        if name == "AQ":
            return a.at[p, turn(q, shift, 8)]
        if name == "BP":
            return b.at[q, turn(p, shift, 8)]
        if name == "AP":
            return a.at[turn(p, shift, 8), group(q, unit, GROUP)]
        if name == "BQ":
            return b.at[turn(q, shift, 8), group(p, unit, GROUP)]
        if name == "SA":
            return a.at[turn(p, unit, 8)]
        if name == "SB":
            return b.at[turn(q, unit, 8)]
        return cc.at[x]

    def arrived(key):
        return block(key, -key[2] * key[3])

    def send(key):
        m = MESSAGES[key]
        if m["axis"] == "s":
            part = ("SA", "SB", "SC").index(key[0])
            data, target, sems = block(key, 0), sibling, (core_sem.at[0, part], core_sem.at[1, part])
        else:
            by = key[2] * m["hops"]
            data = block(key, -key[2] * (key[3] - m["hops"]))
            target = {
                "x": lambda: device(turn(x, by, 4), p, q),
                "p": lambda: device(x, turn(p, by, 8), q),
                "q": lambda: device(x, p, turn(q, by, 8)),
            }[m["axis"]]()
            sems = send_sem.at[PHASES.index(key[0])], recv_sem.at[RECV[key]]
        pltpu.make_async_remote_copy(
            src_ref=data, dst_ref=data, send_sem=sems[0], recv_sem=sems[1], device_id=target, device_id_type=MESH
        ).start()

    done, sent = set(), set()

    def send_ready():
        for key, m in MESSAGES.items():
            if key not in sent and all(dep in done for dep in m["deps"]):
                sent.add(key)
                send(key)

    def embed_rows():
        ids_copy.wait()
        grad_copy.wait()
        first = lax.broadcasted_iota(jnp.int32, (SEQ, TOK), 0) * ROWS + v * (SEQ * ROWS)
        local = ids_ref[...] - first
        inside = (local >= 0) & (local < ROWS)
        total = jnp.dot(inside.astype(F32).astype(BF16), grad_v[...], preferred_element_type=F32)
        local_id = jnp.max(jnp.where(inside, local, -1).astype(F32), axis=1, keepdims=True)
        tail = jnp.broadcast_to(local_id, (SEQ, 128))
        for j in range(SEQ):
            emb_out[j, :, 0:D] = total[j : j + 1, :]
            emb_out[j, :, D:EXTRA] = tail[j : j + 1, :]
        emb_in[s] = emb_out[s]

    def send_row(r):
        j = lax.rem(s + r, SEQ)
        pltpu.make_async_remote_copy(
            src_ref=emb_out.at[j], dst_ref=emb_in.at[s], send_sem=emb_sem.at[0], recv_sem=emb_sem.at[1],
            device_id=(v, j), device_id_type=MESH,
        ).start()

    def embed_arrived():
        wait_bytes(emb_in.at[pl.ds(0, SEQ - 1)], emb_sem.at[1])
        lane_ids = lax.broadcasted_iota(jnp.int32, (1, 256), 1).astype(F32)
        for j in range(SEQ):
            emb_rows[j : j + 1, :] = emb_in[j, :, 0:D]
            emb_hot[j : j + 1, :] = (lane_ids == emb_in[j, :, D : D + 1]).astype(F32)

    needed = {key for key in MESSAGES if key[0] in ("XA", "XB", "AQ", "BP")}
    middle = max(36, 1 + max(ORDER.index(key) for key in needed))
    others = [functools.partial(split_columns, *split) for split in splits[8:]]
    others += [embed_rows] + [functools.partial(send_row, r) for r in range(1, SEQ)]
    send_ready()
    for i, key in enumerate(ORDER):
        wait_bytes(arrived(key), recv_sem.at[RECV[key]])
        done.add(key)
        send_ready()
        if i >= middle and others:
            others.pop(0)()
    assert not others

    targets_copy.wait()
    def blocks_of(n):
        return lax.div(n, 4), [2 * lax.rem(n, 4) + k for k in range(2)]

    def logits_step(n, core):
        xl, blocks = blocks_of(n)
        columns = [
            jnp.concatenate([core_features(parts, core, half, xl, z_at, slice(None)).reshape(HALF // 2, TOK) for half in range(2)], axis=0)
            for z_at in blocks
        ]
        values = jnp.dot(table_c[core], jnp.concatenate(columns, axis=1), preferred_element_type=F32)
        return xl, [(z_at, values[:, k * TOK : (k + 1) * TOK]) for k, z_at in enumerate(blocks)]

    def statistics_step(n):
        xl, blocks = blocks_of(n)
        for z_at in blocks:
            values = expo[xl, z_at]
            top = jnp.max(values, axis=0, keepdims=True)
            above = jnp.exp(values - top)
            most[xl, pl.ds(z_at, 1), :] = top
            lse_out[xl, 0, pl.ds(z_at, 1), :] = top + jnp.log(jnp.sum(above, axis=0, keepdims=True))
            hit = hit_of(targets_ref, xl, z_at)
            pick_first[z_at, pl.ds(xl, 1), :] = jnp.sum(jnp.where(hit, values, 0.0), axis=0, keepdims=True)
            expo[xl, z_at] = above

    def round_refs(stream, step):
        if stream < 2:
            return lse_out.at[stream, step], lse_in.at[stream, step]
        return pick_out.at[max(step, 1)], pick_in.at[step]

    def send_round(stream, step):
        data, into = round_refs(stream, step)
        axis = step if stream < 2 else 2 - step
        here = (side, y, z)[axis]
        for r, peer in enumerate((x_peers, y_peers, z_peers)[axis]):
            scatter = stream == 2 and step == 0
            pltpu.make_async_remote_copy(
                src_ref=pick_first.at[z_places[r]] if scatter else data, dst_ref=into.at[here],
                send_sem=round_send.at[stream, step], recv_sem=round_recv.at[stream, step],
                device_id=peer, device_id_type=MESH,
            ).start()
        into[here] = pick_first[z] if stream == 2 and step == 0 else data[...]

    def merged(stream, step):
        _, into = round_refs(stream, step)
        wait_bytes(into.at[0:7], round_recv.at[stream, step])
        values = into[...]
        if stream == 2:
            return jnp.sum(values, axis=0)
        top = jnp.max(values, axis=0)
        return top + jnp.log(jnp.sum(jnp.exp(values - top), axis=0))

    def first_pass(core):
        def step(n, carry):
            xl, values = logits_step(n, core)
            for z_at, value in values:
                expo[xl, z_at] = value
            return carry

        lax.fori_loop(0, 8, step, 0)

    def second_pass(core):
        def add(n):
            xl, values = logits_step(n, core)
            for z_at, value in values:
                expo[xl, z_at] += value

        def step(n, carry):
            statistics_step(n - 1)
            add(n)
            return carry

        add(jnp.int32(0))
        lax.fori_loop(1, 5, step, 0)
        send_round(0, 0)
        lax.fori_loop(5, 8, step, 0)

    for core in range(2):
        pl.when(c == core)(functools.partial(first_pass, core))
    for i, data in enumerate((part_a, part_b, part_c)):
        wait_bytes(data.at[1 - c], core_sem.at[1, i])
    for core in range(2):
        pl.when(c == 1 - core)(functools.partial(second_pass, core))
    statistics_step(jnp.int32(7))
    send_round(1, 0)
    send_round(2, 0)
    for step in range(2):
        for stream in range(3):
            data, _ = round_refs(stream, step + 1)
            data[...] = merged(stream, step)
            send_round(stream, step + 1)
    embed_arrived()

    hot = emb_hot[...].astype(BF16)
    hot = jnp.concatenate([hot, hot, hot], axis=0)
    lse[0] = merged(0, 2)
    fill_score(0, expo, most, lse, targets_ref, score)

    for i in range(4):
        rest = emb_rows[:, i * (D // 4) : (i + 1) * (D // 4)]
        high = rest.astype(BF16)
        rest = rest - high.astype(F32)
        middle = rest.astype(BF16)
        low = (rest - middle.astype(F32)).astype(BF16)
        terms = jnp.concatenate([high, middle, low], axis=0)
        embed = lax.dot_general(terms, hot, (((0,), (0,)), ((), ())), preferred_element_type=F32)
        turned[i] = head_block(parts, 0, i, score) + embed
    lse[1] = merged(1, 2)
    pick_out[0] = merged(2, 2)
    loss_ref[...] = lse[xl_here, pl.ds(z, 1), :] - pick_out[0, pl.ds(xl_here, 1), :]
    for stream in range(3):
        for step in range(3):
            wait_bytes(round_refs(stream, step)[1].at[0:7], round_send.at[stream, step])
    wait_bytes(a.at[p, q, 0:3], send_sem.at[0])
    wait_bytes(b.at[q, p, 0:3], send_sem.at[1])
    wait_bytes(cc.at[x, p, 0:7], send_sem.at[2])
    wait_bytes(cc.at[x, 0:7], send_sem.at[3])
    wait_bytes(cc.at[0:3], send_sem.at[4])
    wait_bytes(a.at[p, 0:7], send_sem.at[5])
    wait_bytes(b.at[q, 0:7], send_sem.at[6])
    wait_bytes(a.at[0:7], send_sem.at[7])
    wait_bytes(b.at[0:7], send_sem.at[8])
    wait_bytes(emb_out.at[pl.ds(0, SEQ - 1)], emb_sem.at[0])
    for i, data in enumerate((part_a, part_b, part_c)):
        wait_bytes(data.at[c], core_sem.at[0, i])


def hit_of(targets_ref, xl, z_at):
    row_start = (lax.axis_index("vocab") * SEQ + lax.axis_index("seq")) * ROWS
    row_ids = lax.broadcasted_iota(jnp.int32, (ROWS, TOK), 0)
    return (targets_ref[pl.ds(8 * xl + z_at, 1), :] - row_start) == row_ids


def core_features(parts, core, xh, xl, z_at, ys):
    part_a, part_b, part_c = parts
    x = 2 * xh + xl
    if core == 0:
        return jnp.concatenate([part_a[0, z_at, ys, x], part_b[0, ys, z_at, x], part_c[0, x, z_at, ys]], axis=1)
    return jnp.concatenate([part_a[1, ys, z_at, x], part_b[1, z_at, ys, x], part_c[1, x, ys, z_at]], axis=1)


def features_of(parts, xh, xl, z_at, ys):
    both = jnp.stack([core_features(parts, core, xh, xl, z_at, ys) for core in range(2)], axis=1)
    return both.reshape(both.shape[0] * 2 * FEAT, TOK)


def fill_score(xl, expo, most, lse, targets_ref, score):
    factor = jnp.exp(most[xl] - lse[xl])
    for z_at in range(8):
        value = expo[xl, z_at] * factor[z_at : z_at + 1, :] - hit_of(targets_ref, xl, z_at).astype(F32)
        score[0:ROWS, z_at * TOK : (z_at + 1) * TOK] = value.astype(BF16)


def head_block(parts, xl, i, score):
    xh, ys = i // 2, slice(4 * (i % 2), 4 * (i % 2) + 4)
    features = jnp.concatenate([features_of(parts, xh, xl, z_at, ys) for z_at in range(8)], axis=1)
    return lax.dot_general(features, score[...], (((1,), (1,)), ((), ())), preferred_element_type=F32)


def head_kernel(
    part_a, part_b, part_c, expo, most, lse, targets_ref, turned, loss_in,
    loss_ref, out_ref,
    score, out_v, out_sem,
):
    parts = (part_a, part_b, part_c)
    loss_ref[...] = loss_in[...]
    fill_score(1, expo, most, lse, targets_ref, score)

    ready = None
    for i in range(5):
        total = (turned[i] + head_block(parts, 1, i, score)).astype(BF16) if i < 4 else None
        if ready is not None:
            at = pl.ds((i - 1) * (D // 4), D // 4)
            out_v[:, at] = jnp.transpose(ready)[0:ROWS, :]
            pltpu.make_async_copy(out_v.at[:, at], out_ref.at[:, at], out_sem).start()
        ready = total
    pltpu.make_async_copy(out_v, out_ref, out_sem).wait()


def on_device(hidden, table, targets, token_ids, input_grad):
    any_space = pl.BlockSpec(memory_space=pl.ANY)
    vmem = pl.BlockSpec(memory_space=pltpu.VMEM)
    dma = pltpu.SemaphoreType.DMA
    tiles = pltpu.VMEM((2, 8, TOK), F32)
    targets = targets.reshape(SEQ, TOK)
    *parts, targets, expo, most, lse, loss, turned = pl.pallas_call(
        main_kernel,
        out_shape=(
            pltpu.VMEM((2, 8, 8, 4, LEN_A, TOK), BF16),
            pltpu.VMEM((2, 8, 8, 4, LEN_B, TOK), BF16),
            pltpu.VMEM((2, 4, 8, 8, LEN_C, TOK), BF16),
            pltpu.VMEM((SEQ, TOK), jnp.int32),
            pltpu.VMEM((2, 8, ROWS, TOK), F32),
            tiles,
            tiles,
            pltpu.VMEM((1, TOK), F32),
            pltpu.VMEM((4, D // 4, 256), F32),
        ),
        in_specs=[any_space] * 5,
        out_specs=(vmem,) * 9,
        scratch_shapes=[
            pltpu.VMEM((ROWS, D), BF16),
            pltpu.VMEM((2, ROWS, HALF), BF16),
            pltpu.VMEM((1, TOK), jnp.int32),
            pltpu.VMEM((TOK, D), BF16),
            pltpu.VMEM((SEQ, 1, EXTRA), F32),
            pltpu.VMEM((SEQ, 1, EXTRA), F32),
            pltpu.VMEM((SEQ, D), F32),
            pltpu.VMEM((SEQ, 256), F32),
            pltpu.VMEM((2, 3, 8, TOK), F32),
            pltpu.VMEM((2, 3, 8, 8, TOK), F32),
            pltpu.VMEM((8, 8, TOK), F32),
            pltpu.VMEM((3, 8, TOK), F32),
            pltpu.VMEM((3, 8, 8, TOK), F32),
            pltpu.VMEM((256, 8 * TOK), BF16),
            dma((len(ORDER),)),
            dma((len(PHASES),)),
            dma((2, 3)),
            dma((2,)),
            dma((7,)),
            dma((3, 3)),
            dma((3, 3)),
        ],
        compiler_params=pltpu.CompilerParams(collective_id=0, has_side_effects=True, vmem_limit_bytes=41 * 2**20),
        cost_estimate=pl.CostEstimate(flops=3 * 2048 * ROWS * D, bytes_accessed=2**22, transcendentals=2048 * ROWS),
        name="main",
    )(hidden.T, token_ids.reshape(1, TOK), input_grad, table, targets)
    loss, table_grad = pl.pallas_call(
        head_kernel,
        out_shape=(jax.ShapeDtypeStruct((1, TOK), F32), jax.ShapeDtypeStruct((ROWS, D), BF16)),
        in_specs=[vmem] * 9,
        out_specs=(vmem, any_space),
        scratch_shapes=[pltpu.VMEM((256, 8 * TOK), BF16), pltpu.VMEM((ROWS, D), BF16), dma],
        compiler_params=pltpu.CompilerParams(vmem_limit_bytes=14 * 2**20),
        cost_estimate=pl.CostEstimate(flops=2 * 2048 * ROWS * D, bytes_accessed=2**21, transcendentals=2048 * ROWS),
        name="head",
    )(*parts, expo, most, lse, targets, turned, loss)
    return loss.reshape(TOK), table_grad


def solution(mesh):
    in_specs = (P("seq", "vocab"), P(("vocab", "seq"), None), P(), P("seq"), P("seq", None))
    out_specs = (P("seq"), P(("vocab", "seq"), None))
    return jax.shard_map(
        on_device, mesh=mesh, in_specs=in_specs, out_specs=out_specs, check_vma=False
    )
```

```python
import functools
import heapq
import itertools

import jax
import jax.numpy as jnp
from jax import lax
from jax.experimental import pallas as pl
from jax.experimental.pallas import tpu as pltpu
from jax.sharding import PartitionSpec as P

MESH = pl.DeviceIdType.MESH
F32 = jnp.float32
BF16 = jnp.bfloat16

D = 3584
TOK = 128
FEAT = 112
ROWS = 250
SEQ = 16
HALF = D // 2
EXTRA = D + 128
LEN_A, LEN_B, LEN_C = 32, 32, 48
GROUP = 4
PAIR = 1


def plan_messages():
    messages = {}

    def put(key, size, axis, hops, deps):
        messages[key] = dict(size=size * 256, axis=axis, hops=hops, deps=list(deps))

    def direct(name, axis, size, rels):
        for rel in rels:
            put((name, 0, 1 if rel > 0 else -1, abs(rel)), size, axis, abs(rel), [])

    def ring(name, unit, axis, size, length, deps, flip, hops_of=(1, 1, 1, 1)):
        far = (length // 2, length // 2 - 1)
        for step, most in zip((1, -1), far[::-1] if flip else far):
            for dist in sorted(range(1, most + 1), key=lambda at: -hops_of[at - 1]):
                hops = hops_of[dist - 1]
                put((name, unit, step, dist), size, axis, hops, deps if dist == hops else [(name, unit, step, dist - hops)])

    def item(name, rel, flip):
        rel %= 8
        back = 4 if flip else 3
        if rel == 0:
            return []
        return [(name, 0, -1, rel)] if rel <= back else [(name, 0, 1, 8 - rel)]

    def of(*names):
        return [key for key in messages if key[0] in names]

    whole = {
        1: {rel: (rel,) for rel in (0, 1, 7, 2, 6, 3, 5, 4)},
        2: {0: (1, -1), 1: (1, 2, 3), 3: (-1, -2, -3), 2: (2, 3, 4, 5, 6)},
        4: {0: (1, 2, 3, -1, -2, -3), 1: tuple(range(1, 8))},
    }
    direct("CQ", "q", LEN_C, (4, 3, -3, 2, -2, 1, -1))
    direct("XA", "x", LEN_A, (2, 1, -1))
    direct("XB", "x", LEN_B, (2, 1, -1))
    ring("CP", 0, "p", 8 * LEN_C, 8, of("CQ"), False)
    for unit, rels in whole[PAIR].items():
        deps = of("CQ") + [key for rel in rels for key in item("CP", rel, False)]
        ring("CX", unit, "x", PAIR * 8 * LEN_C, 4, deps, unit % 2 == 1)
    ring("AQ", 0, "q", 4 * LEN_A, 8, of("XA"), False, (1, 2, 1, 2))
    ring("BP", 0, "p", 4 * LEN_B, 8, of("XB"), True, (1, 2, 1, 2))
    for name, axis, first, source, flip, size in (("AP", "p", "XA", "AQ", False, LEN_A), ("BQ", "q", "XB", "BP", True, LEN_B)):
        for unit, rels in whole[GROUP].items():
            deps = of(first) + [key for rel in rels for key in item(source, rel, flip)]
            ring(name, unit, axis, 4 * GROUP * size, 8, deps, unit % 2 == 1)
    put(("SA", 0, 0, 0), 32 * LEN_A, "s", 1, of("XA", "AQ"))
    put(("SB", 0, 0, 0), 32 * LEN_B, "s", 1, of("XB", "BP"))
    put(("SC", 0, 0, 0), 64 * LEN_C, "s", 1, of("CQ", "CP"))
    for rel in range(1, 8):
        for name, source, size in (("SA", "AP", LEN_A), ("SB", "BQ", LEN_B)):
            keys = [key for key in of(source) if (-key[2] * key[3]) % 8 == rel]
            if rel == 4:
                for key in keys:
                    put((name,) + key, messages[key]["size"] // 256, "s", 1, [key])
            else:
                put((name, rel, 0, 0), 32 * size, "s", 1, keys)
    for key in of("CX"):
        put(("SC",) + key, PAIR * 8 * LEN_C, "s", 1, [key])
    return messages


def plan_order(messages):
    turned = {"x": "x", "p": "q", "q": "p", "s": "s"}
    counter = itertools.count()
    link, free, events = {}, [0.0, 0.0], []
    arrival = [{}, {}]
    waits = [{key: set(m["deps"]) for key, m in messages.items()} for _ in range(2)]
    after = {}
    for key, m in messages.items():
        for dep in m["deps"]:
            after.setdefault(dep, []).append(key)

    def start(core, key, now):
        m = messages[key]
        free[core] = now = max(now, free[core]) + 0.05
        lane = ("s", core) if m["axis"] == "s" else (turned[m["axis"]] if core else m["axis"], key[2])
        rate = 6e5 if m["axis"] == "s" else 8.5e4
        link[lane] = max(now, link.get(lane, 0.0)) + m["size"] * m["hops"] / rate
        heapq.heappush(events, (link[lane] + 3.0 + 0.5 * (m["hops"] - 1), next(counter), core, key))

    for core in range(2):
        for key, m in messages.items():
            if not m["deps"]:
                start(core, key, 0.0)
    while events:
        now, _, core, key = heapq.heappop(events)
        arrival[core][key] = now
        for later in after.get(key, []):
            waits[core][later].discard(key)
            if not waits[core][later]:
                start(core, later, now)
    here = [key for key, m in messages.items() if m["axis"] != "s"]
    return sorted(here, key=lambda key: arrival[0][key] + arrival[1][key])


MESSAGES = plan_messages()
ORDER = plan_order(MESSAGES)
RECV = {key: i for i, key in enumerate(ORDER)}
PHASES = ("XA", "XB", "CQ", "CP", "CX", "AQ", "BP", "AP", "BQ")


def wait_bytes(data, sem):
    pltpu.make_async_copy(data, data, sem).wait()


def main_kernel(
    hidden_ref, ids_hbm, input_grad_ref, table_ref, targets_hbm,
    part_a, part_b, part_c, targets_ref, expo, most, lse, loss_ref, turned,
    table_v, table_c, ids_ref, grad_v, emb_out, emb_in, emb_rows, emb_hot,
    lse_out, lse_in, pick_first, pick_out, pick_in, score,
    recv_sem, send_sem, core_sem, emb_sem, local_sem, round_send, round_recv,
):
    parts = (part_a, part_b, part_c)
    v, s = lax.axis_index("vocab"), lax.axis_index("seq")
    c = lax.rem(v, 2)
    y = lax.rem(lax.div(v, 2), 8)
    z = lax.rem(s, 8)
    x = 2 * lax.div(v, 16) + lax.div(s, 8)
    p = z + c * (y - z)
    q = y + c * (z - y)

    def device(x_at, p_at, q_at):
        z_at = p_at + c * (q_at - p_at)
        y_at = q_at + c * (p_at - q_at)
        return (lax.div(x_at, 2) * 16 + y_at * 2 + c, lax.rem(x_at, 2) * 8 + z_at)

    def turn(at, by, length):
        return lax.rem(at + (by + length), length) if by else at

    xh, xl_here = lax.div(x, 2), lax.rem(x, 2)
    side = 2 * x + c

    def z_peer(r):
        return (v, xl_here * 8 + lax.rem(z + r, 8))

    def y_peer(r):
        return (xh * 16 + lax.rem(y + r, 8) * 2 + c, s)

    def x_peer(r):
        other = lax.rem(side + r, 8)
        x_at = lax.div(other, 2)
        return (lax.div(x_at, 2) * 16 + y * 2 + lax.rem(other, 2), lax.rem(x_at, 2) * 8 + z)

    far_first = (4, 3, 5, 2, 6, 1, 7)
    x_peers, y_peers, z_peers = ([peer(r) for r in far_first] for peer in (x_peer, y_peer, z_peer))
    z_places = [lax.rem(z + r, 8) for r in far_first]
    sibling = (v + 1 - 2 * c, s)
    a, b, cc = part_a.at[c], part_b.at[c], part_c.at[c]

    own = [
        pltpu.make_async_copy(hidden_ref.at[pl.ds(LEN_A + LEN_B, LEN_C)], cc.at[x, p, q], local_sem.at[0]),
        pltpu.make_async_copy(hidden_ref.at[pl.ds(0, LEN_A)], a.at[p, q, x], local_sem.at[1]),
        pltpu.make_async_copy(hidden_ref.at[pl.ds(LEN_A, LEN_B)], b.at[q, p, x], local_sem.at[2]),
    ]
    ids_copy = pltpu.make_async_copy(ids_hbm, ids_ref, local_sem.at[3])
    grad_copy = pltpu.make_async_copy(input_grad_ref, grad_v, local_sem.at[4])
    targets_copy = pltpu.make_async_copy(targets_hbm, targets_ref, local_sem.at[5])
    table_copy = pltpu.make_async_copy(table_ref, table_v, local_sem.at[6])
    partners = [device(x, p, turn(q, d, 8)) for d in (4, 3, -3, 2, -2, 1, -1)]
    partners += [device(x, turn(p, d, 8), q) for d in (2, -2, 1, -1)]
    partners += [device(turn(x, d, 4), p, q) for d in (2, 1, -1)]
    partners += [sibling]
    barrier = pltpu.get_barrier_semaphore()
    for partner in partners:
        pl.semaphore_signal(barrier, inc=1, device_id=partner, device_id_type=MESH)
    for copy in own + [table_copy, ids_copy, grad_copy, targets_copy]:
        copy.start()

    def split_columns(core, j):
        n0 = 256 * j
        low = (n0 + FEAT * (n0 // FEAT) + FEAT * core) // 128 * 128
        width = min(768, D - low)
        n = lax.broadcasted_iota(jnp.int32, (1, 256), 1) + n0
        chunk = sum((n >= FEAT * k).astype(jnp.int32) for k in range(n0 // FEAT + 1, (n0 + 255) // FEAT + 1))
        source = n + FEAT * (chunk + n0 // FEAT + core) - low
        pick = (lax.broadcasted_iota(jnp.int32, (width, 256), 0) == source).astype(F32).astype(BF16)
        columns = jnp.dot(table_v[:, low : low + width], pick, preferred_element_type=F32)
        table_c[core, :, n0 : n0 + 256] = columns.astype(BF16)

    splits = [(core, j) for core in range(2) for j in range(HALF // 256)]
    table_copy.wait()
    for core, j in splits[:8]:
        split_columns(core, j)
    for copy in own:
        copy.wait()
    pl.semaphore_wait(barrier, len(partners))

    def group(at, unit, size):
        return pl.ds(size * turn(lax.div(at, size), unit, 8 // size), size)

    def block(key, shift):
        name, unit = key[0], key[1]
        if isinstance(unit, str):
            return arrived(key[1:])
        if name == "XA":
            return a.at[p, q, turn(x, shift, 4)]
        if name == "XB":
            return b.at[q, p, turn(x, shift, 4)]
        if name == "CQ":
            return cc.at[x, p, turn(q, shift, 8)]
        if name == "CP":
            return cc.at[x, turn(p, shift, 8)]
        if name == "CX":
            return cc.at[turn(x, shift, 4), group(p, unit, PAIR)]
        if name == "AQ":
            return a.at[p, turn(q, shift, 8)]
        if name == "BP":
            return b.at[q, turn(p, shift, 8)]
        if name == "AP":
            return a.at[turn(p, shift, 8), group(q, unit, GROUP)]
        if name == "BQ":
            return b.at[turn(q, shift, 8), group(p, unit, GROUP)]
        if name == "SA":
            return a.at[turn(p, unit, 8)]
        if name == "SB":
            return b.at[turn(q, unit, 8)]
        return cc.at[x]

    def arrived(key):
        return block(key, -key[2] * key[3])

    def send(key):
        m = MESSAGES[key]
        if m["axis"] == "s":
            part = ("SA", "SB", "SC").index(key[0])
            data, target, sems = block(key, 0), sibling, (core_sem.at[0, part], core_sem.at[1, part])
        else:
            by = key[2] * m["hops"]
            data = block(key, -key[2] * (key[3] - m["hops"]))
            target = {
                "x": lambda: device(turn(x, by, 4), p, q),
                "p": lambda: device(x, turn(p, by, 8), q),
                "q": lambda: device(x, p, turn(q, by, 8)),
            }[m["axis"]]()
            sems = send_sem.at[PHASES.index(key[0])], recv_sem.at[RECV[key]]
        pltpu.make_async_remote_copy(
            src_ref=data, dst_ref=data, send_sem=sems[0], recv_sem=sems[1], device_id=target, device_id_type=MESH
        ).start()

    done, sent = set(), set()

    def send_ready():
        for key, m in MESSAGES.items():
            if key not in sent and all(dep in done for dep in m["deps"]):
                sent.add(key)
                send(key)

    def embed_rows():
        ids_copy.wait()
        grad_copy.wait()
        first = lax.broadcasted_iota(jnp.int32, (SEQ, TOK), 0) * ROWS + v * (SEQ * ROWS)
        local = ids_ref[...] - first
        inside = (local >= 0) & (local < ROWS)
        total = jnp.dot(inside.astype(F32).astype(BF16), grad_v[...], preferred_element_type=F32)
        local_id = jnp.max(jnp.where(inside, local, -1).astype(F32), axis=1, keepdims=True)
        tail = jnp.broadcast_to(local_id, (SEQ, 128))
        for j in range(SEQ):
            emb_out[j, :, 0:D] = total[j : j + 1, :]
            emb_out[j, :, D:EXTRA] = tail[j : j + 1, :]
        emb_in[s] = emb_out[s]

    def send_row(r):
        j = lax.rem(s + r, SEQ)
        pltpu.make_async_remote_copy(
            src_ref=emb_out.at[j], dst_ref=emb_in.at[s], send_sem=emb_sem.at[0], recv_sem=emb_sem.at[1],
            device_id=(v, j), device_id_type=MESH,
        ).start()

    def embed_arrived():
        wait_bytes(emb_in.at[pl.ds(0, SEQ - 1)], emb_sem.at[1])
        lane_ids = lax.broadcasted_iota(jnp.int32, (1, 256), 1).astype(F32)
        for j in range(SEQ):
            emb_rows[j : j + 1, :] = emb_in[j, :, 0:D]
            emb_hot[j : j + 1, :] = (lane_ids == emb_in[j, :, D : D + 1]).astype(F32)

    needed = {key for key in MESSAGES if key[0] in ("XA", "XB", "AQ", "BP")}
    middle = max(36, 1 + max(ORDER.index(key) for key in needed))
    others = [functools.partial(split_columns, *split) for split in splits[8:]]
    others += [embed_rows] + [functools.partial(send_row, r) for r in range(1, SEQ)]
    send_ready()
    for i, key in enumerate(ORDER):
        wait_bytes(arrived(key), recv_sem.at[RECV[key]])
        done.add(key)
        send_ready()
        if i >= middle and others:
            others.pop(0)()
    assert not others

    targets_copy.wait()
    def blocks_of(n):
        return lax.div(n, 4), [2 * lax.rem(n, 4) + k for k in range(2)]

    def logits_step(n, core):
        xl, blocks = blocks_of(n)
        columns = [
            jnp.concatenate([core_features(parts, core, half, xl, z_at, slice(None)).reshape(HALF // 2, TOK) for half in range(2)], axis=0)
            for z_at in blocks
        ]
        values = jnp.dot(table_c[core], jnp.concatenate(columns, axis=1), preferred_element_type=F32)
        return xl, [(z_at, values[:, k * TOK : (k + 1) * TOK]) for k, z_at in enumerate(blocks)]

    def statistics_step(n):
        xl, blocks = blocks_of(n)
        for z_at in blocks:
            values = expo[xl, z_at]
            top = jnp.max(values, axis=0, keepdims=True)
            above = jnp.exp(values - top)
            most[xl, pl.ds(z_at, 1), :] = top
            lse_out[xl, 0, pl.ds(z_at, 1), :] = top + jnp.log(jnp.sum(above, axis=0, keepdims=True))
            hit = hit_of(targets_ref, xl, z_at)
            pick_first[z_at, pl.ds(xl, 1), :] = jnp.sum(jnp.where(hit, values, 0.0), axis=0, keepdims=True)
            expo[xl, z_at] = above

    def round_refs(stream, step):
        if stream < 2:
            return lse_out.at[stream, step], lse_in.at[stream, step]
        return pick_out.at[max(step, 1)], pick_in.at[step]

    def send_round(stream, step):
        data, into = round_refs(stream, step)
        axis = step if stream < 2 else 2 - step
        here = (side, y, z)[axis]
        for r, peer in enumerate((x_peers, y_peers, z_peers)[axis]):
            scatter = stream == 2 and step == 0
            pltpu.make_async_remote_copy(
                src_ref=pick_first.at[z_places[r]] if scatter else data, dst_ref=into.at[here],
                send_sem=round_send.at[stream, step], recv_sem=round_recv.at[stream, step],
                device_id=peer, device_id_type=MESH,
            ).start()
        into[here] = pick_first[z] if stream == 2 and step == 0 else data[...]

    def merged(stream, step):
        _, into = round_refs(stream, step)
        wait_bytes(into.at[0:7], round_recv.at[stream, step])
        values = into[...]
        if stream == 2:
            return jnp.sum(values, axis=0)
        top = jnp.max(values, axis=0)
        return top + jnp.log(jnp.sum(jnp.exp(values - top), axis=0))

    def first_pass(core):
        def step(n, carry):
            xl, values = logits_step(n, core)
            for z_at, value in values:
                expo[xl, z_at] = value
            return carry

        lax.fori_loop(0, 8, step, 0)

    def second_pass(core):
        def add(n):
            xl, values = logits_step(n, core)
            for z_at, value in values:
                expo[xl, z_at] += value

        def step(n, carry):
            statistics_step(n - 1)
            add(n)
            return carry

        add(jnp.int32(0))
        lax.fori_loop(1, 5, step, 0)
        send_round(0, 0)
        lax.fori_loop(5, 8, step, 0)

    for core in range(2):
        pl.when(c == core)(functools.partial(first_pass, core))
    for i, data in enumerate((part_a, part_b, part_c)):
        wait_bytes(data.at[1 - c], core_sem.at[1, i])
    for core in range(2):
        pl.when(c == 1 - core)(functools.partial(second_pass, core))
    statistics_step(jnp.int32(7))
    send_round(1, 0)
    send_round(2, 0)

    def next_round(stream, step):
        data, _ = round_refs(stream, step + 1)
        data[...] = merged(stream, step)
        send_round(stream, step + 1)

    for stream, step in ((0, 0), (1, 0), (2, 0), (0, 1), (1, 1)):
        next_round(stream, step)

    embed_arrived()
    hot = emb_hot[...].astype(BF16)
    hot = jnp.concatenate([hot, hot, hot], axis=0)
    for i in range(4):
        rest = emb_rows[:, i * (D // 4) : (i + 1) * (D // 4)]
        high = rest.astype(BF16)
        rest = rest - high.astype(F32)
        middle = rest.astype(BF16)
        low = (rest - middle.astype(F32)).astype(BF16)
        terms = jnp.concatenate([high, middle, low], axis=0)
        turned[i] = lax.dot_general(terms, hot, (((0,), (0,)), ((), ())), preferred_element_type=F32)

    next_round(2, 1)
    lse[0] = merged(0, 2)
    fill_score(0, expo, most, lse, targets_ref, score)
    for i in range(4):
        turned[i] += head_block(parts, 0, i, score)
    lse[1] = merged(1, 2)
    pick_out[0] = merged(2, 2)
    loss_ref[...] = lse[xl_here, pl.ds(z, 1), :] - pick_out[0, pl.ds(xl_here, 1), :]
    for stream in range(3):
        for step in range(3):
            wait_bytes(round_refs(stream, step)[1].at[0:7], round_send.at[stream, step])
    wait_bytes(a.at[p, q, 0:3], send_sem.at[0])
    wait_bytes(b.at[q, p, 0:3], send_sem.at[1])
    wait_bytes(cc.at[x, p, 0:7], send_sem.at[2])
    wait_bytes(cc.at[x, 0:7], send_sem.at[3])
    wait_bytes(cc.at[0:3], send_sem.at[4])
    wait_bytes(a.at[p, 0:7], send_sem.at[5])
    wait_bytes(b.at[q, 0:7], send_sem.at[6])
    wait_bytes(a.at[0:7], send_sem.at[7])
    wait_bytes(b.at[0:7], send_sem.at[8])
    wait_bytes(emb_out.at[pl.ds(0, SEQ - 1)], emb_sem.at[0])
    for i, data in enumerate((part_a, part_b, part_c)):
        wait_bytes(data.at[c], core_sem.at[0, i])


def hit_of(targets_ref, xl, z_at):
    row_start = (lax.axis_index("vocab") * SEQ + lax.axis_index("seq")) * ROWS
    row_ids = lax.broadcasted_iota(jnp.int32, (ROWS, TOK), 0)
    return (targets_ref[pl.ds(8 * xl + z_at, 1), :] - row_start) == row_ids


def core_features(parts, core, xh, xl, z_at, ys):
    part_a, part_b, part_c = parts
    x = 2 * xh + xl
    if core == 0:
        return jnp.concatenate([part_a[0, z_at, ys, x], part_b[0, ys, z_at, x], part_c[0, x, z_at, ys]], axis=1)
    return jnp.concatenate([part_a[1, ys, z_at, x], part_b[1, z_at, ys, x], part_c[1, x, ys, z_at]], axis=1)


def features_of(parts, xh, xl, z_at, ys):
    both = jnp.stack([core_features(parts, core, xh, xl, z_at, ys) for core in range(2)], axis=1)
    return both.reshape(both.shape[0] * 2 * FEAT, TOK)


def fill_score(xl, expo, most, lse, targets_ref, score):
    factor = jnp.exp(most[xl] - lse[xl])
    for z_at in range(8):
        value = expo[xl, z_at] * factor[z_at : z_at + 1, :] - hit_of(targets_ref, xl, z_at).astype(F32)
        score[0:ROWS, z_at * TOK : (z_at + 1) * TOK] = value.astype(BF16)


def head_block(parts, xl, i, score):
    xh, ys = i // 2, slice(4 * (i % 2), 4 * (i % 2) + 4)
    features = jnp.concatenate([features_of(parts, xh, xl, z_at, ys) for z_at in range(8)], axis=1)
    return lax.dot_general(features, score[...], (((1,), (1,)), ((), ())), preferred_element_type=F32)


def head_kernel(
    part_a, part_b, part_c, expo, most, lse, targets_ref, turned, loss_in,
    loss_ref, out_ref,
    score, out_v, out_sem,
):
    parts = (part_a, part_b, part_c)
    loss_ref[...] = loss_in[...]
    fill_score(1, expo, most, lse, targets_ref, score)

    ready = None
    for i in range(5):
        total = (turned[i] + head_block(parts, 1, i, score)).astype(BF16) if i < 4 else None
        if ready is not None:
            at = pl.ds((i - 1) * (D // 4), D // 4)
            out_v[:, at] = jnp.transpose(ready)[0:ROWS, :]
            pltpu.make_async_copy(out_v.at[:, at], out_ref.at[:, at], out_sem).start()
        ready = total
    pltpu.make_async_copy(out_v, out_ref, out_sem).wait()


def on_device(hidden, table, targets, token_ids, input_grad):
    any_space = pl.BlockSpec(memory_space=pl.ANY)
    vmem = pl.BlockSpec(memory_space=pltpu.VMEM)
    dma = pltpu.SemaphoreType.DMA
    tiles = pltpu.VMEM((2, 8, TOK), F32)
    targets = targets.reshape(SEQ, TOK)
    *parts, targets, expo, most, lse, loss, turned = pl.pallas_call(
        main_kernel,
        out_shape=(
            pltpu.VMEM((2, 8, 8, 4, LEN_A, TOK), BF16),
            pltpu.VMEM((2, 8, 8, 4, LEN_B, TOK), BF16),
            pltpu.VMEM((2, 4, 8, 8, LEN_C, TOK), BF16),
            pltpu.VMEM((SEQ, TOK), jnp.int32),
            pltpu.VMEM((2, 8, ROWS, TOK), F32),
            tiles,
            tiles,
            pltpu.VMEM((1, TOK), F32),
            pltpu.VMEM((4, D // 4, 256), F32),
        ),
        in_specs=[any_space] * 5,
        out_specs=(vmem,) * 9,
        scratch_shapes=[
            pltpu.VMEM((ROWS, D), BF16),
            pltpu.VMEM((2, ROWS, HALF), BF16),
            pltpu.VMEM((1, TOK), jnp.int32),
            pltpu.VMEM((TOK, D), BF16),
            pltpu.VMEM((SEQ, 1, EXTRA), F32),
            pltpu.VMEM((SEQ, 1, EXTRA), F32),
            pltpu.VMEM((SEQ, D), F32),
            pltpu.VMEM((SEQ, 256), F32),
            pltpu.VMEM((2, 3, 8, TOK), F32),
            pltpu.VMEM((2, 3, 8, 8, TOK), F32),
            pltpu.VMEM((8, 8, TOK), F32),
            pltpu.VMEM((3, 8, TOK), F32),
            pltpu.VMEM((3, 8, 8, TOK), F32),
            pltpu.VMEM((256, 8 * TOK), BF16),
            dma((len(ORDER),)),
            dma((len(PHASES),)),
            dma((2, 3)),
            dma((2,)),
            dma((7,)),
            dma((3, 3)),
            dma((3, 3)),
        ],
        compiler_params=pltpu.CompilerParams(collective_id=0, has_side_effects=True, vmem_limit_bytes=41 * 2**20),
        cost_estimate=pl.CostEstimate(flops=3 * 2048 * ROWS * D, bytes_accessed=2**22, transcendentals=2048 * ROWS),
        name="main",
    )(hidden.T, token_ids.reshape(1, TOK), input_grad, table, targets)
    loss, table_grad = pl.pallas_call(
        head_kernel,
        out_shape=(jax.ShapeDtypeStruct((1, TOK), F32), jax.ShapeDtypeStruct((ROWS, D), BF16)),
        in_specs=[vmem] * 9,
        out_specs=(vmem, any_space),
        scratch_shapes=[pltpu.VMEM((256, 8 * TOK), BF16), pltpu.VMEM((ROWS, D), BF16), dma],
        compiler_params=pltpu.CompilerParams(vmem_limit_bytes=14 * 2**20),
        cost_estimate=pl.CostEstimate(flops=2 * 2048 * ROWS * D, bytes_accessed=2**21, transcendentals=2048 * ROWS),
        name="head",
    )(*parts, expo, most, lse, targets, turned, loss)
    return loss.reshape(TOK), table_grad


def solution(mesh):
    in_specs = (P("seq", "vocab"), P(("vocab", "seq"), None), P(), P("seq"), P("seq", None))
    out_specs = (P("seq"), P(("vocab", "seq"), None))
    return jax.shard_map(
        on_device, mesh=mesh, in_specs=in_specs, out_specs=out_specs, check_vma=False
    )
```

```python
import functools
import heapq
import itertools

import jax
import jax.numpy as jnp
from jax import lax
from jax.experimental import pallas as pl
from jax.experimental.pallas import tpu as pltpu
from jax.sharding import PartitionSpec as P

MESH = pl.DeviceIdType.MESH
F32 = jnp.float32
BF16 = jnp.bfloat16

D = 3584
TOK = 128
FEAT = 112
ROWS = 250
SEQ = 16
HALF = D // 2
EXTRA = D + 128
LEN_A, LEN_B, LEN_C = 32, 32, 48
GROUP = 4
PAIR = 1


def plan_messages():
    messages = {}

    def put(key, size, axis, hops, deps):
        messages[key] = dict(size=size * 256, axis=axis, hops=hops, deps=list(deps))

    def direct(name, axis, size, rels):
        for rel in rels:
            put((name, 0, 1 if rel > 0 else -1, abs(rel)), size, axis, abs(rel), [])

    def ring(name, unit, axis, size, length, deps, flip, hops_of=(1, 1, 1, 1)):
        far = (length // 2, length // 2 - 1)
        for step, most in zip((1, -1), far[::-1] if flip else far):
            for dist in sorted(range(1, most + 1), key=lambda at: -hops_of[at - 1]):
                hops = hops_of[dist - 1]
                put((name, unit, step, dist), size, axis, hops, deps if dist == hops else [(name, unit, step, dist - hops)])

    def item(name, rel, flip):
        rel %= 8
        back = 4 if flip else 3
        if rel == 0:
            return []
        return [(name, 0, -1, rel)] if rel <= back else [(name, 0, 1, 8 - rel)]

    def of(*names):
        return [key for key in messages if key[0] in names]

    whole = {
        1: {rel: (rel,) for rel in (0, 1, 7, 2, 6, 3, 5, 4)},
        2: {0: (1, -1), 1: (1, 2, 3), 3: (-1, -2, -3), 2: (2, 3, 4, 5, 6)},
        4: {0: (1, 2, 3, -1, -2, -3), 1: tuple(range(1, 8))},
    }
    direct("CQ", "q", LEN_C, (4, 3, -3, 2, -2, 1, -1))
    direct("XA", "x", LEN_A, (2, 1, -1))
    direct("XB", "x", LEN_B, (2, 1, -1))
    ring("CP", 0, "p", 8 * LEN_C, 8, of("CQ"), False)
    for unit, rels in whole[PAIR].items():
        deps = of("CQ") + [key for rel in rels for key in item("CP", rel, False)]
        ring("CX", unit, "x", PAIR * 8 * LEN_C, 4, deps, unit % 2 == 1)
    ring("AQ", 0, "q", 4 * LEN_A, 8, of("XA"), False, (1, 2, 1, 2))
    ring("BP", 0, "p", 4 * LEN_B, 8, of("XB"), True, (1, 2, 1, 2))
    for name, axis, first, source, flip, size in (("AP", "p", "XA", "AQ", False, LEN_A), ("BQ", "q", "XB", "BP", True, LEN_B)):
        for unit, rels in whole[GROUP].items():
            deps = of(first) + [key for rel in rels for key in item(source, rel, flip)]
            ring(name, unit, axis, 4 * GROUP * size, 8, deps, unit % 2 == 1)
    put(("SA", 0, 0, 0), 32 * LEN_A, "s", 1, of("XA", "AQ"))
    put(("SB", 0, 0, 0), 32 * LEN_B, "s", 1, of("XB", "BP"))
    for rel in range(1, 8):
        for name, source, size in (("SA", "AP", LEN_A), ("SB", "BQ", LEN_B)):
            keys = [key for key in of(source) if (-key[2] * key[3]) % 8 == rel]
            if rel == 4:
                for key in keys:
                    put((name,) + key, messages[key]["size"] // 256, "s", 1, [key])
            else:
                put((name, rel, 0, 0), 32 * size, "s", 1, keys)
    for rel in range(8):
        keys = [key for key in of("CP") if (-key[2] * key[3]) % 8 == rel] + [key for key in of("CX") if key[1] == rel]
        if rel == 4:
            for key in keys:
                put(("SC",) + key, messages[key]["size"] // 256, "s", 1, [key])
        else:
            put(("SC", rel, 0, 0), 32 * LEN_C, "s", 1, of("CQ") + keys)
    return messages


def plan_order(messages):
    turned = {"x": "x", "p": "q", "q": "p", "s": "s"}
    counter = itertools.count()
    link, free, events = {}, [0.0, 0.0], []
    arrival = [{}, {}]
    waits = [{key: set(m["deps"]) for key, m in messages.items()} for _ in range(2)]
    after = {}
    for key, m in messages.items():
        for dep in m["deps"]:
            after.setdefault(dep, []).append(key)

    def start(core, key, now):
        m = messages[key]
        free[core] = now = max(now, free[core]) + 0.05
        lane = ("s", core) if m["axis"] == "s" else (turned[m["axis"]] if core else m["axis"], key[2])
        rate = 6e5 if m["axis"] == "s" else 8.5e4
        link[lane] = max(now, link.get(lane, 0.0)) + m["size"] * m["hops"] / rate
        heapq.heappush(events, (link[lane] + 3.0 + 0.5 * (m["hops"] - 1), next(counter), core, key))

    for core in range(2):
        for key, m in messages.items():
            if not m["deps"]:
                start(core, key, 0.0)
    while events:
        now, _, core, key = heapq.heappop(events)
        arrival[core][key] = now
        for later in after.get(key, []):
            waits[core][later].discard(key)
            if not waits[core][later]:
                start(core, later, now)
    here = [key for key, m in messages.items() if m["axis"] != "s"]
    return sorted(here, key=lambda key: arrival[0][key] + arrival[1][key])


MESSAGES = plan_messages()
ORDER = plan_order(MESSAGES)
RECV = {key: i for i, key in enumerate(ORDER)}
PHASES = ("XA", "XB", "CQ", "CP", "CX", "AQ", "BP", "AP", "BQ")


def wait_bytes(data, sem):
    pltpu.make_async_copy(data, data, sem).wait()


def main_kernel(
    hidden_ref, ids_hbm, input_grad_ref, table_ref, targets_hbm,
    part_a, part_b, part_c, targets_ref, expo, most, lse, loss_ref, turned,
    table_v, table_c, ids_ref, grad_v, emb_out, emb_in, emb_rows, emb_hot,
    lse_out, lse_in, pick_first, pick_out, pick_in, score,
    recv_sem, send_sem, core_sem, emb_sem, local_sem, round_send, round_recv,
):
    parts = (part_a, part_b, part_c)
    v, s = lax.axis_index("vocab"), lax.axis_index("seq")
    c = lax.rem(v, 2)
    y = lax.rem(lax.div(v, 2), 8)
    z = lax.rem(s, 8)
    x = 2 * lax.div(v, 16) + lax.div(s, 8)
    p = z + c * (y - z)
    q = y + c * (z - y)

    def device(x_at, p_at, q_at):
        z_at = p_at + c * (q_at - p_at)
        y_at = q_at + c * (p_at - q_at)
        return (lax.div(x_at, 2) * 16 + y_at * 2 + c, lax.rem(x_at, 2) * 8 + z_at)

    def turn(at, by, length):
        return lax.rem(at + (by + length), length) if by else at

    xh, xl_here = lax.div(x, 2), lax.rem(x, 2)
    side = 2 * x + c

    def z_peer(r):
        return (v, xl_here * 8 + lax.rem(z + r, 8))

    def y_peer(r):
        return (xh * 16 + lax.rem(y + r, 8) * 2 + c, s)

    def x_peer(r):
        other = lax.rem(side + r, 8)
        x_at = lax.div(other, 2)
        return (lax.div(x_at, 2) * 16 + y * 2 + lax.rem(other, 2), lax.rem(x_at, 2) * 8 + z)

    far_first = (4, 3, 5, 2, 6, 1, 7)
    x_peers, y_peers, z_peers = ([peer(r) for r in far_first] for peer in (x_peer, y_peer, z_peer))
    z_places = [lax.rem(z + r, 8) for r in far_first]
    sibling = (v + 1 - 2 * c, s)
    a, b, cc = part_a.at[c], part_b.at[c], part_c.at[c]

    own = [
        pltpu.make_async_copy(hidden_ref.at[pl.ds(LEN_A + LEN_B, LEN_C)], cc.at[x, p, q], local_sem.at[0]),
        pltpu.make_async_copy(hidden_ref.at[pl.ds(0, LEN_A)], a.at[p, q, x], local_sem.at[1]),
        pltpu.make_async_copy(hidden_ref.at[pl.ds(LEN_A, LEN_B)], b.at[q, p, x], local_sem.at[2]),
    ]
    ids_copy = pltpu.make_async_copy(ids_hbm, ids_ref, local_sem.at[3])
    grad_copy = pltpu.make_async_copy(input_grad_ref, grad_v, local_sem.at[4])
    targets_copy = pltpu.make_async_copy(targets_hbm, targets_ref, local_sem.at[5])
    table_copy = pltpu.make_async_copy(table_ref, table_v, local_sem.at[6])
    partners = [device(x, p, turn(q, d, 8)) for d in (4, 3, -3, 2, -2, 1, -1)]
    partners += [device(x, turn(p, d, 8), q) for d in (2, -2, 1, -1)]
    partners += [device(turn(x, d, 4), p, q) for d in (2, 1, -1)]
    partners += [sibling]
    barrier = pltpu.get_barrier_semaphore()
    for partner in partners:
        pl.semaphore_signal(barrier, inc=1, device_id=partner, device_id_type=MESH)
    for copy in own + [table_copy, ids_copy, grad_copy, targets_copy]:
        copy.start()

    def split_columns(core, j):
        n0 = 256 * j
        low = (n0 + FEAT * (n0 // FEAT) + FEAT * core) // 128 * 128
        width = min(768, D - low)
        n = lax.broadcasted_iota(jnp.int32, (1, 256), 1) + n0
        chunk = sum((n >= FEAT * k).astype(jnp.int32) for k in range(n0 // FEAT + 1, (n0 + 255) // FEAT + 1))
        source = n + FEAT * (chunk + n0 // FEAT + core) - low
        pick = (lax.broadcasted_iota(jnp.int32, (width, 256), 0) == source).astype(F32).astype(BF16)
        columns = jnp.dot(table_v[:, low : low + width], pick, preferred_element_type=F32)
        table_c[core, :, n0 : n0 + 256] = columns.astype(BF16)

    splits = [(core, j) for core in range(2) for j in range(HALF // 256)]
    table_copy.wait()
    for core, j in splits[:5]:
        split_columns(core, j)
    for copy in own:
        copy.wait()
    pl.semaphore_wait(barrier, len(partners))

    def group(at, unit, size):
        return pl.ds(size * turn(lax.div(at, size), unit, 8 // size), size)

    def block(key, shift):
        name, unit = key[0], key[1]
        if isinstance(unit, str):
            return arrived(key[1:])
        if name == "XA":
            return a.at[p, q, turn(x, shift, 4)]
        if name == "XB":
            return b.at[q, p, turn(x, shift, 4)]
        if name == "CQ":
            return cc.at[x, p, turn(q, shift, 8)]
        if name == "CP":
            return cc.at[x, turn(p, shift, 8)]
        if name == "CX":
            return cc.at[turn(x, shift, 4), group(p, unit, PAIR)]
        if name == "AQ":
            return a.at[p, turn(q, shift, 8)]
        if name == "BP":
            return b.at[q, turn(p, shift, 8)]
        if name == "AP":
            return a.at[turn(p, shift, 8), group(q, unit, GROUP)]
        if name == "BQ":
            return b.at[turn(q, shift, 8), group(p, unit, GROUP)]
        if name == "SA":
            return a.at[turn(p, unit, 8)]
        if name == "SB":
            return b.at[turn(q, unit, 8)]
        return cc.at[:, turn(p, unit, 8)]

    def arrived(key):
        return block(key, -key[2] * key[3])

    def send(key):
        m = MESSAGES[key]
        if m["axis"] == "s":
            part = ("SA", "SB", "SC").index(key[0])
            data, target, sems = block(key, 0), sibling, (core_sem.at[0, part], core_sem.at[1, part])
        else:
            by = key[2] * m["hops"]
            data = block(key, -key[2] * (key[3] - m["hops"]))
            target = {
                "x": lambda: device(turn(x, by, 4), p, q),
                "p": lambda: device(x, turn(p, by, 8), q),
                "q": lambda: device(x, p, turn(q, by, 8)),
            }[m["axis"]]()
            sems = send_sem.at[PHASES.index(key[0])], recv_sem.at[RECV[key]]
        pltpu.make_async_remote_copy(
            src_ref=data, dst_ref=data, send_sem=sems[0], recv_sem=sems[1], device_id=target, device_id_type=MESH
        ).start()

    done, sent = set(), set()

    def send_ready():
        for key, m in MESSAGES.items():
            if key not in sent and all(dep in done for dep in m["deps"]):
                sent.add(key)
                send(key)

    def embed_rows():
        ids_copy.wait()
        grad_copy.wait()
        first = lax.broadcasted_iota(jnp.int32, (SEQ, TOK), 0) * ROWS + v * (SEQ * ROWS)
        local = ids_ref[...] - first
        inside = (local >= 0) & (local < ROWS)
        total = jnp.dot(inside.astype(F32).astype(BF16), grad_v[...], preferred_element_type=F32)
        local_id = jnp.max(jnp.where(inside, local, -1).astype(F32), axis=1, keepdims=True)
        tail = jnp.broadcast_to(local_id, (SEQ, 128))
        for j in range(SEQ):
            emb_out[j, :, 0:D] = total[j : j + 1, :]
            emb_out[j, :, D:EXTRA] = tail[j : j + 1, :]
        emb_in[s] = emb_out[s]

    def send_row(r):
        j = lax.rem(s + r, SEQ)
        pltpu.make_async_remote_copy(
            src_ref=emb_out.at[j], dst_ref=emb_in.at[s], send_sem=emb_sem.at[0], recv_sem=emb_sem.at[1],
            device_id=(v, j), device_id_type=MESH,
        ).start()

    def embed_arrived():
        wait_bytes(emb_in.at[pl.ds(0, SEQ - 1)], emb_sem.at[1])
        lane_ids = lax.broadcasted_iota(jnp.int32, (1, 256), 1).astype(F32)
        for j in range(SEQ):
            emb_rows[j : j + 1, :] = emb_in[j, :, 0:D]
            emb_hot[j : j + 1, :] = (lane_ids == emb_in[j, :, D : D + 1]).astype(F32)

    needed = {key for key in MESSAGES if key[0] in ("XA", "XB", "AQ", "BP")}
    middle = max(36, 1 + max(ORDER.index(key) for key in needed))
    others = [functools.partial(split_columns, *split) for split in splits[5:]]
    others += [embed_rows] + [functools.partial(send_row, r) for r in range(1, SEQ)]
    send_ready()
    for i, key in enumerate(ORDER):
        wait_bytes(arrived(key), recv_sem.at[RECV[key]])
        done.add(key)
        send_ready()
        if i >= middle and others:
            others.pop(0)()
    assert not others

    targets_copy.wait()
    def blocks_of(n):
        return lax.div(n, 4), [2 * lax.rem(n, 4) + k for k in range(2)]

    def logits_step(n, core):
        xl, blocks = blocks_of(n)
        columns = [
            jnp.concatenate([core_features(parts, core, half, xl, z_at, slice(None)).reshape(HALF // 2, TOK) for half in range(2)], axis=0)
            for z_at in blocks
        ]
        values = jnp.dot(table_c[core], jnp.concatenate(columns, axis=1), preferred_element_type=F32)
        return xl, [(z_at, values[:, k * TOK : (k + 1) * TOK]) for k, z_at in enumerate(blocks)]

    def statistics_step(n):
        xl, blocks = blocks_of(n)
        for z_at in blocks:
            values = expo[xl, z_at]
            top = jnp.max(values, axis=0, keepdims=True)
            above = jnp.exp(values - top)
            most[xl, pl.ds(z_at, 1), :] = top
            lse_out[xl, 0, pl.ds(z_at, 1), :] = top + jnp.log(jnp.sum(above, axis=0, keepdims=True))
            hit = hit_of(targets_ref, xl, z_at)
            pick_first[z_at, pl.ds(xl, 1), :] = jnp.sum(jnp.where(hit, values, 0.0), axis=0, keepdims=True)
            expo[xl, z_at] = above

    def round_refs(stream, step):
        if stream < 2:
            return lse_out.at[stream, step], lse_in.at[stream, step]
        return pick_out.at[max(step, 1)], pick_in.at[step]

    def send_round(stream, step):
        data, into = round_refs(stream, step)
        axis = step if stream < 2 else 2 - step
        here = (side, y, z)[axis]
        for r, peer in enumerate((x_peers, y_peers, z_peers)[axis]):
            scatter = stream == 2 and step == 0
            pltpu.make_async_remote_copy(
                src_ref=pick_first.at[z_places[r]] if scatter else data, dst_ref=into.at[here],
                send_sem=round_send.at[stream, step], recv_sem=round_recv.at[stream, step],
                device_id=peer, device_id_type=MESH,
            ).start()
        into[here] = pick_first[z] if stream == 2 and step == 0 else data[...]

    def merged(stream, step):
        _, into = round_refs(stream, step)
        wait_bytes(into.at[0:7], round_recv.at[stream, step])
        values = into[...]
        if stream == 2:
            return jnp.sum(values, axis=0)
        top = jnp.max(values, axis=0)
        return top + jnp.log(jnp.sum(jnp.exp(values - top), axis=0))

    def first_pass(core):
        def step(n, carry):
            xl, values = logits_step(n, core)
            for z_at, value in values:
                expo[xl, z_at] = value
            return carry

        lax.fori_loop(0, 8, step, 0)

    def second_pass(core):
        def add(n):
            xl, values = logits_step(n, core)
            for z_at, value in values:
                expo[xl, z_at] += value

        def step(n, carry):
            statistics_step(n - 1)
            add(n)
            return carry

        add(jnp.int32(0))
        lax.fori_loop(1, 5, step, 0)
        send_round(0, 0)
        lax.fori_loop(5, 8, step, 0)

    for core in range(2):
        pl.when(c == core)(functools.partial(first_pass, core))
    for i, data in enumerate((part_a, part_b, part_c)):
        wait_bytes(data.at[1 - c], core_sem.at[1, i])
    for core in range(2):
        pl.when(c == 1 - core)(functools.partial(second_pass, core))
    statistics_step(jnp.int32(7))
    send_round(1, 0)
    send_round(2, 0)

    def next_round(stream, step):
        data, _ = round_refs(stream, step + 1)
        data[...] = merged(stream, step)
        send_round(stream, step + 1)

    for stream, step in ((0, 0), (1, 0), (2, 0), (0, 1), (1, 1)):
        next_round(stream, step)

    embed_arrived()
    hot = emb_hot[...].astype(BF16)
    hot = jnp.concatenate([hot, hot, hot], axis=0)
    for i in range(4):
        rest = emb_rows[:, i * (D // 4) : (i + 1) * (D // 4)]
        high = rest.astype(BF16)
        rest = rest - high.astype(F32)
        middle = rest.astype(BF16)
        low = (rest - middle.astype(F32)).astype(BF16)
        terms = jnp.concatenate([high, middle, low], axis=0)
        turned[i] = lax.dot_general(terms, hot, (((0,), (0,)), ((), ())), preferred_element_type=F32)

    next_round(2, 1)
    lse[0] = merged(0, 2)
    fill_score(0, expo, most, lse, targets_ref, score)
    for i in range(4):
        turned[i] += head_block(parts, 0, i, score)
    lse[1] = merged(1, 2)
    pick_out[0] = merged(2, 2)
    loss_ref[...] = lse[xl_here, pl.ds(z, 1), :] - pick_out[0, pl.ds(xl_here, 1), :]
    for stream in range(3):
        for step in range(3):
            wait_bytes(round_refs(stream, step)[1].at[0:7], round_send.at[stream, step])
    wait_bytes(a.at[p, q, 0:3], send_sem.at[0])
    wait_bytes(b.at[q, p, 0:3], send_sem.at[1])
    wait_bytes(cc.at[x, p, 0:7], send_sem.at[2])
    wait_bytes(cc.at[x, 0:7], send_sem.at[3])
    wait_bytes(cc.at[0:3], send_sem.at[4])
    wait_bytes(a.at[p, 0:7], send_sem.at[5])
    wait_bytes(b.at[q, 0:7], send_sem.at[6])
    wait_bytes(a.at[0:7], send_sem.at[7])
    wait_bytes(b.at[0:7], send_sem.at[8])
    wait_bytes(emb_out.at[pl.ds(0, SEQ - 1)], emb_sem.at[0])
    for i, data in enumerate((part_a, part_b, part_c)):
        wait_bytes(data.at[c], core_sem.at[0, i])


def hit_of(targets_ref, xl, z_at):
    row_start = (lax.axis_index("vocab") * SEQ + lax.axis_index("seq")) * ROWS
    row_ids = lax.broadcasted_iota(jnp.int32, (ROWS, TOK), 0)
    return (targets_ref[pl.ds(8 * xl + z_at, 1), :] - row_start) == row_ids


def core_features(parts, core, xh, xl, z_at, ys):
    part_a, part_b, part_c = parts
    x = 2 * xh + xl
    if core == 0:
        return jnp.concatenate([part_a[0, z_at, ys, x], part_b[0, ys, z_at, x], part_c[0, x, z_at, ys]], axis=1)
    return jnp.concatenate([part_a[1, ys, z_at, x], part_b[1, z_at, ys, x], part_c[1, x, ys, z_at]], axis=1)


def features_of(parts, xh, xl, z_at, ys):
    both = jnp.stack([core_features(parts, core, xh, xl, z_at, ys) for core in range(2)], axis=1)
    return both.reshape(both.shape[0] * 2 * FEAT, TOK)


def fill_score(xl, expo, most, lse, targets_ref, score):
    factor = jnp.exp(most[xl] - lse[xl])
    for z_at in range(8):
        value = expo[xl, z_at] * factor[z_at : z_at + 1, :] - hit_of(targets_ref, xl, z_at).astype(F32)
        score[0:ROWS, z_at * TOK : (z_at + 1) * TOK] = value.astype(BF16)


def head_block(parts, xl, i, score):
    xh, ys = i // 2, slice(4 * (i % 2), 4 * (i % 2) + 4)
    features = jnp.concatenate([features_of(parts, xh, xl, z_at, ys) for z_at in range(8)], axis=1)
    return lax.dot_general(features, score[...], (((1,), (1,)), ((), ())), preferred_element_type=F32)


def head_kernel(
    part_a, part_b, part_c, expo, most, lse, targets_ref, turned, loss_in,
    loss_ref, out_ref,
    score, out_v, out_sem,
):
    parts = (part_a, part_b, part_c)
    loss_ref[...] = loss_in[...]
    fill_score(1, expo, most, lse, targets_ref, score)

    ready = None
    for i in range(5):
        total = (turned[i] + head_block(parts, 1, i, score)).astype(BF16) if i < 4 else None
        if ready is not None:
            at = pl.ds((i - 1) * (D // 4), D // 4)
            out_v[:, at] = jnp.transpose(ready)[0:ROWS, :]
            pltpu.make_async_copy(out_v.at[:, at], out_ref.at[:, at], out_sem).start()
        ready = total
    pltpu.make_async_copy(out_v, out_ref, out_sem).wait()


def on_device(hidden, table, targets, token_ids, input_grad):
    any_space = pl.BlockSpec(memory_space=pl.ANY)
    vmem = pl.BlockSpec(memory_space=pltpu.VMEM)
    dma = pltpu.SemaphoreType.DMA
    tiles = pltpu.VMEM((2, 8, TOK), F32)
    targets = targets.reshape(SEQ, TOK)
    *parts, targets, expo, most, lse, loss, turned = pl.pallas_call(
        main_kernel,
        out_shape=(
            pltpu.VMEM((2, 8, 8, 4, LEN_A, TOK), BF16),
            pltpu.VMEM((2, 8, 8, 4, LEN_B, TOK), BF16),
            pltpu.VMEM((2, 4, 8, 8, LEN_C, TOK), BF16),
            pltpu.VMEM((SEQ, TOK), jnp.int32),
            pltpu.VMEM((2, 8, ROWS, TOK), F32),
            tiles,
            tiles,
            pltpu.VMEM((1, TOK), F32),
            pltpu.VMEM((4, D // 4, 256), F32),
        ),
        in_specs=[any_space] * 5,
        out_specs=(vmem,) * 9,
        scratch_shapes=[
            pltpu.VMEM((ROWS, D), BF16),
            pltpu.VMEM((2, ROWS, HALF), BF16),
            pltpu.VMEM((1, TOK), jnp.int32),
            pltpu.VMEM((TOK, D), BF16),
            pltpu.VMEM((SEQ, 1, EXTRA), F32),
            pltpu.VMEM((SEQ, 1, EXTRA), F32),
            pltpu.VMEM((SEQ, D), F32),
            pltpu.VMEM((SEQ, 256), F32),
            pltpu.VMEM((2, 3, 8, TOK), F32),
            pltpu.VMEM((2, 3, 8, 8, TOK), F32),
            pltpu.VMEM((8, 8, TOK), F32),
            pltpu.VMEM((3, 8, TOK), F32),
            pltpu.VMEM((3, 8, 8, TOK), F32),
            pltpu.VMEM((256, 8 * TOK), BF16),
            dma((len(ORDER),)),
            dma((len(PHASES),)),
            dma((2, 3)),
            dma((2,)),
            dma((7,)),
            dma((3, 3)),
            dma((3, 3)),
        ],
        compiler_params=pltpu.CompilerParams(collective_id=0, has_side_effects=True, vmem_limit_bytes=41 * 2**20),
        cost_estimate=pl.CostEstimate(flops=3 * 2048 * ROWS * D, bytes_accessed=2**22, transcendentals=2048 * ROWS),
        name="main",
    )(hidden.T, token_ids.reshape(1, TOK), input_grad, table, targets)
    loss, table_grad = pl.pallas_call(
        head_kernel,
        out_shape=(jax.ShapeDtypeStruct((1, TOK), F32), jax.ShapeDtypeStruct((ROWS, D), BF16)),
        in_specs=[vmem] * 9,
        out_specs=(vmem, any_space),
        scratch_shapes=[pltpu.VMEM((256, 8 * TOK), BF16), pltpu.VMEM((ROWS, D), BF16), dma],
        compiler_params=pltpu.CompilerParams(vmem_limit_bytes=14 * 2**20),
        cost_estimate=pl.CostEstimate(flops=2 * 2048 * ROWS * D, bytes_accessed=2**21, transcendentals=2048 * ROWS),
        name="head",
    )(*parts, expo, most, lse, targets, turned, loss)
    return loss.reshape(TOK), table_grad


def solution(mesh):
    in_specs = (P("seq", "vocab"), P(("vocab", "seq"), None), P(), P("seq"), P("seq", None))
    out_specs = (P("seq"), P(("vocab", "seq"), None))
    return jax.shard_map(
        on_device, mesh=mesh, in_specs=in_specs, out_specs=out_specs, check_vma=False
    )
```

```python
import functools
import heapq
import itertools

import jax
import jax.numpy as jnp
from jax import lax
from jax.experimental import pallas as pl
from jax.experimental.pallas import tpu as pltpu
from jax.sharding import PartitionSpec as P

MESH = pl.DeviceIdType.MESH
F32 = jnp.float32
BF16 = jnp.bfloat16

D = 3584
TOK = 128
FEAT = 112
ROWS = 250
SEQ = 16
HALF = D // 2
EXTRA = D + 128
LEN_A, LEN_B, LEN_C = 32, 32, 48
GROUP = 4
PAIR = 1


def plan_messages():
    messages = {}

    def put(key, size, axis, hops, deps):
        messages[key] = dict(size=size * 256, axis=axis, hops=hops, deps=list(deps))

    def direct(name, axis, size, rels):
        for rel in rels:
            put((name, 0, 1 if rel > 0 else -1, abs(rel)), size, axis, abs(rel), [])

    def ring(name, unit, axis, size, length, deps, flip, hops_of=(1, 1, 1, 1)):
        far = (length // 2, length // 2 - 1)
        for step, most in zip((1, -1), far[::-1] if flip else far):
            for dist in sorted(range(1, most + 1), key=lambda at: -hops_of[at - 1]):
                hops = hops_of[dist - 1]
                put((name, unit, step, dist), size, axis, hops, deps if dist == hops else [(name, unit, step, dist - hops)])

    def item(name, rel, flip):
        rel %= 8
        back = 4 if flip else 3
        if rel == 0:
            return []
        return [(name, 0, -1, rel)] if rel <= back else [(name, 0, 1, 8 - rel)]

    def of(*names):
        return [key for key in messages if key[0] in names]

    whole = {
        1: {rel: (rel,) for rel in (0, 1, 7, 2, 6, 3, 5, 4)},
        2: {0: (1, -1), 1: (1, 2, 3), 3: (-1, -2, -3), 2: (2, 3, 4, 5, 6)},
        4: {0: (1, 2, 3, -1, -2, -3), 1: tuple(range(1, 8))},
    }
    direct("CQ", "q", LEN_C, (4, 3, -3, 2, -2, 1, -1))
    direct("XA", "x", LEN_A, (2, 1, -1))
    direct("XB", "x", LEN_B, (2, 1, -1))
    ring("CP", 0, "p", 8 * LEN_C, 8, of("CQ"), False)
    for unit, rels in whole[PAIR].items():
        deps = of("CQ") + [key for rel in rels for key in item("CP", rel, False)]
        ring("CX", unit, "x", PAIR * 8 * LEN_C, 4, deps, unit % 2 == 1)
    ring("AQ", 0, "q", 4 * LEN_A, 8, of("XA"), False, (1, 2, 1, 2))
    ring("BP", 0, "p", 4 * LEN_B, 8, of("XB"), True, (1, 2, 1, 2))
    for name, axis, first, source, flip, size in (("AP", "p", "XA", "AQ", False, LEN_A), ("BQ", "q", "XB", "BP", True, LEN_B)):
        for unit, rels in whole[GROUP].items():
            deps = of(first) + [key for rel in rels for key in item(source, rel, flip)]
            ring(name, unit, axis, 4 * GROUP * size, 8, deps, unit % 2 == 1)
    put(("SA", 0, 0, 0), 32 * LEN_A, "s", 1, of("XA", "AQ"))
    put(("SB", 0, 0, 0), 32 * LEN_B, "s", 1, of("XB", "BP"))
    for rel in range(1, 8):
        for name, source, size in (("SA", "AP", LEN_A), ("SB", "BQ", LEN_B)):
            keys = [key for key in of(source) if (-key[2] * key[3]) % 8 == rel]
            if rel == 4:
                for key in keys:
                    put((name,) + key, messages[key]["size"] // 256, "s", 1, [key])
            else:
                put((name, rel, 0, 0), 32 * size, "s", 1, keys)
    for rel in range(8):
        keys = [key for key in of("CP") if (-key[2] * key[3]) % 8 == rel] + [key for key in of("CX") if key[1] == rel]
        if rel == 4:
            for key in keys:
                put(("SC",) + key, messages[key]["size"] // 256, "s", 1, [key])
        else:
            put(("SC", rel, 0, 0), 32 * LEN_C, "s", 1, of("CQ") + keys)
    return messages


def plan_order(messages):
    turned = {"x": "x", "p": "q", "q": "p", "s": "s"}
    counter = itertools.count()
    link, free, events = {}, [0.0, 0.0], []
    arrival = [{}, {}]
    waits = [{key: set(m["deps"]) for key, m in messages.items()} for _ in range(2)]
    after = {}
    for key, m in messages.items():
        for dep in m["deps"]:
            after.setdefault(dep, []).append(key)

    def start(core, key, now):
        m = messages[key]
        free[core] = now = max(now, free[core]) + 0.05
        lane = ("s", core) if m["axis"] == "s" else (turned[m["axis"]] if core else m["axis"], key[2])
        rate = 6e5 if m["axis"] == "s" else 8.5e4
        link[lane] = max(now, link.get(lane, 0.0)) + m["size"] * m["hops"] / rate
        heapq.heappush(events, (link[lane] + 3.0 + 0.5 * (m["hops"] - 1), next(counter), core, key))

    for core in range(2):
        for key, m in messages.items():
            if not m["deps"]:
                start(core, key, 0.0)
    while events:
        now, _, core, key = heapq.heappop(events)
        arrival[core][key] = now
        for later in after.get(key, []):
            waits[core][later].discard(key)
            if not waits[core][later]:
                start(core, later, now)
    here = [key for key, m in messages.items() if m["axis"] != "s"]
    return sorted(here, key=lambda key: arrival[0][key] + arrival[1][key])


MESSAGES = plan_messages()
ORDER = plan_order(MESSAGES)
RECV = {key: i for i, key in enumerate(ORDER)}
OWN_ROWS = {"XA": pl.ds(0, LEN_A), "XB": pl.ds(LEN_A, LEN_B), "CQ": pl.ds(LEN_A + LEN_B, LEN_C)}
PHASES = ("XA", "XB", "CQ", "CP", "CX", "AQ", "BP", "AP", "BQ")


def wait_bytes(data, sem):
    pltpu.make_async_copy(data, data, sem).wait()


def main_kernel(
    hidden_ref, ids_hbm, input_grad_ref, table_ref, targets_hbm,
    part_a, part_b, part_c, targets_ref, expo, most, lse, loss_ref, turned,
    table_v, table_c, ids_ref, grad_v, emb_out, emb_in, emb_rows, emb_hot,
    lse_out, lse_in, pick_first, pick_out, pick_in, score,
    recv_sem, send_sem, core_sem, emb_sem, local_sem, round_send, round_recv,
):
    parts = (part_a, part_b, part_c)
    v, s = lax.axis_index("vocab"), lax.axis_index("seq")
    c = lax.rem(v, 2)
    y = lax.rem(lax.div(v, 2), 8)
    z = lax.rem(s, 8)
    x = 2 * lax.div(v, 16) + lax.div(s, 8)
    p = z + c * (y - z)
    q = y + c * (z - y)

    def device(x_at, p_at, q_at):
        z_at = p_at + c * (q_at - p_at)
        y_at = q_at + c * (p_at - q_at)
        return (lax.div(x_at, 2) * 16 + y_at * 2 + c, lax.rem(x_at, 2) * 8 + z_at)

    def turn(at, by, length):
        return lax.rem(at + (by + length), length) if by else at

    xh, xl_here = lax.div(x, 2), lax.rem(x, 2)
    side = 2 * x + c

    def z_peer(r):
        return (v, xl_here * 8 + lax.rem(z + r, 8))

    def y_peer(r):
        return (xh * 16 + lax.rem(y + r, 8) * 2 + c, s)

    def x_peer(r):
        other = lax.rem(side + r, 8)
        x_at = lax.div(other, 2)
        return (lax.div(x_at, 2) * 16 + y * 2 + lax.rem(other, 2), lax.rem(x_at, 2) * 8 + z)

    far_first = (4, 3, 5, 2, 6, 1, 7)
    x_peers, y_peers, z_peers = ([peer(r) for r in far_first] for peer in (x_peer, y_peer, z_peer))
    z_places = [lax.rem(z + r, 8) for r in far_first]
    sibling = (v + 1 - 2 * c, s)
    a, b, cc = part_a.at[c], part_b.at[c], part_c.at[c]

    own = [
        pltpu.make_async_copy(hidden_ref.at[pl.ds(LEN_A + LEN_B, LEN_C)], cc.at[x, p, q], local_sem.at[0]),
        pltpu.make_async_copy(hidden_ref.at[pl.ds(0, LEN_A)], a.at[p, q, x], local_sem.at[1]),
        pltpu.make_async_copy(hidden_ref.at[pl.ds(LEN_A, LEN_B)], b.at[q, p, x], local_sem.at[2]),
    ]
    ids_copy = pltpu.make_async_copy(ids_hbm, ids_ref, local_sem.at[3])
    grad_copy = pltpu.make_async_copy(input_grad_ref, grad_v, local_sem.at[4])
    targets_copy = pltpu.make_async_copy(targets_hbm, targets_ref, local_sem.at[5])
    table_copy = pltpu.make_async_copy(table_ref, table_v, local_sem.at[6])
    partners = [device(x, p, turn(q, d, 8)) for d in (4, 3, -3, 2, -2, 1, -1)]
    partners += [device(x, turn(p, d, 8), q) for d in (2, -2, 1, -1)]
    partners += [device(turn(x, d, 4), p, q) for d in (2, 1, -1)]
    partners += [sibling]
    barrier = pltpu.get_barrier_semaphore()
    for partner in partners:
        pl.semaphore_signal(barrier, inc=1, device_id=partner, device_id_type=MESH)
    for copy in own + [table_copy, ids_copy, grad_copy, targets_copy]:
        copy.start()

    def split_columns(core, j):
        n0 = 256 * j
        low = (n0 + FEAT * (n0 // FEAT) + FEAT * core) // 128 * 128
        width = min(768, D - low)
        n = lax.broadcasted_iota(jnp.int32, (1, 256), 1) + n0
        chunk = sum((n >= FEAT * k).astype(jnp.int32) for k in range(n0 // FEAT + 1, (n0 + 255) // FEAT + 1))
        source = n + FEAT * (chunk + n0 // FEAT + core) - low
        pick = (lax.broadcasted_iota(jnp.int32, (width, 256), 0) == source).astype(F32).astype(BF16)
        columns = jnp.dot(table_v[:, low : low + width], pick, preferred_element_type=F32)
        table_c[core, :, n0 : n0 + 256] = columns.astype(BF16)

    splits = [(core, j) for core in range(2) for j in range(HALF // 256)]
    pl.semaphore_wait(barrier, len(partners))

    def group(at, unit, size):
        return pl.ds(size * turn(lax.div(at, size), unit, 8 // size), size)

    def block(key, shift):
        name, unit = key[0], key[1]
        if isinstance(unit, str):
            return arrived(key[1:])
        if name == "XA":
            return a.at[p, q, turn(x, shift, 4)]
        if name == "XB":
            return b.at[q, p, turn(x, shift, 4)]
        if name == "CQ":
            return cc.at[x, p, turn(q, shift, 8)]
        if name == "CP":
            return cc.at[x, turn(p, shift, 8)]
        if name == "CX":
            return cc.at[turn(x, shift, 4), group(p, unit, PAIR)]
        if name == "AQ":
            return a.at[p, turn(q, shift, 8)]
        if name == "BP":
            return b.at[q, turn(p, shift, 8)]
        if name == "AP":
            return a.at[turn(p, shift, 8), group(q, unit, GROUP)]
        if name == "BQ":
            return b.at[turn(q, shift, 8), group(p, unit, GROUP)]
        if name == "SA":
            return a.at[turn(p, unit, 8)]
        if name == "SB":
            return b.at[turn(q, unit, 8)]
        return cc.at[:, turn(p, unit, 8)]

    def arrived(key):
        return block(key, -key[2] * key[3])

    def send(key):
        m = MESSAGES[key]
        if m["axis"] == "s":
            part = ("SA", "SB", "SC").index(key[0])
            data, target, sems = block(key, 0), sibling, (core_sem.at[0, part], core_sem.at[1, part])
        else:
            by = key[2] * m["hops"]
            data = block(key, -key[2] * (key[3] - m["hops"]))
            target = {
                "x": lambda: device(turn(x, by, 4), p, q),
                "p": lambda: device(x, turn(p, by, 8), q),
                "q": lambda: device(x, p, turn(q, by, 8)),
            }[m["axis"]]()
            sems = send_sem.at[PHASES.index(key[0])], recv_sem.at[RECV[key]]
        source = hidden_ref.at[OWN_ROWS[key[0]]] if key[0] in OWN_ROWS else data
        pltpu.make_async_remote_copy(
            src_ref=source, dst_ref=data, send_sem=sems[0], recv_sem=sems[1], device_id=target, device_id_type=MESH
        ).start()

    done, sent = set(), set()

    def send_ready():
        for key, m in MESSAGES.items():
            if key not in sent and all(dep in done for dep in m["deps"]):
                sent.add(key)
                send(key)

    def embed_rows():
        ids_copy.wait()
        grad_copy.wait()
        first = lax.broadcasted_iota(jnp.int32, (SEQ, TOK), 0) * ROWS + v * (SEQ * ROWS)
        local = ids_ref[...] - first
        inside = (local >= 0) & (local < ROWS)
        total = jnp.dot(inside.astype(F32).astype(BF16), grad_v[...], preferred_element_type=F32)
        local_id = jnp.max(jnp.where(inside, local, -1).astype(F32), axis=1, keepdims=True)
        tail = jnp.broadcast_to(local_id, (SEQ, 128))
        for j in range(SEQ):
            emb_out[j, :, 0:D] = total[j : j + 1, :]
            emb_out[j, :, D:EXTRA] = tail[j : j + 1, :]
        emb_in[s] = emb_out[s]

    def send_row(r):
        j = lax.rem(s + r, SEQ)
        pltpu.make_async_remote_copy(
            src_ref=emb_out.at[j], dst_ref=emb_in.at[s], send_sem=emb_sem.at[0], recv_sem=emb_sem.at[1],
            device_id=(v, j), device_id_type=MESH,
        ).start()

    def embed_arrived():
        wait_bytes(emb_in.at[pl.ds(0, SEQ - 1)], emb_sem.at[1])
        lane_ids = lax.broadcasted_iota(jnp.int32, (1, 256), 1).astype(F32)
        for j in range(SEQ):
            emb_rows[j : j + 1, :] = emb_in[j, :, 0:D]
            emb_hot[j : j + 1, :] = (lane_ids == emb_in[j, :, D : D + 1]).astype(F32)

    needed = {key for key in MESSAGES if key[0] in ("XA", "XB", "AQ", "BP")}
    middle = max(36, 1 + max(ORDER.index(key) for key in needed))
    others = [functools.partial(split_columns, *split) for split in splits[9:]]
    others += [embed_rows] + [functools.partial(send_row, r) for r in range(1, SEQ)]
    send_ready()
    table_copy.wait()
    for core, j in splits[:9]:
        split_columns(core, j)
    for copy in own:
        copy.wait()
    for i, key in enumerate(ORDER):
        wait_bytes(arrived(key), recv_sem.at[RECV[key]])
        done.add(key)
        send_ready()
        if i >= middle and others:
            others.pop(0)()
    assert not others

    targets_copy.wait()
    def blocks_of(n):
        return lax.div(n, 4), [2 * lax.rem(n, 4) + k for k in range(2)]

    def logits_step(n, core):
        xl, blocks = blocks_of(n)
        columns = [
            jnp.concatenate([core_features(parts, core, half, xl, z_at, slice(None)).reshape(HALF // 2, TOK) for half in range(2)], axis=0)
            for z_at in blocks
        ]
        values = jnp.dot(table_c[core], jnp.concatenate(columns, axis=1), preferred_element_type=F32)
        return xl, [(z_at, values[:, k * TOK : (k + 1) * TOK]) for k, z_at in enumerate(blocks)]

    def statistics_step(n):
        xl, blocks = blocks_of(n)
        for z_at in blocks:
            values = expo[xl, z_at]
            top = jnp.max(values, axis=0, keepdims=True)
            above = jnp.exp(values - top)
            most[xl, pl.ds(z_at, 1), :] = top
            lse_out[xl, 0, pl.ds(z_at, 1), :] = top + jnp.log(jnp.sum(above, axis=0, keepdims=True))
            hit = hit_of(targets_ref, xl, z_at)
            pick_first[z_at, pl.ds(xl, 1), :] = jnp.sum(jnp.where(hit, values, 0.0), axis=0, keepdims=True)
            expo[xl, z_at] = above

    def round_refs(stream, step):
        if stream < 2:
            return lse_out.at[stream, step], lse_in.at[stream, step]
        return pick_out.at[max(step, 1)], pick_in.at[step]

    def send_round(stream, step):
        data, into = round_refs(stream, step)
        axis = step if stream < 2 else 2 - step
        here = (side, y, z)[axis]
        for r, peer in enumerate((x_peers, y_peers, z_peers)[axis]):
            scatter = stream == 2 and step == 0
            pltpu.make_async_remote_copy(
                src_ref=pick_first.at[z_places[r]] if scatter else data, dst_ref=into.at[here],
                send_sem=round_send.at[stream, step], recv_sem=round_recv.at[stream, step],
                device_id=peer, device_id_type=MESH,
            ).start()
        into[here] = pick_first[z] if stream == 2 and step == 0 else data[...]

    def merged(stream, step):
        _, into = round_refs(stream, step)
        wait_bytes(into.at[0:7], round_recv.at[stream, step])
        values = into[...]
        if stream == 2:
            return jnp.sum(values, axis=0)
        top = jnp.max(values, axis=0)
        return top + jnp.log(jnp.sum(jnp.exp(values - top), axis=0))

    def first_pass(core):
        def step(n, carry):
            xl, values = logits_step(n, core)
            for z_at, value in values:
                expo[xl, z_at] = value
            return carry

        lax.fori_loop(0, 8, step, 0)

    def second_pass(core):
        def add(n):
            xl, values = logits_step(n, core)
            for z_at, value in values:
                expo[xl, z_at] += value

        def step(n, carry):
            statistics_step(n - 1)
            add(n)
            return carry

        add(jnp.int32(0))
        lax.fori_loop(1, 5, step, 0)
        send_round(0, 0)
        lax.fori_loop(5, 8, step, 0)

    for core in range(2):
        pl.when(c == core)(functools.partial(first_pass, core))
    for i, data in enumerate((part_a, part_b, part_c)):
        wait_bytes(data.at[1 - c], core_sem.at[1, i])
    for core in range(2):
        pl.when(c == 1 - core)(functools.partial(second_pass, core))
    statistics_step(jnp.int32(7))
    send_round(1, 0)
    send_round(2, 0)

    def next_round(stream, step):
        data, _ = round_refs(stream, step + 1)
        data[...] = merged(stream, step)
        send_round(stream, step + 1)

    for stream, step in ((0, 0), (1, 0), (2, 0), (0, 1), (1, 1)):
        next_round(stream, step)

    embed_arrived()
    hot = emb_hot[...].astype(BF16)
    hot = jnp.concatenate([hot, hot, hot], axis=0)
    for i in range(4):
        rest = emb_rows[:, i * (D // 4) : (i + 1) * (D // 4)]
        high = rest.astype(BF16)
        rest = rest - high.astype(F32)
        middle = rest.astype(BF16)
        low = (rest - middle.astype(F32)).astype(BF16)
        terms = jnp.concatenate([high, middle, low], axis=0)
        turned[i] = lax.dot_general(terms, hot, (((0,), (0,)), ((), ())), preferred_element_type=F32)

    next_round(2, 1)
    lse[0] = merged(0, 2)
    fill_score(0, expo, most, lse, targets_ref, score)
    for i in range(4):
        turned[i] += head_block(parts, 0, i, score)
    lse[1] = merged(1, 2)
    pick_out[0] = merged(2, 2)
    loss_ref[...] = lse[xl_here, pl.ds(z, 1), :] - pick_out[0, pl.ds(xl_here, 1), :]
    for stream in range(3):
        for step in range(3):
            wait_bytes(round_refs(stream, step)[1].at[0:7], round_send.at[stream, step])
    wait_bytes(a.at[p, q, 0:3], send_sem.at[0])
    wait_bytes(b.at[q, p, 0:3], send_sem.at[1])
    wait_bytes(cc.at[x, p, 0:7], send_sem.at[2])
    wait_bytes(cc.at[x, 0:7], send_sem.at[3])
    wait_bytes(cc.at[0:3], send_sem.at[4])
    wait_bytes(a.at[p, 0:7], send_sem.at[5])
    wait_bytes(b.at[q, 0:7], send_sem.at[6])
    wait_bytes(a.at[0:7], send_sem.at[7])
    wait_bytes(b.at[0:7], send_sem.at[8])
    wait_bytes(emb_out.at[pl.ds(0, SEQ - 1)], emb_sem.at[0])
    for i, data in enumerate((part_a, part_b, part_c)):
        wait_bytes(data.at[c], core_sem.at[0, i])


def hit_of(targets_ref, xl, z_at):
    row_start = (lax.axis_index("vocab") * SEQ + lax.axis_index("seq")) * ROWS
    row_ids = lax.broadcasted_iota(jnp.int32, (ROWS, TOK), 0)
    return (targets_ref[pl.ds(8 * xl + z_at, 1), :] - row_start) == row_ids


def core_features(parts, core, xh, xl, z_at, ys):
    part_a, part_b, part_c = parts
    x = 2 * xh + xl
    if core == 0:
        return jnp.concatenate([part_a[0, z_at, ys, x], part_b[0, ys, z_at, x], part_c[0, x, z_at, ys]], axis=1)
    return jnp.concatenate([part_a[1, ys, z_at, x], part_b[1, z_at, ys, x], part_c[1, x, ys, z_at]], axis=1)


def features_of(parts, xh, xl, z_at, ys):
    both = jnp.stack([core_features(parts, core, xh, xl, z_at, ys) for core in range(2)], axis=1)
    return both.reshape(both.shape[0] * 2 * FEAT, TOK)


def fill_score(xl, expo, most, lse, targets_ref, score):
    factor = jnp.exp(most[xl] - lse[xl])
    for z_at in range(8):
        value = expo[xl, z_at] * factor[z_at : z_at + 1, :] - hit_of(targets_ref, xl, z_at).astype(F32)
        score[0:ROWS, z_at * TOK : (z_at + 1) * TOK] = value.astype(BF16)


def head_block(parts, xl, i, score):
    xh, ys = i // 2, slice(4 * (i % 2), 4 * (i % 2) + 4)
    features = jnp.concatenate([features_of(parts, xh, xl, z_at, ys) for z_at in range(8)], axis=1)
    return lax.dot_general(features, score[...], (((1,), (1,)), ((), ())), preferred_element_type=F32)


def head_kernel(
    part_a, part_b, part_c, expo, most, lse, targets_ref, turned, loss_in,
    loss_ref, out_ref,
    score, out_v, out_sem,
):
    parts = (part_a, part_b, part_c)
    loss_ref[...] = loss_in[...]
    fill_score(1, expo, most, lse, targets_ref, score)

    ready = None
    for i in range(5):
        total = (turned[i] + head_block(parts, 1, i, score)).astype(BF16) if i < 4 else None
        if ready is not None:
            at = pl.ds((i - 1) * (D // 4), D // 4)
            out_v[:, at] = jnp.transpose(ready)[0:ROWS, :]
            pltpu.make_async_copy(out_v.at[:, at], out_ref.at[:, at], out_sem).start()
        ready = total
    pltpu.make_async_copy(out_v, out_ref, out_sem).wait()


def on_device(hidden, table, targets, token_ids, input_grad):
    any_space = pl.BlockSpec(memory_space=pl.ANY)
    vmem = pl.BlockSpec(memory_space=pltpu.VMEM)
    dma = pltpu.SemaphoreType.DMA
    tiles = pltpu.VMEM((2, 8, TOK), F32)
    targets = targets.reshape(SEQ, TOK)
    *parts, targets, expo, most, lse, loss, turned = pl.pallas_call(
        main_kernel,
        out_shape=(
            pltpu.VMEM((2, 8, 8, 4, LEN_A, TOK), BF16),
            pltpu.VMEM((2, 8, 8, 4, LEN_B, TOK), BF16),
            pltpu.VMEM((2, 4, 8, 8, LEN_C, TOK), BF16),
            pltpu.VMEM((SEQ, TOK), jnp.int32),
            pltpu.VMEM((2, 8, ROWS, TOK), F32),
            tiles,
            tiles,
            pltpu.VMEM((1, TOK), F32),
            pltpu.VMEM((4, D // 4, 256), F32),
        ),
        in_specs=[any_space] * 5,
        out_specs=(vmem,) * 9,
        scratch_shapes=[
            pltpu.VMEM((ROWS, D), BF16),
            pltpu.VMEM((2, ROWS, HALF), BF16),
            pltpu.VMEM((1, TOK), jnp.int32),
            pltpu.VMEM((TOK, D), BF16),
            pltpu.VMEM((SEQ, 1, EXTRA), F32),
            pltpu.VMEM((SEQ, 1, EXTRA), F32),
            pltpu.VMEM((SEQ, D), F32),
            pltpu.VMEM((SEQ, 256), F32),
            pltpu.VMEM((2, 3, 8, TOK), F32),
            pltpu.VMEM((2, 3, 8, 8, TOK), F32),
            pltpu.VMEM((8, 8, TOK), F32),
            pltpu.VMEM((3, 8, TOK), F32),
            pltpu.VMEM((3, 8, 8, TOK), F32),
            pltpu.VMEM((256, 8 * TOK), BF16),
            dma((len(ORDER),)),
            dma((len(PHASES),)),
            dma((2, 3)),
            dma((2,)),
            dma((7,)),
            dma((3, 3)),
            dma((3, 3)),
        ],
        compiler_params=pltpu.CompilerParams(collective_id=0, has_side_effects=True, vmem_limit_bytes=41 * 2**20),
        cost_estimate=pl.CostEstimate(flops=3 * 2048 * ROWS * D, bytes_accessed=2**22, transcendentals=2048 * ROWS),
        name="main",
    )(hidden.T, token_ids.reshape(1, TOK), input_grad, table, targets)
    loss, table_grad = pl.pallas_call(
        head_kernel,
        out_shape=(jax.ShapeDtypeStruct((1, TOK), F32), jax.ShapeDtypeStruct((ROWS, D), BF16)),
        in_specs=[vmem] * 9,
        out_specs=(vmem, any_space),
        scratch_shapes=[pltpu.VMEM((256, 8 * TOK), BF16), pltpu.VMEM((ROWS, D), BF16), dma],
        compiler_params=pltpu.CompilerParams(vmem_limit_bytes=14 * 2**20),
        cost_estimate=pl.CostEstimate(flops=2 * 2048 * ROWS * D, bytes_accessed=2**21, transcendentals=2048 * ROWS),
        name="head",
    )(*parts, expo, most, lse, targets, turned, loss)
    return loss.reshape(TOK), table_grad


def solution(mesh):
    in_specs = (P("seq", "vocab"), P(("vocab", "seq"), None), P(), P("seq"), P("seq", None))
    out_specs = (P("seq"), P(("vocab", "seq"), None))
    return jax.shard_map(
        on_device, mesh=mesh, in_specs=in_specs, out_specs=out_specs, check_vma=False
    )
```
